256 devices in a mesh: lat: 8 (over x, y_hi), lon: 8 (over z), tp: 4 (over y_lo, core).
Axes of the slice: x: 4, y: 4 (y_hi: 2, y_lo: 2; y = y_hi * 2 + y_lo), z: 8, core: 2. Of those that a mesh axis runs over, the one named last changes fastest.
Arguments:
- tokens: bfloat16 [2, 192, 384, 512], P(None, 'lat', 'lon'), may hold values from -6 to 6
- cotangent: bfloat16 [2, 192, 384, 512], P(None, 'lat', 'lon'), may hold values from -6 to 6
- norm_gain: float32 [512], replicated, may hold values from 0.1 to 1.9
- norm_bias: float32 [512], replicated, may hold values from -3 to 3
- w_qkv: bfloat16 [512, 3, 512], P(None, None, 'tp'), as said below
- w_out: bfloat16 [512, 512], P('tp'), may hold values from -0.25 to 0.25
Outputs:
- grad_tokens: bfloat16 [2, 192, 384, 512], P(None, 'lat', 'lon')
- grad_gain: float32 [512], replicated
- grad_bias: float32 [512], replicated
- grad_qkv: float32 [512, 3, 512], P(None, None, 'tp')
- grad_out: float32 [512, 512], P('tp')
The draws below stay inside these ranges and needn't reach their ends.
Inputs may be any that keep to these rules, and one draw needn't show every extreme that they name: `w_qkv`: a projection matrix of the normalised tokens to queries, keys and values.
All inputs are finite; a program needn't handle non-finite values.
Results may differ from the reference program's by a relative error of at most 0.02.
Values may be sent and summed in bfloat16 or wider, within the bound.
No kernel may reach another device: no remote copies, remote signals or barrier semaphores. Data moves between devices by JAX's collectives and lax.ppermute only.
A program may use at most 128 MiB of HBM per device.

```python
import jax
import jax.numpy as jnp
from jax import lax

D = 512
HEAD_DIM = 64
LEV = 2
WLAT = 6
WLON = 12
SLAT = 3
SLON = 6
NLAT = 192
NLON = 384


def draw_w_qkv(key, part):
    key = jax.random.fold_in(key, 11)
    base = jax.random.normal(key, (D, 3, D), jnp.float32) * D ** (-0.5)
    return base.astype(jnp.bfloat16)


def shard_levels(key, dims, cuts, smallest, largest):
    factor_of, own = 1.0, jax.random.fold_in(key, 6)
    for dim, shards_of in cuts:
        heights = jnp.exp(jax.random.uniform(jax.random.fold_in(own, dim), (shards_of,), jnp.float32, smallest / len(cuts), largest / len(cuts)))
        factor_of = factor_of * jnp.repeat(heights, dims[dim] // shards_of).reshape([-1 if axis == dim else 1 for axis in range(len(dims))])
    return factor_of


def scatter_about(key, dims, scale, reach, cuts=(), kind=jnp.bfloat16):
    entries = scale * jax.random.normal(key, dims, jnp.float32)
    if cuts:
        entries = entries * shard_levels(key, dims, cuts, -0.22, 0.18)
    return jnp.clip(entries, -reach, reach).astype(kind)


def setup_inputs(seed: int = 0) -> dict:
    seeds = jax.random.split(jax.random.key(seed), 7)
    tokens = scatter_about(seeds[0], (LEV, NLAT, NLON, D), 1.0, 6.0, ((1, 8), (2, 8)))
    cotangent = scatter_about(seeds[1], (LEV, NLAT, NLON, D), 1.0, 6.0, ((1, 8), (2, 8)))
    norm_gain = jnp.clip(1.0 + 0.18 * jax.random.normal(seeds[2], (D,), jnp.float32), 0.1, 1.9)
    norm_bias = scatter_about(seeds[3], (D,), 0.5, 3.0, (), jnp.float32)
    w_qkv = draw_w_qkv(jax.random.fold_in(seeds[6], 71), 0)
    w_out = scatter_about(seeds[5], (D, D), D ** -0.5, 0.25, ((0, 4),))
    return dict(tokens=tokens, cotangent=cotangent, norm_gain=norm_gain, norm_bias=norm_bias, w_qkv=w_qkv, w_out=w_out)


def mult(form, left, right):
    return jnp.einsum(form, left.astype(jnp.float32), right.astype(jnp.float32))

def windows(array):
    levels, rows, columns, width = array.shape
    array = array.reshape(levels, rows // WLAT, WLAT, columns // WLON, WLON, width)
    array = array.transpose(1, 3, 0, 2, 4, 5)
    return array.reshape(rows // WLAT * (columns // WLON), levels * WLAT * WLON, width)

def unwindows(array, levels, rows, columns):
    width = array.shape[-1]
    array = array.reshape(rows // WLAT, columns // WLON, levels, WLAT, WLON, width)
    return array.transpose(2, 0, 3, 1, 4, 5).reshape(levels, rows, columns, width)

def window_grad(normed, moved_grad, labels, w_qkv, w_out):
    levels, rows, columns, width = normed.shape
    head_cols = w_out.shape[0]
    heads = head_cols // HEAD_DIM
    normed_win = windows(normed)
    grads_win = windows(moved_grad)
    marks = windows(jnp.broadcast_to(labels[None, :, None, None], (levels, rows, columns, 1)))[:, :, 0]
    same = marks[:, :, None] == marks[:, None, :]
    count, span = (normed_win.shape[0], normed_win.shape[1])
    project = mult('nsd,dte->nste', normed_win, w_qkv).astype(jnp.bfloat16)
    project = project.reshape(count, span, 3, heads, HEAD_DIM)
    query, keys, values = (project[:, :, 0], project[:, :, 1], project[:, :, 2])
    scale = HEAD_DIM ** (-0.5)
    scores = mult('nqhc,nkhc->nhqk', query, keys) * scale
    scores = jnp.where(same[:, None], scores, -1e+30)
    top = lax.optimization_barrier(jnp.max(scores, axis=-1, keepdims=True))
    raised = jnp.exp(scores - top)
    probs = (raised / lax.optimization_barrier(jnp.sum(raised, axis=-1, keepdims=True))).astype(jnp.bfloat16)
    attended = mult('nhqk,nkhc->nqhc', probs, values).astype(jnp.bfloat16).reshape(count, span, head_cols)
    d_attended = mult('nsd,ed->nse', grads_win, w_out).astype(jnp.bfloat16)
    grad_out = mult('nse,nsd->ed', attended, grads_win)
    d_heads = d_attended.reshape(count, span, heads, HEAD_DIM)
    d_probs = mult('nqhc,nkhc->nhqk', d_heads, values)
    prob_f = probs.astype(jnp.float32)
    d_scores = (prob_f * (d_probs - lax.optimization_barrier(jnp.sum(prob_f * d_probs, axis=-1, keepdims=True))) * scale).astype(jnp.bfloat16)
    d_query = mult('nhqk,nkhc->nqhc', d_scores, keys).astype(jnp.bfloat16)
    d_keys = mult('nhqk,nqhc->nkhc', d_scores, query).astype(jnp.bfloat16)
    d_values = mult('nhqk,nqhc->nkhc', probs, d_heads).astype(jnp.bfloat16)
    d_project = jnp.stack([d_query, d_keys, d_values], axis=2).reshape(count, span, 3, head_cols)
    d_normed = mult('nste,dte->nsd', d_project, w_qkv)
    grad_qkv = mult('nsd,nste->dte', normed_win, d_project)
    return (unwindows(d_normed, levels, rows, columns), grad_qkv, grad_out)

def reference(tokens, cotangent, norm_gain, norm_bias, w_qkv, w_out):
    moved = jnp.roll(tokens, (-SLAT, -SLON), axis=(1, 2))
    moved_grad = jnp.roll(cotangent, (-SLAT, -SLON), axis=(1, 2))
    value = moved.astype(jnp.float32)
    centered = value - lax.optimization_barrier(jnp.mean(value, axis=-1, keepdims=True))
    inv_std = lax.rsqrt(lax.optimization_barrier(jnp.mean(centered * centered, axis=-1, keepdims=True)) + 1e-05)
    unit = centered * inv_std
    normed = (unit * norm_gain + norm_bias).astype(jnp.bfloat16)
    bands = NLAT // WLAT
    normed_bands = normed.reshape(LEV, bands, WLAT, NLON, D).transpose(1, 0, 2, 3, 4)
    grad_bands = moved_grad.reshape(LEV, bands, WLAT, NLON, D).transpose(1, 0, 2, 3, 4)
    starts = jnp.arange(bands, dtype=jnp.int32) * WLAT

    def step(carry, inputs):
        band_normed, band_grad, start = inputs
        rows_global = start + jnp.arange(WLAT, dtype=jnp.int32)
        labels = (rows_global >= NLAT - SLAT).astype(jnp.int32)
        d_normed, grad_qkv, grad_out = window_grad(band_normed, band_grad, labels, w_qkv, w_out)
        return ((carry[0] + grad_qkv, carry[1] + grad_out), d_normed)
    init = (jnp.zeros((D, 3, D), jnp.float32), jnp.zeros((D, D), jnp.float32))
    (grad_qkv, grad_out), d_stack = lax.scan(step, init, (normed_bands, grad_bands, starts))
    d_normed = d_stack.transpose(1, 0, 2, 3, 4).reshape(LEV, NLAT, NLON, D)
    grad_gain = lax.optimization_barrier(jnp.sum(d_normed * unit, axis=(0, 1, 2)))
    grad_bias = lax.optimization_barrier(jnp.sum(d_normed, axis=(0, 1, 2)))
    scaled = d_normed * norm_gain
    d_moved = moved_grad.astype(jnp.float32) + inv_std * (scaled - lax.optimization_barrier(jnp.mean(scaled, axis=-1, keepdims=True)) - unit * lax.optimization_barrier(jnp.mean(scaled * unit, axis=-1, keepdims=True)))
    d_moved = d_moved.astype(jnp.bfloat16)
    grad_tokens = jnp.roll(d_moved, (SLAT, SLON), axis=(1, 2))
    return (grad_tokens, grad_gain, grad_bias, grad_qkv, grad_out)
```

```python
import jax
import jax.numpy as jnp
from jax import lax
from jax.experimental import pallas as pl
from jax.experimental.pallas import tpu as pltpu
from jax.sharding import PartitionSpec as P

HEAD = 64
SLAT = 3
SLON = 6
SPAN = 144
QUART = 4 * SPAN
D = 512
BF = jnp.bfloat16
F32 = jnp.float32
NT = (((1,), (1,)), ((), ()))
NN = (((1,), (0,)), ((), ()))
TN = (((0,), (0,)), ((), ()))


def dot(a, b, form):
    return lax.dot_general(a, b, form, preferred_element_type=F32)


def move(block, axes, step):
    sizes = [lax.axis_size(axis) for axis in axes]

    def index(coords):
        flat = 0
        for size, coord in zip(sizes, coords):
            flat = flat * size + coord % size
        return flat

    def coords(flat):
        out = []
        for size in reversed(sizes):
            out.append(flat % size)
            flat //= size
        return tuple(reversed(out))

    total = 1
    for size in sizes:
        total *= size
    route = []
    for source in range(total):
        target = step(*coords(source))
        if target is not None:
            route.append((source, index(target)))
    return lax.ppermute(block, axes, route)


def window_pair(ref, column):
    first = ref[:, :, column : column + 8, :].reshape(96, D)
    middle = ref[:, :, column + 8 : column + 16, :]
    last = ref[:, :, column + 16 : column + 24, :].reshape(96, D)
    low, high = middle[0], middle[1]
    turned_low, turned_high = pltpu.roll(low, 4, 1), pltpu.roll(high, 4, 1)
    top = lax.broadcasted_iota(jnp.int32, (6, 8, D), 1) < 4
    mid_a = jnp.where(top, low, turned_high).reshape(48, D)
    mid_b = jnp.where(top, turned_low, high).reshape(48, D)
    return jnp.concatenate([first, mid_a], 0), jnp.concatenate([last, mid_b], 0)


def normalised(x):
    mean = jnp.sum(x, axis=-1, keepdims=True) * (1.0 / D)
    centered = x - mean
    inv_std = lax.rsqrt(jnp.sum(centered * centered, axis=-1, keepdims=True) * (1.0 / D) + 1e-05)
    return centered * inv_std, inv_std


def main_kernel(
    order, edge,
    tok_a, tok_b, cot_a, cot_b, h_lat, h_lon_a, h_lon_b, h_cor, gain_ref, bias_ref, wt_ref, wo_ref,
    dn_ref, x_ref, g_ref, gq_ref, go_ref, gb_ref,
    xs, gs, bias_s,
):
    step = pl.program_id(0)
    row = order[step]
    last = row == 3

    @pl.when(step == 0)
    def _():
        gq_ref[...] = jnp.zeros_like(gq_ref)
        go_ref[...] = jnp.zeros_like(go_ref)
        gb_ref[...] = jnp.zeros_like(gb_ref)

    for scratch, a, b, part in ((xs, tok_a, tok_b, 0), (gs, cot_a, cot_b, 2)):
        scratch[:, 0:3, 0:48, :] = a[...].astype(F32)
        scratch[:, 0:3, 48:54, :] = h_lon_a[part : part + 2].astype(F32)

        @pl.when(jnp.logical_not(last))
        def _():
            scratch[:, 3:6, 0:48, :] = b[...].astype(F32)
            scratch[:, 3:6, 48:54, :] = h_lon_b[part : part + 2].astype(F32)

        @pl.when(last)
        def _():
            scratch[:, 3:6, 0:48, :] = h_lat[part : part + 2].astype(F32)
            scratch[:, 3:6, 48:54, :] = h_cor[part : part + 2].astype(F32)

    key_row = lax.broadcasted_iota(jnp.int32, (SPAN, SPAN), 0) // 8 % 6
    query_row = lax.broadcasted_iota(jnp.int32, (SPAN, SPAN), 1) // 8 % 6
    apart = ((key_row >= 3) != (query_row >= 3)) & (edge[0] == 1) & last
    bias_s[...] = jnp.where(apart, -1e30, 0.0)

    norm_gain = gain_ref[...]
    norm_bias = bias_ref[...]
    left = lax.broadcasted_iota(jnp.int32, (SPAN, 128), 1) < HEAD
    for pair in range(2):
        tokens = window_pair(xs, SLON + 24 * pair)
        grads = window_pair(gs, SLON + 24 * pair)
        for half in range(2):
            w = 2 * pair + half
            x = tokens[half]
            g = grads[half].astype(BF)
            x_ref[0, w] = x.astype(BF)
            g_ref[0, w] = g
            unit, _ = normalised(x)
            normed = (unit * norm_gain + norm_bias).astype(BF)
            kv = dot(normed, wt_ref[128:384, :], NT).astype(BF)
            proj = dot(wt_ref[...], normed, NT).astype(BF)
            da = dot(wo_ref[...], g, NT).astype(BF)
            q = proj[0:128] * 0.125
            k, v = proj[128:256], proj[256:384]
            kt, vt = kv[:, 0:128], kv[:, 128:256]
            zero = jnp.zeros_like(kt)
            kt2 = jnp.concatenate([jnp.where(left, kt, zero), jnp.where(left, zero, kt)], 0)
            vt2 = jnp.concatenate([jnp.where(left, vt, zero), jnp.where(left, zero, vt)], 0)
            scores = dot(kt2, q, NN)
            d_probs = dot(vt2, da, NN)
            att, dq, dk, dv = [], [], [], []
            for head in range(2):
                cut = slice(head * HEAD, (head + 1) * HEAD)
                s = scores[head * SPAN : (head + 1) * SPAN] + bias_s[...]
                raised = jnp.exp(s - jnp.max(s, axis=0, keepdims=True))
                probs = (raised * (1.0 / jnp.sum(raised, axis=0, keepdims=True))).astype(BF)
                pf = probs.astype(F32)
                dp = d_probs[head * SPAN : (head + 1) * SPAN]
                ds = (pf * (dp - jnp.sum(pf * dp, axis=0, keepdims=True))).astype(BF)
                att.append(dot(v[cut], probs, NN).astype(BF))
                dv.append(dot(da[cut], probs, NT).astype(BF))
                dq.append((dot(k[cut], ds, NN) * 0.125).astype(BF))
                dk.append(dot(q[cut], ds, NT).astype(BF))
            attended = jnp.concatenate(att, 0)
            d_project = jnp.concatenate(dq + dk + dv, 0)
            go_ref[...] += dot(attended, g, NN)
            gq_ref[...] += dot(d_project, normed, NN)
            dn = dot(d_project, wt_ref[...], TN)
            gb_ref[0:8, :] += jnp.sum((dn * unit).reshape(SPAN // 8, 8, D), axis=0)
            gb_ref[8:16, :] += jnp.sum(dn.reshape(SPAN // 8, 8, D), axis=0)
            dn_ref[0, w] = dn.astype(BF)


def main_call(order, edge, tokens, cotangent, h_lat, h_lon, h_cor, gain, bias, wt, wo):
    rows = (2, 3, 48, D)

    def a_map(i, order, edge):
        return (0, 2 * order[i] + 1, 0, 0)

    def b_map(i, order, edge):
        return (0, jnp.minimum(2 * order[i] + 2, 7), 0, 0)

    def const(n):
        return lambda i, order, edge: (0,) * n

    def out_map(i, order, edge):
        return (i, 0, 0, 0)

    windows = jax.ShapeDtypeStruct((4, 4, SPAN, D), BF)
    win_spec = pl.BlockSpec((1, 4, SPAN, D), out_map)
    return pl.pallas_call(
        main_kernel,
        grid_spec=pltpu.PrefetchScalarGridSpec(
            num_scalar_prefetch=2,
            grid=(4,),
            in_specs=[
                pl.BlockSpec(rows, a_map),
                pl.BlockSpec(rows, b_map),
                pl.BlockSpec(rows, a_map),
                pl.BlockSpec(rows, b_map),
                pl.BlockSpec((4, 3, 48, D), const(4)),
                pl.BlockSpec((4, 3, 6, D), a_map),
                pl.BlockSpec((4, 3, 6, D), b_map),
                pl.BlockSpec((4, 3, 6, D), const(4)),
                pl.BlockSpec((1, D), const(2)),
                pl.BlockSpec((1, D), const(2)),
                pl.BlockSpec((384, D), const(2)),
                pl.BlockSpec((128, D), const(2)),
            ],
            out_specs=[
                win_spec,
                win_spec,
                win_spec,
                pl.BlockSpec((384, D), const(2)),
                pl.BlockSpec((128, D), const(2)),
                pl.BlockSpec((16, D), const(2)),
            ],
            scratch_shapes=[
                pltpu.VMEM((2, 6, 56, D), F32),
                pltpu.VMEM((2, 6, 56, D), F32),
                pltpu.VMEM((SPAN, SPAN), F32),
            ],
        ),
        out_shape=[
            windows,
            windows,
            windows,
            jax.ShapeDtypeStruct((384, D), F32),
            jax.ShapeDtypeStruct((128, D), F32),
            jax.ShapeDtypeStruct((16, D), F32),
        ],
        compiler_params=pltpu.CompilerParams(
            dimension_semantics=("arbitrary",), vmem_limit_bytes=48 * 1024 * 1024
        ),
        cost_estimate=pl.CostEstimate(
            flops=8_000_000_000, bytes_accessed=20_000_000, transcendentals=700_000
        ),
    )(order, edge, tokens, tokens, cotangent, cotangent, h_lat, h_lon, h_lon, h_cor, gain, bias, wt, wo)


def norm_kernel(d_a, d_b, x_ref, g_ref, gain_ref, out_ref, scratch):
    gain = gain_ref[...]
    top = lax.broadcasted_iota(jnp.int32, (6, 8, D), 1) < 4
    for pair in range(2):
        moved = []
        for half in range(2):
            w = 2 * pair + half
            unit, inv_std = normalised(x_ref[0, w].astype(F32))
            d_normed = d_a[w].astype(F32) + d_b[w].astype(F32)
            scaled = d_normed * gain
            mean = jnp.sum(scaled, axis=-1, keepdims=True) * (1.0 / D)
            along = jnp.sum(scaled * unit, axis=-1, keepdims=True) * (1.0 / D)
            moved.append(g_ref[0, w].astype(F32) + inv_std * (scaled - mean - unit * along))
        a, b = moved
        mid_a, mid_b = a[96:].reshape(6, 8, D), b[96:].reshape(6, 8, D)
        low = jnp.where(top, mid_a, pltpu.roll(mid_b, 4, 1))
        high = jnp.where(top, pltpu.roll(mid_a, 4, 1), mid_b)
        column = 24 * pair
        scratch[:, :, column : column + 8, :] = a[:96].reshape(2, 6, 8, D)
        scratch[0, :, column + 8 : column + 16, :] = low
        scratch[1, :, column + 8 : column + 16, :] = high
        scratch[:, :, column + 16 : column + 24, :] = b[:96].reshape(2, 6, 8, D)
    out_ref[...] = scratch[...].astype(BF)


def norm_call(d_a, d_b, x, g, gain):
    win_spec = pl.BlockSpec((1, 4, SPAN, D), lambda i: (3, 0, 0, 0))
    return pl.pallas_call(
        norm_kernel,
        grid=(1,),
        in_specs=[
            pl.BlockSpec((4, SPAN, D), lambda i: (0, 0, 0)),
            pl.BlockSpec((4, SPAN, D), lambda i: (0, 0, 0)),
            win_spec,
            win_spec,
            pl.BlockSpec((1, D), lambda i: (0, 0)),
        ],
        out_specs=pl.BlockSpec((2, 6, 48, D), lambda i: (0, 0, 0, 0)),
        out_shape=jax.ShapeDtypeStruct((2, 6, 48, D), BF),
        scratch_shapes=[pltpu.VMEM((2, 6, 48, D), F32)],
        compiler_params=pltpu.CompilerParams(vmem_limit_bytes=48 * 1024 * 1024),
        cost_estimate=pl.CostEstimate(flops=6_000_000, bytes_accessed=3_000_000, transcendentals=600),
    )(d_a, d_b, x, g, gain)


def per_device(tokens, cotangent, norm_gain, norm_bias, w_qkv, w_out):
    tp = lax.axis_index("tp")
    core, y = tp % 2, tp // 2
    order = jnp.stack([2 * (1 - y) + 1 - core, 2 * y + 1 - core, 2 * (1 - y) + core, tp]).astype(jnp.int32)
    edge = (lax.axis_index("lat") == lax.axis_size("lat") - 1).astype(jnp.int32).reshape(1)
    both = [tokens, cotangent]
    h_lat = move(
        jnp.concatenate([t[:, :SLAT] for t in both], 0), ("lat",), lambda a: (a - 1,)
    )
    h_lon = move(
        jnp.concatenate([t[:, :, :SLON] for t in both], 0), ("lon",), lambda a: (a - 1,)
    )
    h_cor = move(
        jnp.concatenate([t[:, :SLAT, :SLON] for t in both], 0),
        ("lat", "lon"),
        lambda a, b: (a - 1, b - 1),
    )
    gain = norm_gain.reshape(1, D)
    bias = norm_bias.reshape(1, D)
    wt = w_qkv.transpose(1, 2, 0).reshape(384, D)
    dn, x, g, gq, go, gb = main_call(
        order, edge, tokens, cotangent, h_lat, h_lon, h_cor, gain, bias, wt, w_out
    )
    other = move(dn[0:2], ("tp",), lambda a: (a ^ 1,))
    small = jnp.stack([gb[0:8].sum(0), gb[8:16].sum(0)]).reshape(8, 128)
    small = small + move(small, ("tp",), lambda a: (a ^ 1,))
    small = small + move(small, ("tp",), lambda a: (a ^ 2,))
    half = (dn[2:4].astype(F32) + other.astype(F32)).astype(BF)
    arrived = move(half[0], ("tp",), lambda a: (a ^ 2,))
    tiles = lax.axis_size("lat") * lax.axis_size("lon")
    share = 2048 // tiles
    gq_rows = gq.reshape(3, 128, D).transpose(0, 2, 1).reshape(3 * D, 128)
    go_rows = go.reshape(128, 4, 128).transpose(1, 0, 2).reshape(512, 128)
    grads = jnp.concatenate([gq_rows, go_rows], 0).astype(BF).reshape(tiles, share, 128)
    small_hi = small.astype(BF)
    small_lo = (small - small_hi.astype(F32)).astype(BF)
    spread = jnp.stack([small_hi.reshape(tiles, 16), small_lo.reshape(tiles, 16)], 1)
    spread = jnp.pad(spread, ((0, 0), (0, 6), (0, 112)))
    parts = lax.all_to_all(
        jnp.concatenate([grads, spread], 1), ("lat", "lon"), 0, 0, tiled=True
    )
    total = jnp.sum(parts.astype(F32), axis=0)
    extra = total[share] + total[share + 1]
    extra_hi = extra.astype(BF)
    extra_lo = (extra - extra_hi.astype(F32)).astype(BF)
    total = jnp.concatenate(
        [total[:share].astype(BF), extra_hi[None], extra_lo[None], jnp.zeros((6, 128), BF)], 0
    )
    whole = lax.all_to_all(
        jnp.broadcast_to(total[None], (tiles, share + 8, 128)), ("lat", "lon"), 0, 0, tiled=True
    )
    rows = whole[:, :share].reshape(2048, 128).astype(F32)
    grad_qkv = rows[: 3 * D].reshape(3, D, 128).transpose(1, 0, 2)
    grad_out = rows[3 * D :].reshape(4, 128, 128).transpose(1, 0, 2).reshape(128, D)
    small = (whole[:, share, :16].astype(F32) + whole[:, share + 1, :16].astype(F32)).reshape(2, D)
    d_moved = norm_call(half[1], arrived, x, g, gain)
    over_y = move(d_moved, ("tp",), lambda a: (a ^ 2,))
    lower = jnp.where(y == 0, d_moved, over_y)
    upper = jnp.where(y == 0, over_y, d_moved)
    mine = jnp.stack([lower, upper])
    theirs = move(mine, ("tp",), lambda a: (a ^ 1,))
    even = jnp.where(core == 0, mine, theirs)
    odd = jnp.where(core == 0, theirs, mine)
    d_moved = jnp.concatenate([even[0], odd[0], even[1], odd[1]], 1)
    rear = move(d_moved[:, -SLAT:], ("lat",), lambda a: (a + 1,))
    d_moved = jnp.concatenate([rear, d_moved[:, :-SLAT]], axis=1)
    rear = move(d_moved[:, :, -SLON:], ("lon",), lambda a: (a + 1,))
    grad_tokens = jnp.concatenate([rear, d_moved[:, :, :-SLON]], axis=2)
    return (grad_tokens, small[0], small[1], grad_qkv, grad_out)


def solution(mesh):
    return jax.shard_map(
        per_device,
        mesh=mesh,
        in_specs=(
            P(None, "lat", "lon", None),
            P(None, "lat", "lon", None),
            P(),
            P(),
            P(None, None, "tp"),
            P("tp", None),
        ),
        out_specs=(P(None, "lat", "lon", None), P(), P(), P(None, None, "tp"), P("tp", None)),
        check_vma=False,
    )
```

```python
import jax
import jax.numpy as jnp
from jax import lax
from jax.experimental import pallas as pl
from jax.experimental.pallas import tpu as pltpu
from jax.sharding import PartitionSpec as P

HEAD = 64
SLAT = 3
SLON = 6
SPAN = 144
D = 512
BF = jnp.bfloat16
F32 = jnp.float32
NT = (((1,), (1,)), ((), ()))
NN = (((1,), (0,)), ((), ()))
TN = (((0,), (0,)), ((), ()))
VMEM_BYTES = 48 * 1024 * 1024

PLACE = (
    ((0, 0), (0, 1), (0, 2), (1, 2)),
    ((1, 0), (1, 1), (2, 0), (2, 1)),
    ((3, 0), (3, 1), (3, 2), (2, 2)),
    ((0, 3), (1, 3), (2, 3), (3, 3)),
)


def dot(a, b, form):
    return lax.dot_general(a, b, form, preferred_element_type=F32)


def move(block, axes, step):
    sizes = [lax.axis_size(axis) for axis in axes]
    total = 1
    for size in sizes:
        total *= size

    def index(coords):
        flat = 0
        for size, coord in zip(sizes, coords):
            flat = flat * size + coord % size
        return flat

    def coords(flat):
        out = []
        for size in reversed(sizes):
            out.append(flat % size)
            flat //= size
        return tuple(reversed(out))

    return lax.ppermute(block, axes, [(i, index(step(*coords(i)))) for i in range(total)])


def even_window(ref, row, column):
    rows = slice(row, row + 6)
    top = lax.broadcasted_iota(jnp.int32, (6, 8, D), 1) < 4
    full = ref[:, rows, column : column + 8, :].reshape(96, D)
    rest = jnp.where(
        top, ref[0, rows, column + 8 : column + 16, :], ref[1, rows, column + 4 : column + 12, :]
    )
    return jnp.concatenate([full, rest.reshape(48, D)], 0)


def odd_window(ref, row, column):
    rows = slice(row, row + 6)
    top = lax.broadcasted_iota(jnp.int32, (6, 8, D), 1) < 4
    full = ref[:, rows, column + 4 : column + 12, :].reshape(96, D)
    rest = jnp.where(
        top, ref[0, rows, column : column + 8, :], ref[1, rows, column - 4 : column + 4, :]
    )
    return jnp.concatenate([full, rest.reshape(48, D)], 0)


def normalised(x):
    mean = jnp.sum(x, axis=-1, keepdims=True) * (1.0 / D)
    centered = x - mean
    inv_std = lax.rsqrt(jnp.sum(centered * centered, axis=-1, keepdims=True) * (1.0 / D) + 1e-05)
    return centered * inv_std, inv_std


def window_step(x, g, gain, bias, wt_ref, wo_ref, mask, gq_acc, go_acc, gb_acc):
    unit, _ = normalised(x.astype(F32))
    normed = (unit * gain + bias).astype(BF)
    kv = dot(normed, wt_ref[128:384, :], NT).astype(BF)
    proj = dot(wt_ref[...], normed, NT).astype(BF)
    da = dot(wo_ref[...], g, NT).astype(BF)
    q = proj[0:128] * 0.125
    k, v = proj[128:256], proj[256:384]
    kt, vt = kv[:, 0:128], kv[:, 128:256]
    left = lax.broadcasted_iota(jnp.int32, (SPAN, 128), 1) < HEAD
    zero = jnp.zeros_like(kt)
    kt2 = jnp.concatenate([jnp.where(left, kt, zero), jnp.where(left, zero, kt)], 0)
    vt2 = jnp.concatenate([jnp.where(left, vt, zero), jnp.where(left, zero, vt)], 0)
    scores = dot(kt2, q, NN)
    d_probs = dot(vt2, da, NN)
    att, dq, dk, dv = [], [], [], []
    for head in range(2):
        cut = slice(head * HEAD, (head + 1) * HEAD)
        s = scores[head * SPAN : (head + 1) * SPAN]
        if mask is not None:
            s = s + mask
        raised = jnp.exp(s - jnp.max(s, axis=0, keepdims=True))
        probs = (raised * (1.0 / jnp.sum(raised, axis=0, keepdims=True))).astype(BF)
        pf = probs.astype(F32)
        dp = d_probs[head * SPAN : (head + 1) * SPAN]
        ds = (pf * (dp - jnp.sum(pf * dp, axis=0, keepdims=True))).astype(BF)
        att.append(dot(v[cut], probs, NN).astype(BF))
        dv.append(dot(da[cut], probs, NT).astype(BF))
        dq.append((dot(k[cut], ds, NN) * 0.125).astype(BF))
        dk.append(dot(q[cut], ds, NT).astype(BF))
    attended = jnp.concatenate(att, 0)
    d_project = jnp.concatenate(dq + dk + dv, 0)
    go_acc[...] += dot(attended, g, NN)
    gq_acc[...] += dot(d_project, normed, NN)
    dn = dot(d_project, wt_ref[...], TN)
    gb_acc[0:8, :] += jnp.sum((dn * unit).reshape(SPAN // 8, 8, D), axis=0)
    gb_acc[8:16, :] += jnp.sum(dn.reshape(SPAN // 8, 8, D), axis=0)
    return dn.astype(BF)


def group_steps(scalars, xw, gw, masks, gain_ref, bias_ref, wt_ref, wo_ref, accs, send, keep, x_out, g_out):
    gain, bias = gain_ref[...], bias_ref[...]
    for place in range(4):
        j = scalars[place]
        x, g = xw[j], gw[j]
        mask = None if masks is None else masks[scalars[4 + place]]
        dn = window_step(x, g, gain, bias, wt_ref, wo_ref, mask, *accs)
        target = send if place < 2 else keep
        target[place % 2, 0] = dn
    own = scalars[3]
    x_out[0] = xw[own]
    g_out[0] = gw[own]


def inner_kernel(
    scalars, t0, t1, t2, t3, c0, c1, c2, c3, gain_ref, bias_ref, wt_ref, wo_ref,
    send, keep, x_out, g_out, gq, go, gb, stage, xw, gw,
):
    step = pl.program_id(0)

    @pl.when(step == 0)
    def _():
        gq[...] = jnp.zeros_like(gq)
        go[...] = jnp.zeros_like(go)
        gb[...] = jnp.zeros_like(gb)

    for blocks, out in (((t0, t1, t2, t3), xw), ((c0, c1, c2, c3), gw)):
        for n, block in enumerate(blocks):
            stage[:, 3 * n : 3 * n + 3, :, :] = block[...].astype(F32)
        out[0] = even_window(stage, 0, SLON).astype(BF)
        out[1] = even_window(stage, 0, SLON + 12).astype(BF)

        @pl.when(step == 0)
        def _():
            out[2] = even_window(stage, 0, SLON + 24).astype(BF)
            out[3] = even_window(stage, 6, SLON + 24).astype(BF)

        @pl.when(step == 1)
        def _():
            out[2] = even_window(stage, 6, SLON).astype(BF)
            out[3] = even_window(stage, 6, SLON + 12).astype(BF)

    group_steps(
        scalars, xw, gw, None, gain_ref, bias_ref, wt_ref, wo_ref, (gq, go, gb), send, keep, x_out, g_out
    )


def row_kernel(
    scalars, t5, t6, t7, c5, c6, c7, h_lat, gain_ref, bias_ref, wt_ref, wo_ref, gq_in, go_in, gb_in,
    send, keep, x_out, g_out, gq, go, gb, stage, xw, gw, masks,
):
    gq[...] = gq_in[...]
    go[...] = go_in[...]
    gb[...] = gb_in[...]
    fill_masks(masks)
    for part, blocks, out in ((0, (t5, t6, t7), xw), (2, (c5, c6, c7), gw)):
        for n, block in enumerate(blocks):
            stage[:, 3 * n : 3 * n + 3, :, :] = block[...].astype(F32)
        stage[:, 9:12, :, :] = h_lat[part : part + 2].astype(F32)
        for j in range(3):
            out[j] = even_window(stage, 6, SLON + 12 * j).astype(BF)
        out[3] = even_window(stage, 0, SLON + 24).astype(BF)
    group_steps(
        scalars, xw, gw, masks, gain_ref, bias_ref, wt_ref, wo_ref, (gq, go, gb), send, keep, x_out, g_out
    )


def column_kernel(
    scalars, tok, cot, h_lat, mine, theirs, cor_mine, cor_theirs, gain_ref, bias_ref, wt_ref, wo_ref,
    gq_in, go_in, gb_in,
    send, keep, x_out, g_out, payload, gb, stage, xw, gw, masks, gq, go,
):
    gq[...] = gq_in[...]
    go[...] = go_in[...]
    gb[...] = gb_in[...]
    fill_masks(masks)
    core = scalars[8]
    for part, block, out in ((0, tok, xw), (2, cot, gw)):
        first = core == part // 2
        stage[:, 0:21, 0:16, :] = block[:, 3:24, :, :].astype(F32)
        stage[:, 21:24, 0:16, :] = h_lat[part : part + 2].astype(F32)
        lon = jnp.where(first, mine[...].astype(F32), theirs[...].astype(F32))
        cor = jnp.where(first, cor_mine[...].astype(F32), cor_theirs[...].astype(F32))
        stage[:, 0:21, 16:24, :] = lon[:, 3:24]
        stage[:, 21:24, 16:24, :] = cor
        for j in range(4):
            out[j] = odd_window(stage, 6 * j, 10).astype(BF)
    group_steps(
        scalars, xw, gw, masks, gain_ref, bias_ref, wt_ref, wo_ref, (gq, go, gb), send, keep, x_out, g_out
    )
    for t in range(3):
        payload[512 * t : 512 * t + 512, :] = gq[128 * t : 128 * t + 128, :].T.astype(BF)
    for n in range(4):
        payload[1536 + 128 * n : 1664 + 128 * n, :] = go[:, 128 * n : 128 * n + 128].astype(BF)


def fill_masks(masks):
    key_row = lax.broadcasted_iota(jnp.int32, (SPAN, SPAN), 0) // 8 % 6
    query_row = lax.broadcasted_iota(jnp.int32, (SPAN, SPAN), 1) // 8 % 6
    masks[0] = jnp.zeros((SPAN, SPAN), F32)
    masks[1] = jnp.where((key_row >= 3) != (query_row >= 3), -1e30, 0.0)


def const(n):
    return lambda i, scalars: (0,) * n


def whole(shape):
    return pl.BlockSpec(shape, const(len(shape)))


def rows_at(index):
    return pl.BlockSpec((2, 3, 48, D), lambda i, scalars: (0, index(i), 0, 0))


PARAMS = [(1, D), (1, D), (384, D), (128, D)]
SUMS = [((384, D), F32), ((128, D), F32), ((16, D), F32)]


def call(kernel, steps, scalars, specs, args, extra_out, scratch, flops):
    half = pl.BlockSpec((2, 1, SPAN, D), lambda i, scalars: (0, i, 0, 0))
    one = pl.BlockSpec((1, SPAN, D), lambda i, scalars: (i, 0, 0))
    outs = [((2, steps, SPAN, D), BF)] * 2 + [((steps, SPAN, D), BF)] * 2 + extra_out
    return pl.pallas_call(
        kernel,
        grid_spec=pltpu.PrefetchScalarGridSpec(
            num_scalar_prefetch=1,
            grid=(steps,),
            in_specs=specs,
            out_specs=[half, half, one, one] + [whole(shape) for shape, _ in extra_out],
            scratch_shapes=scratch,
        ),
        out_shape=[jax.ShapeDtypeStruct(*out) for out in outs],
        compiler_params=pltpu.CompilerParams(
            dimension_semantics=("arbitrary",), vmem_limit_bytes=VMEM_BYTES
        ),
        cost_estimate=pl.CostEstimate(
            flops=flops, bytes_accessed=steps * 4_000_000, transcendentals=steps * 170_000
        ),
    )(scalars, *args)


def norm_kernel(
    scalars, x1, x2, x3, g1, g2, g3, k1, r1, a1, k2, r2, a2, k3, r3, a3, gain_ref,
    out_ref, lat_ref, lon_ref, cor_ref,
):
    gain = gain_ref[...]
    last = []
    for group in range(4):
        if group < 2:
            x, g = x1[group], g1[group]
            parts = k1[1, group], r1[1, group], a1[group]
        elif group == 2:
            x, g = x2[0], g2[0]
            parts = k2[1, 0], r2[1, 0], a2[0]
        else:
            x, g = x3[0], g3[0]
            parts = k3[1, 0], r3[1, 0], a3[0]
        unit, inv_std = normalised(x.astype(F32))
        d_normed = parts[0].astype(F32) + parts[1].astype(F32) + parts[2].astype(F32)
        scaled = d_normed * gain
        mean = jnp.sum(scaled, axis=-1, keepdims=True) * (1.0 / D)
        along = jnp.sum(scaled * unit, axis=-1, keepdims=True) * (1.0 / D)
        moved = g.astype(F32) + inv_std * (scaled - mean - unit * along)
        out_ref[group] = moved.astype(BF)
        last.append(moved)
    row, column = last[2], last[3]
    corner_device = scalars[3] == 3
    edge = jnp.where(corner_device, column, row).reshape(3, 6, 8, D)[:, 3:6].reshape(72, D)
    lat_ref[...] = jnp.concatenate([edge, jnp.zeros((8, D), F32)], 0).astype(BF)
    lon_ref[...] = column[:96].astype(BF)
    cor_ref[...] = column[:96].reshape(2, 6, 8, D)[:, 3:6].reshape(48, D).astype(BF)


def simple(kernel, args, outs, scratch=(), scalars=None):
    count = 0 if scalars is None else 1

    def spec(shape):
        return pl.BlockSpec(shape, lambda i, *s: (0,) * len(shape))

    many = isinstance(outs, list)
    out_list = outs if many else [outs]
    result = pl.pallas_call(
        kernel,
        grid_spec=pltpu.PrefetchScalarGridSpec(
            num_scalar_prefetch=count,
            grid=(1,),
            in_specs=[spec(a.shape) for a in args],
            out_specs=[spec(shape) for shape, _ in out_list],
            scratch_shapes=scratch,
        ),
        out_shape=[jax.ShapeDtypeStruct(*out) for out in out_list],
        compiler_params=pltpu.CompilerParams(vmem_limit_bytes=VMEM_BYTES),
        cost_estimate=pl.CostEstimate(flops=5_000_000, bytes_accessed=4_000_000, transcendentals=0),
    )(*([] if scalars is None else [scalars]), *args)
    return result if many else result[0]


def sum_kernel(parts, out):
    total = jnp.sum(parts[...].astype(F32), axis=0)
    extra = total[32:33] + total[33:34]
    high = extra.astype(BF).astype(F32)
    total = jnp.concatenate([total[:32], high, extra - high, jnp.zeros((6, 128), F32)], 0)
    out[...] = jnp.broadcast_to(total.astype(BF)[None], out.shape)


def unpack_kernel(parts, gq, go, small):
    values = parts[...].astype(F32)
    rows = values[:, :32].reshape(2048, 128)
    for t in range(3):
        gq[t] = rows[512 * t : 512 * t + 512]
    for n in range(4):
        go[:, 128 * n : 128 * n + 128] = rows[1536 + 128 * n : 1664 + 128 * n]
    small[...] = values[:, 32] + values[:, 33]


def tile_kernel(scalars, a, b, c, d, ha, hb, hc, hd, out, windows, halos, stage):
    for n, (ref, halo) in enumerate(((a, ha), (b, hb), (c, hc), (d, hd))):
        windows[n] = ref[...]
        halos[n] = halo[...]
    core, y = scalars[8], scalars[9]

    def holder(j):
        return jnp.where(core == j % 2, 0, 2) + jnp.where(y == j // 2, 0, 1)

    for j in range(4):
        edge = halos[holder(j ^ 2), 0:80, :].astype(F32)[:72].reshape(3, 3, 8, D)
        column = 14 + 12 * j
        wide, narrow = (0, 8) if j < 3 else (4, 0)
        stage[:, 0:3, column + wide : column + wide + 8, :] = edge[0:2]
        stage[0, 0:3, column + narrow : column + narrow + 4, :] = edge[2, :, 0:4]
        stage[1, 0:3, column + narrow : column + narrow + 4, :] = edge[2, :, 4:8]
        rows = 6 if j < 3 else 3
        strip = halos[holder(j), 80:176, :].astype(F32).reshape(2, 6, 8, D)
        stage[:, 3 + 6 * j : 3 + 6 * j + rows, 6:14, :] = strip[:, :rows]
    stage[:, 0:3, 6:14, :] = halos[holder(3), 176:224, :].astype(F32).reshape(2, 3, 8, D)
    for group in range(4):
        for j in range(4):
            row, col = PLACE[group][j]
            rows = 6 if row < 3 else 3
            value = windows[holder(j), group].astype(F32)
            full = value[:96].reshape(2, 6, 8, D)[:, :rows]
            rest = value[96:].reshape(6, 8, D)[:rows]
            column = 14 + 12 * col
            wide, narrow = (0, 8) if group < 3 else (4, 0)
            at = slice(3 + 6 * row, 3 + 6 * row + rows)
            stage[:, at, column + wide : column + wide + 8, :] = full
            stage[0, at, column + narrow : column + narrow + 4, :] = rest[:, 0:4]
            stage[1, at, column + narrow : column + narrow + 4, :] = rest[:, 4:8]
    out[...] = stage[:, :, 8:56, :].astype(BF)


def per_device(tokens, cotangent, norm_gain, norm_bias, w_qkv, w_out):
    tp = lax.axis_index("tp")
    core, y = tp % 2, tp // 2
    edge = lax.axis_index("lat") == lax.axis_size("lat") - 1
    order = jnp.stack([2 * (1 - y) + 1 - core, 2 * y + 1 - core, 2 * (1 - y) + core, tp])
    place = jnp.stack([core, y])

    def scalars(masked):
        return jnp.concatenate([order, jnp.where(edge & masked, 1, 0), place]).astype(jnp.int32)

    no_mask = scalars(order < 0)
    row_mask = scalars(order < 3)
    column_mask = scalars(order == 3)

    h_lat = move(
        jnp.concatenate([tokens[:, :SLAT], cotangent[:, :SLAT]], 0),
        ("lat", "tp"),
        lambda a, t: (a - 1, t ^ 2),
    )
    strip = jnp.where(core == 0, tokens[:, :, :8], cotangent[:, :, :8])
    h_lon = move(strip, ("lon",), lambda a: (a - 1,))
    h_cor = move(strip[:, :SLAT], ("lat", "lon"), lambda a, b: (a - 1, b - 1))

    params = [norm_gain.reshape(1, D), norm_bias.reshape(1, D), w_qkv.transpose(1, 2, 0).reshape(384, D), w_out]
    param_specs = [whole(shape) for shape in PARAMS]
    sum_specs = [whole(shape) for shape, _ in SUMS]
    windows = [pltpu.VMEM((4, SPAN, D), BF)] * 2
    masks = [pltpu.VMEM((2, SPAN, SPAN), F32)]
    inner_rows = [rows_at(lambda i, n=n: 2 * i + n) for n in range(1, 5)]
    s1, k1, x1, g1, gq, go, gb = call(
        inner_kernel,
        2,
        no_mask,
        inner_rows + inner_rows + param_specs,
        [tokens] * 4 + [cotangent] * 4 + params,
        SUMS,
        [pltpu.VMEM((2, 12, 48, D), F32)] + windows,
        2_000_000_000,
    )
    r1 = move(s1, ("tp",), lambda t: (t ^ 1,))
    o_lon = move(h_lon, ("tp",), lambda t: (t ^ 1,))
    o_cor = move(h_cor, ("tp",), lambda t: (t ^ 1,))
    last_rows = [rows_at(lambda i, n=n: n) for n in (5, 6, 7)]
    s2, k2, x2, g2, gq, go, gb = call(
        row_kernel,
        1,
        row_mask,
        last_rows + last_rows + [whole((4, 3, 48, D))] + param_specs + sum_specs,
        [tokens] * 3 + [cotangent] * 3 + [h_lat] + params + [gq, go, gb],
        SUMS,
        [pltpu.VMEM((2, 12, 48, D), F32)] + windows + masks,
        1_000_000_000,
    )
    r2 = move(s2, ("tp",), lambda t: (t ^ 1,))
    a1 = move((k1[0].astype(F32) + r1[0].astype(F32)).astype(BF), ("tp",), lambda t: (t ^ 2,))
    strip_spec = pl.BlockSpec((2, 24, 16, D), lambda i, scalars: (0, 0, 2, 0))
    s3, k3, x3, g3, payload, gb = call(
        column_kernel,
        1,
        column_mask,
        [strip_spec, strip_spec, pl.BlockSpec((4, 3, 16, D), lambda i, scalars: (0, 0, 2, 0))]
        + [whole((2, 24, 8, D))] * 2
        + [whole((2, 3, 8, D))] * 2
        + param_specs
        + sum_specs,
        [tokens, cotangent, h_lat, h_lon, o_lon, h_cor, o_cor] + params + [gq, go, gb],
        [((2048, 128), BF), SUMS[2]],
        [pltpu.VMEM((2, 24, 24, D), F32)]
        + windows
        + masks
        + [pltpu.VMEM((384, D), F32), pltpu.VMEM((128, D), F32)],
        1_000_000_000,
    )
    r3 = move(s3, ("tp",), lambda t: (t ^ 1,))
    a2 = move((k2[0].astype(F32) + r2[0].astype(F32)).astype(BF), ("tp",), lambda t: (t ^ 2,))

    tiles = lax.axis_size("lat") * lax.axis_size("lon")
    small = jnp.sum(gb.reshape(2, 8, D), axis=1).reshape(tiles, 1, 16)
    small_high = small.astype(BF)
    small_low = (small - small_high.astype(F32)).astype(BF)
    ride = jnp.pad(jnp.concatenate([small_high, small_low], 1), ((0, 0), (0, 6), (0, 112)))
    packed = jnp.concatenate([payload.reshape(tiles, 32, 128), ride], 1)
    parts = lax.all_to_all(packed, ("lat", "lon"), 0, 0, tiled=True)
    a3 = move((k3[0].astype(F32) + r3[0].astype(F32)).astype(BF), ("tp",), lambda t: (t ^ 2,))
    spread = simple(sum_kernel, [parts], (parts.shape, BF))
    gathered = lax.all_to_all(spread, ("lat", "lon"), 0, 0, tiled=True)

    mine, lat_edge, lon_edge, cor_edge = simple(
        norm_kernel,
        [x1, x2, x3, g1, g2, g3, k1, r1, a1, k2, r2, a2, k3, r3, a3, params[0]],
        [((4, SPAN, D), BF), ((80, D), BF), ((96, D), BF), ((48, D), BF)],
        (),
        no_mask,
    )
    over_y = move(mine, ("tp",), lambda t: (t ^ 2,))
    lat_edge = move(lat_edge, ("lat", "tp"), lambda a, t: (a + 1, t ^ 2))
    lon_edge = move(lon_edge, ("lon",), lambda a: (a + 1,))
    cor_edge = move(cor_edge, ("lat", "lon"), lambda a, b: (a + 1, b + 1))
    edges = jnp.concatenate([lat_edge, lon_edge, cor_edge], 0)
    edges_y = move(edges, ("tp",), lambda t: (t ^ 2,))
    gathered_windows = [mine, over_y] + [move(v, ("tp",), lambda t: (t ^ 1,)) for v in (mine, over_y)]
    gathered_edges = [edges, edges_y] + [move(v, ("tp",), lambda t: (t ^ 1,)) for v in (edges, edges_y)]
    grad_tokens = simple(
        tile_kernel,
        gathered_windows + gathered_edges,
        (tokens.shape, BF),
        [
            pltpu.VMEM((4, 4, SPAN, D), BF),
            pltpu.VMEM((4, 224, D), BF),
            pltpu.VMEM((2, 24, 64, D), F32),
        ],
        no_mask,
    )
    grad_qkv, grad_out, small = simple(
        unpack_kernel,
        [gathered],
        [((3, D, 128), F32), ((128, D), F32), ((tiles, 128), F32)],
    )
    small = small + move(small, ("tp",), lambda t: (t ^ 1,))
    small = small + move(small, ("tp",), lambda t: (t ^ 2,))
    small = small[:, :16].reshape(2, D)
    return (grad_tokens, small[0], small[1], grad_qkv.transpose(1, 0, 2), grad_out)


def solution(mesh):
    return jax.shard_map(
        per_device,
        mesh=mesh,
        in_specs=(
            P(None, "lat", "lon", None),
            P(None, "lat", "lon", None),
            P(),
            P(),
            P(None, None, "tp"),
            P("tp", None),
        ),
        out_specs=(P(None, "lat", "lon", None), P(), P(), P(None, None, "tp"), P("tp", None)),
        check_vma=False,
    )
```

```python
import jax
import jax.numpy as jnp
from jax import lax
from jax.experimental import pallas as pl
from jax.experimental.pallas import tpu as pltpu
from jax.sharding import PartitionSpec as P

HEAD = 64
SLAT = 3
SLON = 6
SPAN = 144
D = 512
BF = jnp.bfloat16
F32 = jnp.float32
NT = (((1,), (1,)), ((), ()))
NN = (((1,), (0,)), ((), ()))
TN = (((0,), (0,)), ((), ()))
FLOPS = 4_000_000_000, 4_000_000_000, 50_000_000
INSIDE = pl.BlockSpec(memory_space=pltpu.VMEM)
ANYWHERE = pl.BlockSpec(memory_space=pl.ANY)
VMEM_BYTES = 32 * 1024 * 1024

PLACE = (
    ((0, 0), (0, 1), (0, 2), (1, 2)),
    ((1, 0), (1, 1), (2, 0), (2, 1)),
    ((3, 0), (3, 2), (3, 1), (2, 2)),
    ((0, 3), (1, 3), (2, 3), (3, 3)),
)


def dot(a, b, form):
    return lax.dot_general(a, b, form, preferred_element_type=F32)


def move(block, axes, step):
    sizes = [lax.axis_size(axis) for axis in axes]
    total = 1
    for size in sizes:
        total *= size

    def index(coords):
        flat = 0
        for size, coord in zip(sizes, coords):
            flat = flat * size + coord % size
        return flat

    def coords(flat):
        out = []
        for size in reversed(sizes):
            out.append(flat % size)
            flat //= size
        return tuple(reversed(out))

    return lax.ppermute(block, axes, [(i, index(step(*coords(i)))) for i in range(total)])


def even_window(ref, row, column):
    rows = slice(row, row + 6)
    top = lax.broadcasted_iota(jnp.int32, (6, 8, D), 1) < 4
    full = ref[:, rows, column : column + 8, :].reshape(96, D)
    rest = jnp.where(
        top, ref[0, rows, column + 8 : column + 16, :], ref[1, rows, column + 4 : column + 12, :]
    )
    return jnp.concatenate([full, rest.reshape(48, D)], 0)


def odd_window(ref, row, column):
    rows = slice(row, row + 6)
    top = lax.broadcasted_iota(jnp.int32, (6, 8, D), 1) < 4
    full = ref[:, rows, column + 4 : column + 12, :].reshape(96, D)
    rest = jnp.where(
        top, ref[0, rows, column : column + 8, :], ref[1, rows, column - 4 : column + 4, :]
    )
    return jnp.concatenate([full, rest.reshape(48, D)], 0)


def normalised(x):
    mean = jnp.sum(x, axis=-1, keepdims=True) * (1.0 / D)
    centered = x - mean
    inv_std = lax.rsqrt(jnp.sum(centered * centered, axis=-1, keepdims=True) * (1.0 / D) + 1e-05)
    return centered * inv_std, inv_std


def window_steps(xs, gs, gain, bias, weights, masks, sums, gb_acc):
    left = lax.broadcasted_iota(jnp.int32, (SPAN, 128), 1) < HEAD
    zero = jnp.zeros((SPAN, 128), BF)

    def by_head(a):
        return jnp.concatenate([jnp.where(left, a, zero), jnp.where(left, zero, a)], 0)

    count = range(len(xs))
    unit = [normalised(x.astype(F32))[0] for x in xs]
    normed = [(u * gain + bias).astype(BF) for u in unit]
    both = [(n, w) for n in count for w in range(2)]
    proj = {(n, w): dot(weights[w][0:384, :], normed[n], NT).astype(BF) for n, w in both}
    kv = {(n, w): dot(normed[n], weights[w][128:384, :], NT).astype(BF) for n, w in both}
    da = {(n, w): dot(weights[w][384:512, :], gs[n], NT).astype(BF) for n, w in both}
    q = {i: p[0:128] * 0.125 for i, p in proj.items()}
    k = {i: p[128:256] for i, p in proj.items()}
    v = {i: p[256:384] for i, p in proj.items()}
    scores = {i: dot(by_head(kv[i][:, 0:128]), q[i], NN) for i in both}
    d_probs = {i: dot(by_head(kv[i][:, 128:256]), da[i], NN) for i in both}
    heads = [(i, head) for i in both for head in range(2)]
    probs, ds = {}, {}
    for i, head in heads:
        s = scores[i][head * SPAN : (head + 1) * SPAN]
        if masks is not None:
            s = s + masks[i[0]]
        raised = jnp.exp(s - jnp.max(s, axis=0, keepdims=True))
        probs[i, head] = (raised * (1.0 / jnp.sum(raised, axis=0, keepdims=True))).astype(BF)
    for i, head in heads:
        pf = probs[i, head].astype(F32)
        dp = d_probs[i][head * SPAN : (head + 1) * SPAN]
        ds[i, head] = (pf * (dp - jnp.sum(pf * dp, axis=0, keepdims=True))).astype(BF)
    cuts = [slice(0, HEAD), slice(HEAD, 2 * HEAD)]
    att = {(i, h): dot(v[i][cuts[h]], probs[i, h], NN).astype(BF) for i, h in heads}
    dv = {(i, h): dot(da[i][cuts[h]], probs[i, h], NT).astype(BF) for i, h in heads}
    dq = {(i, h): (dot(k[i][cuts[h]], ds[i, h], NN) * 0.125).astype(BF) for i, h in heads}
    dk = {(i, h): dot(q[i][cuts[h]], ds[i, h], NT).astype(BF) for i, h in heads}
    attended = {i: jnp.concatenate([att[i, 0], att[i, 1]], 0) for i in both}
    d_project = {
        i: jnp.concatenate([dq[i, 0], dq[i, 1], dk[i, 0], dk[i, 1], dv[i, 0], dv[i, 1]], 0) for i in both
    }
    for w in range(2):
        sums[w][0:384, :] += sum(dot(d_project[n, w], normed[n], NN) for n in count)
        sums[w][384:512, :] += sum(dot(attended[n, w], gs[n], NN) for n in count)
    dn = [sum(dot(d_project[n, w], weights[w][0:384, :], TN) for w in range(2)) for n in count]
    gb_acc[0:8, :] += sum(jnp.sum((dn[n] * unit[n]).reshape(SPAN // 8, 8, D), axis=0) for n in count)
    gb_acc[8:16, :] += sum(jnp.sum(dn[n].reshape(SPAN // 8, 8, D), axis=0) for n in count)
    return [d.astype(BF) for d in dn]


def group_steps(scalars, xw, gw, masks, gain_ref, bias_ref, weights, sums, gb_acc, out):
    xs, gs = [xw[0, n] for n in range(2)], [gw[0, n] for n in range(2)]
    added = None if masks is None else [masks[scalars[n]] for n in range(2)]
    dn = window_steps(xs, gs, gain_ref[...], bias_ref[...], weights, added, sums, gb_acc)
    for n in range(2):
        out[0, n] = dn[n]


def inner_kernel(
    scalars, t0, t1, t2, t3, c0, c1, c2, c3, gain_ref, bias_ref, mine, theirs,
    dn, xw, gw, sum_mine, sum_theirs, gb, stage,
):
    step = pl.program_id(0)
    core = scalars[2]

    @pl.when(step == 0)
    def _():
        sum_mine[...] = jnp.zeros_like(sum_mine)
        sum_theirs[...] = jnp.zeros_like(sum_theirs)
        gb[...] = jnp.zeros_like(gb)

    for blocks, out in (((t0, t1, t2, t3), xw), ((c0, c1, c2, c3), gw)):
        for n, block in enumerate(blocks):
            stage[:, 3 * n : 3 * n + 3, :, :] = block[...].astype(F32)
        for group in range(2):
            for c in range(2):

                @pl.when((step == group) & (core == c))
                def _():
                    for n in range(2):
                        row, column = PLACE[group][2 * n + c]
                        out[0, n] = even_window(stage, 6 * (row - group), SLON + 12 * column).astype(BF)

    group_steps(
        scalars, xw, gw, None, gain_ref, bias_ref, (mine, theirs), (sum_mine, sum_theirs), gb, dn
    )


def row_kernel(
    scalars, t5, t6, t7, c5, c6, c7, h_lat, gain_ref, bias_ref, mine, theirs, in_mine, in_theirs, gb_in,
    dn, xw, gw, sum_mine, sum_theirs, gb, stage, masks,
):
    fill_masks(masks)
    core = scalars[2]
    for part, blocks, out in ((0, (t5, t6, t7), xw), (2, (c5, c6, c7), gw)):
        for n, block in enumerate(blocks):
            stage[:, 3 * n : 3 * n + 3, :, :] = block[...].astype(F32)
        for c in range(2):

            @pl.when(core == c)
            def _():
                stage[:, 9:12, 16 * c : 16 * c + 32, :] = h_lat[part : part + 2].astype(F32)
                for n in range(2):
                    row, column = PLACE[2][2 * n + c]
                    out[0, n] = even_window(stage, 6 * (row - 2), SLON + 12 * column).astype(BF)

    group_steps(
        scalars, xw, gw, masks, gain_ref, bias_ref, (mine, theirs), (sum_mine, sum_theirs), gb, dn
    )


def column_kernel(
    scalars, tok, cot, h_lat, h_lon, h_cor, gain_ref, bias_ref, mine, theirs, in_mine, in_theirs, gb_in,
    dn, xw, gw, sum_mine, sum_theirs, gb, payload_mine, payload_theirs, stage, masks,
):
    fill_masks(masks)
    core = scalars[2]
    for part, block, out in ((0, tok, xw), (2, cot, gw)):
        for n in range(2):
            stage[:, 6 * n : 6 * n + 3, 0:16, :] = block[:, pl.ds(3 + 12 * n + 6 * core, 3), :, :].astype(F32)
            stage[:, 6 * n : 6 * n + 6, 16:24, :] = h_lon[part : part + 2, 6 * n : 6 * n + 6].astype(F32)
        stage[:, 3:6, 0:16, :] = block[:, pl.ds(6 + 6 * core, 3), :, :].astype(F32)

        @pl.when(core == 0)
        def _():
            stage[:, 9:12, 0:16, :] = block[:, 18:21, :, :].astype(F32)

        @pl.when(core == 1)
        def _():
            stage[:, 9:12, 0:16, :] = h_lat[part : part + 2, :, 16:32, :].astype(F32)
            stage[:, 9:12, 16:24, :] = h_cor[part : part + 2].astype(F32)

        for n in range(2):
            out[0, n] = odd_window(stage, 6 * n, 10).astype(BF)
    group_steps(
        scalars, xw, gw, masks, gain_ref, bias_ref, (mine, theirs), (sum_mine, sum_theirs), gb, dn
    )
    for sums, payload in ((sum_mine, payload_mine), (sum_theirs, payload_theirs)):
        for t in range(3):
            rows = sums[128 * t : 128 * t + 128, :].T
            payload[512 * t : 512 * t + 512, :] = rows.astype(payload.dtype)
        for n in range(4):
            part = sums[384:512, 128 * n : 128 * n + 128]
            payload[1536 + 128 * n : 1664 + 128 * n, :] = part.astype(payload.dtype)


def fill_masks(masks):
    key_row = lax.broadcasted_iota(jnp.int32, (SPAN, SPAN), 0) // 8 % 6
    query_row = lax.broadcasted_iota(jnp.int32, (SPAN, SPAN), 1) // 8 % 6
    masks[0] = jnp.zeros((SPAN, SPAN), F32)
    masks[1] = jnp.where((key_row >= 3) != (query_row >= 3), -1e30, 0.0)


def rows_at(index):
    return pl.BlockSpec((2, 3, 48, D), lambda i, scalars: (0, index(i), 0, 0))


def whole(shape):
    return pl.BlockSpec(shape, lambda i, scalars: (0,) * len(shape))


def columns_at(start):
    return pl.BlockSpec((2, 24, 16, D), lambda i, scalars: (0, 0, start // 16, 0))


SUMS = [((512, D), F32), ((512, D), F32), ((16, D), F32)]


def kernel_call(kernel, steps, scalars, blocks, args, outs, scratch=(), waits=(), aliases=None, flops=5_000_000):
    many = isinstance(outs, list)
    out_list = outs if many else [outs]
    first = 1 + len(blocks) + len(args)

    def body(*refs):
        kernel(*refs[:first], *refs[first + len(waits) :])

    result = pl.pallas_call(
        body,
        grid_spec=pltpu.PrefetchScalarGridSpec(
            num_scalar_prefetch=1,
            grid=(steps,),
            in_specs=[spec for _, spec in blocks] + [INSIDE] * len(args) + [ANYWHERE] * len(waits),
            out_specs=[out[2] if len(out) > 2 else INSIDE for out in out_list],
            scratch_shapes=scratch,
        ),
        out_shape=[
            pltpu.HBM(*out[:2]) if len(out) > 2 else jax.ShapeDtypeStruct(*out) for out in out_list
        ],
        input_output_aliases=aliases or {},
        compiler_params=pltpu.CompilerParams(
            dimension_semantics=("arbitrary",), vmem_limit_bytes=VMEM_BYTES
        ),
        cost_estimate=pl.CostEstimate(flops=flops, bytes_accessed=1_000_000, transcendentals=0),
    )(
        scalars,
        *(pltpu.with_memory_space_constraint(array, pltpu.HBM) for array, _ in blocks),
        *args,
        *waits,
    )
    return result if many else result[0]


def group_call(kernel, steps, scalars, blocks, args, sums, extra_out, scratch, flops):
    pair = ((steps, 2, SPAN, D), BF, pl.BlockSpec((1, 2, SPAN, D), lambda i, scalars: (i, 0, 0, 0)))
    outs = [pair] * 3 + SUMS + extra_out
    start = 1 + len(blocks) + len(args)
    aliases = {start + n: 3 + n for n in range(len(sums))}
    return kernel_call(
        kernel, steps, scalars, blocks, args + sums, outs, scratch, (), aliases, flops
    )


def halo_kernel(scalars, t_rows, c_rows, t_cols, c_cols, w_ref, wo_ref, lat, lon, cor, weights):
    core = scalars[2]
    for part, rows, cols in ((0, t_rows, t_cols), (2, c_rows, c_cols)):
        for c in range(2):

            @pl.when(core == c)
            def _():
                lat[part : part + 2] = rows[:, :, 16 * c : 16 * c + 32, :]
                for n in range(4):
                    row = min(3 + 6 * c + 12 * (n // 2) + 3 * (n % 2), 21)
                    strip = cols[:, row : row + 3, :, :].astype(F32)[:, :, 0:8]
                    lon[part : part + 2, 3 * n : 3 * n + 3] = strip.astype(BF)

        cor[part : part + 2] = cols[:, 0:3, :, :].astype(F32)[:, :, 0:8].astype(BF)
    for t in range(3):
        weights[128 * t : 128 * t + 128, :] = w_ref[t].T
    weights[384:512, :] = wo_ref[...]


def moved_gradient(x, g, parts, gain):
    unit, inv_std = normalised(x.astype(F32))
    d_normed = parts[0].astype(F32) + parts[1].astype(F32)
    scaled = d_normed * gain
    mean = jnp.sum(scaled, axis=-1, keepdims=True) * (1.0 / D)
    along = jnp.sum(scaled * unit, axis=-1, keepdims=True) * (1.0 / D)
    return g.astype(F32) + inv_std * (scaled - mean - unit * along)


def norm_kernel(scalars, x, g, half, other, gain, out):
    for group in range(2):
        for n in range(2):
            parts = half[group, n], other[group, n]
            out[group, n] = moved_gradient(x[group, n], g[group, n], parts, gain[...]).astype(BF)


def last_norm_kernel(scalars, x2, g2, half2, x3, g3, half3, other2, other3, gain, out, lat, lon, cor):
    corner = scalars[2] == 1
    for n in range(2):
        row = moved_gradient(x2[0, n], g2[0, n], (half2[0, n], other2[0, n]), gain[...])
        column = moved_gradient(x3[0, n], g3[0, n], (half3[0, n], other3[0, n]), gain[...])
        out[0, n] = row.astype(BF)
        out[1, n] = column.astype(BF)
        if n == 1:
            row = jnp.where(corner, column, row)
            cor[...] = column[:96].reshape(2, 6, 8, D)[:, 3:6].reshape(48, D).astype(BF)
        edge = row.reshape(3, 6, 8, D)[:, 3:6].reshape(72, D)
        lat[n] = jnp.concatenate([edge, jnp.zeros((8, D), F32)], 0).astype(BF)
        lon[n] = column[:96].astype(BF)


def join_kernel(scalars, lat, lon, cor, out):
    out[0:80] = lat[0]
    out[80:160] = lat[1]
    out[160:256] = lon[0]
    out[256:352] = lon[1]
    out[352:400] = cor[...]


def pack_kernel(scalars, payload, other, gb, out):
    share = out.shape[0]
    rows = (payload[...] + other[...].astype(F32)).reshape(share, 2048 // share, 128)
    small = [jnp.sum(gb[8 * n : 8 * n + 8, :], axis=0, keepdims=True) for n in range(2)]
    small = jnp.concatenate([s[:, 128 * n : 128 * n + 128] for s in small for n in range(4)], 0)
    high = small.astype(BF).astype(F32)
    pair = jnp.concatenate([high[:, None], (small - high)[:, None], jnp.zeros((8, 6, 128), F32)], 1)
    ride = jnp.concatenate([pair, jnp.zeros((share - 8, 8, 128), F32)], 0)
    out[...] = jnp.concatenate([rows, ride], 1).astype(BF)


def sum_kernel(scalars, parts, out):
    out[...] = jnp.sum(parts[...].astype(F32), axis=0)


def spread_kernel(scalars, a, b, out):
    total = a[...] + b[...]
    rows = total.shape[0] - 8
    extra = total[rows : rows + 1] + total[rows + 1 : rows + 2]
    high = extra.astype(BF).astype(F32)
    total = jnp.concatenate([total[:rows], high, extra - high, jnp.zeros((6, 128), F32)], 0)
    out[...] = jnp.broadcast_to(total.astype(BF)[None], out.shape)


def unpack_kernel(scalars, parts, gq, go, small):
    values = parts[...].astype(F32)
    rows = values.shape[1] - 8
    small[...] = values[0:8, rows] + values[0:8, rows + 1]
    rows = values[:, :rows].reshape(2048, 128)
    for t in range(3):
        gq[t] = rows[512 * t : 512 * t + 512]
    for n in range(4):
        go[:, 128 * n : 128 * n + 128] = rows[1536 + 128 * n : 1664 + 128 * n]


def tile_kernel(scalars, a0, a1, b0, b1, ha, hb, out, windows, halos, stage):
    for n, (early, late, halo) in enumerate(((a0, a1, ha), (b0, b1, hb))):
        windows[n, 0:2] = early[...]
        windows[n, 2:4] = late[...]
        halos[n] = halo[...]
    core = scalars[2]

    def holder(j):
        return jnp.where(core == j % 2, 0, 1)

    for j in range(4):
        at = 80 * (j % 2)
        edge = halos[holder(j // 2), at : at + 80, :].astype(F32)[:72].reshape(3, 3, 8, D)
        column = 14 + 12 * j
        wide, narrow = (0, 8) if j < 3 else (4, 0)
        stage[:, 0:3, column + wide : column + wide + 8, :] = edge[0:2]
        stage[0, 0:3, column + narrow : column + narrow + 4, :] = edge[2, :, 0:4]
        stage[1, 0:3, column + narrow : column + narrow + 4, :] = edge[2, :, 4:8]
        rows = 6 if j < 3 else 3
        at = 160 + 96 * (j // 2)
        strip = halos[holder(j), at : at + 96, :].astype(F32).reshape(2, 6, 8, D)
        stage[:, 3 + 6 * j : 3 + 6 * j + rows, 6:14, :] = strip[:, :rows]
    stage[:, 0:3, 6:14, :] = halos[holder(3), 352:400, :].astype(F32).reshape(2, 3, 8, D)
    for group in range(4):
        for j in range(4):
            row, col = PLACE[group][j]
            rows = 6 if row < 3 else 3
            value = windows[holder(j), group, j // 2].astype(F32)
            full = value[:96].reshape(2, 6, 8, D)[:, :rows]
            rest = value[96:].reshape(6, 8, D)[:rows]
            column = 14 + 12 * col
            wide, narrow = (0, 8) if group < 3 else (4, 0)
            at = slice(3 + 6 * row, 3 + 6 * row + rows)
            stage[:, at, column + wide : column + wide + 8, :] = full
            stage[0, at, column + narrow : column + narrow + 4, :] = rest[:, 0:4]
            stage[1, at, column + narrow : column + narrow + 4, :] = rest[:, 4:8]
    out[...] = stage[:, :, 8:56, :].astype(BF)


def per_device(tokens, cotangent, norm_gain, norm_bias, w_qkv, w_out):
    core = lax.axis_index("tp") % 2
    edge = lax.axis_index("lat") == lax.axis_size("lat") - 1

    def scalars(first, second):
        masked = jnp.stack([edge & first, edge & second])
        return jnp.concatenate([jnp.where(masked, 1, 0), core.reshape(1)]).astype(jnp.int32)

    never = core < 0
    no_mask, row_mask, column_mask = scalars(never, never), scalars(core >= 0, core == 0), scalars(never, core == 1)

    def swap(block, bit):
        return move(block, ("tp",), lambda t: (t ^ bit,))

    both = (tokens, cotangent)
    h_lat, h_lon, h_cor, mine = kernel_call(
        halo_kernel,
        1,
        no_mask,
        [(t, rows_at(lambda i: 0)) for t in both] + [(t, columns_at(0)) for t in both],
        [w_qkv.transpose(1, 0, 2), w_out],
        [((4, 3, 32, D), BF), ((4, 12, 8, D), BF), ((4, 3, 8, D), BF), ((512, D), BF)],
    )
    theirs = swap(mine, 1)
    h_lat = move(h_lat, ("lat", "tp"), lambda a, t: (a - 1, t ^ 2))
    h_lon = move(h_lon, ("lon",), lambda a: (a - 1,))
    h_cor = move(h_cor, ("lat", "lon"), lambda a, b: (a - 1, b - 1))

    gain = norm_gain.reshape(1, D)
    params = [gain, norm_bias.reshape(1, D), mine, theirs]
    masks = [pltpu.VMEM((2, SPAN, SPAN), F32)]
    half1, x1, g1, *sums = group_call(
        inner_kernel,
        2,
        no_mask,
        [(t, rows_at(lambda i, n=n: 2 * i + n)) for t in both for n in (1, 2, 3, 4)],
        params,
        [],
        [],
        [pltpu.VMEM((2, 12, 48, D), F32)],
        FLOPS[0],
    )
    other1 = swap(half1, 2)
    half2, x2, g2, *sums = group_call(
        row_kernel,
        1,
        row_mask,
        [(t, rows_at(lambda i, n=n: n)) for t in both for n in (5, 6, 7)],
        [h_lat] + params,
        sums,
        [],
        [pltpu.VMEM((2, 12, 48, D), F32)] + masks,
        FLOPS[1],
    )
    other2 = swap(half2, 2)
    half3, x3, g3, _, _, gb, payload, payload_theirs = group_call(
        column_kernel,
        1,
        column_mask,
        [(t, columns_at(32)) for t in both],
        [h_lat, h_lon, h_cor] + params,
        sums,
        [((2048, 128), F32), ((2048, 128), BF)],
        [pltpu.VMEM((2, 12, 24, D), F32)] + masks,
        FLOPS[2],
    )
    other3 = swap(half3, 2)

    lats, lons = lax.axis_size("lat"), lax.axis_size("lon")
    tiles = lats // 2 * lons
    shares = ((tiles, 2048 // tiles + 8, 128), BF)
    halves = [[a * lons + b for a in range(half, lats, 2) for b in range(lons)] for half in range(2)]

    def exchange(block):
        return lax.all_to_all(block, ("lat", "lon"), 0, 0, axis_index_groups=halves, tiled=True)

    packed = kernel_call(
        pack_kernel, 1, no_mask, [], [payload, swap(payload_theirs, 1), gb], shares, (), [other1]
    )
    parts = exchange(packed)

    early = kernel_call(
        norm_kernel, 1, no_mask, [(a, whole(a.shape)) for a in (x1, g1, half1)], [other1, gain], (x1.shape, BF)
    )
    late, lat_edge, lon_edge, cor_edge = kernel_call(
        last_norm_kernel,
        1,
        no_mask,
        [(a, whole(a.shape)) for a in (x2, g2, half2, x3, g3, half3)],
        [other2, other3, gain],
        [((2, 2, SPAN, D), BF), ((2, 80, D), BF), ((2, 96, D), BF), ((48, D), BF)],
    )
    lat_edge = move(lat_edge, ("lat", "tp"), lambda a, t: (a + 1, t ^ 2))
    lon_edge = move(lon_edge, ("lon",), lambda a: (a + 1,))
    cor_edge = move(cor_edge, ("lat", "lon"), lambda a, b: (a + 1, b + 1))
    edges = kernel_call(join_kernel, 1, no_mask, [], [lat_edge, lon_edge, cor_edge], ((400, D), BF))
    total = kernel_call(sum_kernel, 1, no_mask, [], [parts], (shares[0][1:], F32))
    total_half = move(total, ("lat",), lambda a: (a ^ 1,))
    spread = kernel_call(spread_kernel, 1, no_mask, [], [total, total_half], shares, (), [late])
    gathered = exchange(spread)
    grad_tokens = kernel_call(
        tile_kernel,
        1,
        no_mask,
        [],
        [early, late, swap(early, 1), swap(late, 1), edges, swap(edges, 1)],
        (tokens.shape, BF, whole(tokens.shape)),
        [
            pltpu.VMEM((2, 4, 2, SPAN, D), BF),
            pltpu.VMEM((2, 400, D), BF),
            pltpu.VMEM((2, 24, 64, D), F32),
        ],
    )
    grad_qkv, grad_out, small = kernel_call(
        unpack_kernel,
        1,
        no_mask,
        [],
        [gathered],
        [((3, D, 128), F32, whole((3, D, 128))), ((128, D), F32, whole((128, D))), ((8, 128), F32)],
    )
    small = (small + swap(small, 1)) + (swap(small, 2) + swap(small, 3))
    small = small.reshape(2, D)
    return (grad_tokens, small[0], small[1], grad_qkv.transpose(1, 0, 2), grad_out)


def solution(mesh):
    return jax.shard_map(
        per_device,
        mesh=mesh,
        in_specs=(
            P(None, "lat", "lon", None),
            P(None, "lat", "lon", None),
            P(),
            P(),
            P(None, None, "tp"),
            P("tp", None),
        ),
        out_specs=(P(None, "lat", "lon", None), P(), P(), P(None, None, "tp"), P("tp", None)),
        check_vma=False,
    )
```

```python
import jax
import jax.numpy as jnp
from jax import lax
from jax.experimental import pallas as pl
from jax.experimental.pallas import tpu as pltpu
from jax.sharding import PartitionSpec as P

HEAD = 64
SLAT = 3
SLON = 6
SPAN = 144
D = 512
BF = jnp.bfloat16
F32 = jnp.float32
NT = (((1,), (1,)), ((), ()))
NN = (((1,), (0,)), ((), ()))
TN = (((0,), (0,)), ((), ()))
FLOPS = 4_000_000_000, 50_000_000, 50_000_000, 50_000_000, 8_000_000_000
INSIDE = pl.BlockSpec(memory_space=pltpu.VMEM)
ANYWHERE = pl.BlockSpec(memory_space=pl.ANY)
VMEM_BYTES = 32 * 1024 * 1024

PLACE = (
    ((0, 0), (2, 0), (0, 1), (2, 1)),
    ((1, 0), (0, 2), (1, 1), (1, 2)),
    ((3, 0), (3, 2), (3, 1), (2, 2)),
    ((0, 3), (1, 3), (2, 3), (3, 3)),
)


def dot(a, b, form):
    return lax.dot_general(a, b, form, preferred_element_type=F32)


def move(block, axes, step):
    sizes = [lax.axis_size(axis) for axis in axes]
    total = 1
    for size in sizes:
        total *= size

    def index(coords):
        flat = 0
        for size, coord in zip(sizes, coords):
            flat = flat * size + coord % size
        return flat

    def coords(flat):
        out = []
        for size in reversed(sizes):
            out.append(flat % size)
            flat //= size
        return tuple(reversed(out))

    return lax.ppermute(block, axes, [(i, index(step(*coords(i)))) for i in range(total)])


def even_window(ref, row, column):
    rows = slice(row, row + 6)
    top = lax.broadcasted_iota(jnp.int32, (6, 8, D), 1) < 4
    full = ref[:, rows, column : column + 8, :].reshape(96, D)
    rest = jnp.where(
        top, ref[0, rows, column + 8 : column + 16, :], ref[1, rows, column + 4 : column + 12, :]
    )
    return jnp.concatenate([full, rest.reshape(48, D)], 0)


def odd_window(ref, row, column):
    rows = slice(row, row + 6)
    top = lax.broadcasted_iota(jnp.int32, (6, 8, D), 1) < 4
    full = ref[:, rows, column + 4 : column + 12, :].reshape(96, D)
    rest = jnp.where(
        top, ref[0, rows, column : column + 8, :], ref[1, rows, column - 4 : column + 4, :]
    )
    return jnp.concatenate([full, rest.reshape(48, D)], 0)


def normalised(x):
    mean = jnp.sum(x, axis=-1, keepdims=True) * (1.0 / D)
    centered = x - mean
    inv_std = lax.rsqrt(jnp.sum(centered * centered, axis=-1, keepdims=True) * (1.0 / D) + 1e-05)
    return centered * inv_std, inv_std


def window_steps(xs, gs, gain, bias, weights, masks, sums, gb_acc):
    left = lax.broadcasted_iota(jnp.int32, (SPAN, 128), 1) < HEAD
    zero = jnp.zeros((SPAN, 128), BF)

    def by_head(a):
        return jnp.concatenate([jnp.where(left, a, zero), jnp.where(left, zero, a)], 0)

    count = range(len(xs))
    unit = [normalised(x.astype(F32))[0] for x in xs]
    normed = [(u * gain + bias).astype(BF) for u in unit]
    both = [(n, w) for n in count for w in range(2)]
    proj = {(n, w): dot(weights[w][0:384, :], normed[n], NT).astype(BF) for n, w in both}
    kv = {(n, w): dot(normed[n], weights[w][128:384, :], NT).astype(BF) for n, w in both}
    da = {(n, w): dot(weights[w][384:512, :], gs[n], NT).astype(BF) for n, w in both}
    q = {i: p[0:128] * 0.125 for i, p in proj.items()}
    k = {i: p[128:256] for i, p in proj.items()}
    v = {i: p[256:384] for i, p in proj.items()}
    scores = {i: dot(by_head(kv[i][:, 0:128]), q[i], NN) for i in both}
    d_probs = {i: dot(by_head(kv[i][:, 128:256]), da[i], NN) for i in both}
    heads = [(i, head) for i in both for head in range(2)]
    probs, ds = {}, {}
    for i, head in heads:
        s = scores[i][head * SPAN : (head + 1) * SPAN]
        if masks is not None:
            s = s + masks[i[0]]
        raised = jnp.exp(s - jnp.max(s, axis=0, keepdims=True))
        probs[i, head] = (raised * (1.0 / jnp.sum(raised, axis=0, keepdims=True))).astype(BF)
    for i, head in heads:
        pf = probs[i, head].astype(F32)
        dp = d_probs[i][head * SPAN : (head + 1) * SPAN]
        ds[i, head] = (pf * (dp - jnp.sum(pf * dp, axis=0, keepdims=True))).astype(BF)
    cuts = [slice(0, HEAD), slice(HEAD, 2 * HEAD)]
    att = {(i, h): dot(v[i][cuts[h]], probs[i, h], NN).astype(BF) for i, h in heads}
    dv = {(i, h): dot(da[i][cuts[h]], probs[i, h], NT).astype(BF) for i, h in heads}
    dq = {(i, h): (dot(k[i][cuts[h]], ds[i, h], NN) * 0.125).astype(BF) for i, h in heads}
    dk = {(i, h): dot(q[i][cuts[h]], ds[i, h], NT).astype(BF) for i, h in heads}
    attended = {i: jnp.concatenate([att[i, 0], att[i, 1]], 0) for i in both}
    d_project = {
        i: jnp.concatenate([dq[i, 0], dq[i, 1], dk[i, 0], dk[i, 1], dv[i, 0], dv[i, 1]], 0) for i in both
    }
    for w in range(2):
        sums[w][0:384, :] += sum(dot(d_project[n, w], normed[n], NN) for n in count)
        sums[w][384:512, :] += sum(dot(attended[n, w], gs[n], NN) for n in count)
    dn = [sum(dot(d_project[n, w], weights[w][0:384, :], TN) for w in range(2)) for n in count]
    gb_acc[0:8, :] += sum(jnp.sum((dn[n] * unit[n]).reshape(SPAN // 8, 8, D), axis=0) for n in count)
    gb_acc[8:16, :] += sum(jnp.sum(dn[n].reshape(SPAN // 8, 8, D), axis=0) for n in count)
    return [d.astype(BF) for d in dn]


def group_steps(scalars, windows, stores, masks, gain_ref, bias_ref, weights, sums, gb_acc, out):
    for store in stores:
        store.start()
    xs, gs = ([ref[n] for n in range(2)] for ref in windows)
    added = None if masks is None else [masks[scalars[n]] for n in range(2)]
    dn = window_steps(xs, gs, gain_ref[...], bias_ref[...], weights, added, sums, gb_acc)
    for n in range(2):
        out[0, n] = dn[n]
    for store in stores:
        store.wait()


def inner_kernel(group):
    def kernel(scalars, *refs):
        core = scalars[2]
        if group == 0:
            hbm, refs = refs[:2], refs[2:]
            gain, bias, mine, theirs, dn, x_out, g_out, sum_mine, sum_theirs, gb, *tiles = refs[:12]
            stage, xw, gw, sems, load_sems = refs[12:]
            pieces = ((3 + 12 * core, 6), (9, 6), (15 - 12 * core, 6), (21, 3))
            loads = [
                [
                    pltpu.make_async_copy(
                        hbm[n].at[:, pl.ds(start, rows)], tiles[n].at[:, pl.ds(start, rows)], load_sems.at[n, m]
                    )
                    for n in range(2)
                ]
                for m, (start, rows) in enumerate(pieces)
            ]
            for piece in loads:
                for load in piece:
                    load.start()
            sum_mine[...] = jnp.zeros_like(sum_mine)
            sum_theirs[...] = jnp.zeros_like(sum_theirs)
            gb[...] = jnp.zeros_like(gb)
            for load in loads[0]:
                load.wait()
            rows = [2 * core]
        else:
            tiles, refs = refs[:2], refs[2:]
            gain, bias, mine, theirs = refs[:4]
            dn, x_out, g_out, sum_mine, sum_theirs, gb, stage, xw, gw, sems = refs[7:]
            loads = []
            rows = [1 - core, 1]
        for tile, out in zip(tiles, (xw, gw)):
            for n, row in enumerate(rows):
                stage[:, 6 * n : 6 * n + 6, :, :] = tile[:, pl.ds(3 + 6 * row, 6), :, :].astype(F32)
            for c in range(2):

                @pl.when(core == c)
                def _():
                    for n in range(2):
                        column = PLACE[group][2 * n + c][1]
                        out[n] = even_window(stage, 6 * n * group, SLON + 12 * column).astype(BF)

        stores = stores_of(xw, gw, x_out, g_out, sems)
        group_steps(
            scalars, (xw, gw), stores, None, gain, bias, (mine, theirs), (sum_mine, sum_theirs), gb, dn
        )
        for piece in loads[1:]:
            for load in piece:
                load.wait()

    return kernel


def stores_of(xw, gw, x_out, g_out, sems):
    return [pltpu.make_async_copy(xw, x_out.at[0], sems.at[0]), pltpu.make_async_copy(gw, g_out.at[0], sems.at[1])]


def row_kernel(
    scalars, tok, cot, h_lat, gain_ref, bias_ref, mine, theirs, in_mine, in_theirs, gb_in,
    dn, x_out, g_out, sum_mine, sum_theirs, gb, stage, xw, gw, sems, masks,
):
    fill_masks(masks)
    core = scalars[2]
    for part, tile, out in ((0, tok, xw), (2, cot, gw)):
        stage[:, 0:9, :, :] = tile[:, 15:24, :, :].astype(F32)
        for c in range(2):

            @pl.when(core == c)
            def _():
                stage[:, 9:12, 16 * c : 16 * c + 32, :] = h_lat[part : part + 2].astype(F32)
                for n in range(2):
                    row, column = PLACE[2][2 * n + c]
                    out[n] = even_window(stage, 6 * (row - 2), SLON + 12 * column).astype(BF)

    stores = stores_of(xw, gw, x_out, g_out, sems)
    group_steps(
        scalars, (xw, gw), stores, masks, gain_ref, bias_ref, (mine, theirs), (sum_mine, sum_theirs), gb, dn
    )


def column_kernel(
    scalars, tok, cot, h_lat, h_lon, h_cor, gain_ref, bias_ref, mine, theirs, in_mine, in_theirs, gb_in,
    dn, x_out, g_out, sum_mine, sum_theirs, gb, payload_mine, first_theirs, second_theirs, small,
    stage, xw, gw, sems, masks,
):
    fill_masks(masks)
    core = scalars[2]
    for part, tile, out in ((0, tok, xw), (2, cot, gw)):
        for n in range(2):
            rows = pl.ds(3 + 12 * n + 6 * core, 3)
            stage[:, 6 * n : 6 * n + 3, 0:16, :] = tile[:, rows, 32:48, :].astype(F32)
            stage[:, 6 * n : 6 * n + 6, 16:24, :] = h_lon[part : part + 2, 6 * n : 6 * n + 6].astype(F32)
        stage[:, 3:6, 0:16, :] = tile[:, pl.ds(6 + 6 * core, 3), 32:48, :].astype(F32)

        @pl.when(core == 0)
        def _():
            stage[:, 9:12, 0:16, :] = tile[:, 18:21, 32:48, :].astype(F32)

        @pl.when(core == 1)
        def _():
            stage[:, 9:12, 0:16, :] = h_lat[part : part + 2, :, 16:32, :].astype(F32)
            stage[:, 9:12, 16:24, :] = h_cor[part : part + 2].astype(F32)

        for n in range(2):
            out[n] = odd_window(stage, 6 * n, 10).astype(BF)
    stores = stores_of(xw, gw, x_out, g_out, sems)
    group_steps(
        scalars, (xw, gw), stores, masks, gain_ref, bias_ref, (mine, theirs), (sum_mine, sum_theirs), gb, dn
    )
    for t in range(4):
        for sums, payload in (sum_mine, (payload_mine, t)), (sum_theirs, ((first_theirs, second_theirs)[t // 2], t % 2)):
            ref, place = payload
            if t < 3:
                rows = sums[128 * t : 128 * t + 128, :].T
            else:
                rows = jnp.concatenate([sums[384:512, 128 * n : 128 * n + 128] for n in range(4)], 0)
            ref[512 * place : 512 * place + 512, :] = rows.astype(ref.dtype)
    pair = [jnp.sum(gb[8 * n : 8 * n + 8, :], axis=0, keepdims=True) for n in range(2)]
    small[...] = jnp.concatenate([s[:, 128 * n : 128 * n + 128] for s in pair for n in range(4)], 0)


def fill_masks(masks):
    key_row = lax.broadcasted_iota(jnp.int32, (SPAN, SPAN), 0) // 8 % 6
    query_row = lax.broadcasted_iota(jnp.int32, (SPAN, SPAN), 1) // 8 % 6
    masks[0] = jnp.zeros((SPAN, SPAN), F32)
    masks[1] = jnp.where((key_row >= 3) != (query_row >= 3), -1e30, 0.0)


def whole(shape):
    return pl.BlockSpec(shape, lambda i, scalars: (0,) * len(shape))


SUMS = [((512, D), F32), ((512, D), F32), ((16, D), F32)]


def kernel_call(kernel, steps, scalars, blocks, args, outs, scratch=(), waits=(), aliases=None, flops=5_000_000):
    many = isinstance(outs, list)
    out_list = outs if many else [outs]
    first = 1 + len(blocks) + len(args)

    def body(*refs):
        kernel(*refs[:first], *refs[first + len(waits) :])

    result = pl.pallas_call(
        body,
        grid_spec=pltpu.PrefetchScalarGridSpec(
            num_scalar_prefetch=1,
            grid=(steps,),
            in_specs=[spec for _, spec in blocks] + [INSIDE] * len(args) + [ANYWHERE] * len(waits),
            out_specs=[out[2] if len(out) > 2 else INSIDE for out in out_list],
            scratch_shapes=scratch,
        ),
        out_shape=[
            pltpu.HBM(*out[:2]) if len(out) > 2 else jax.ShapeDtypeStruct(*out) for out in out_list
        ],
        input_output_aliases=aliases or {},
        compiler_params=pltpu.CompilerParams(
            dimension_semantics=("arbitrary",), vmem_limit_bytes=VMEM_BYTES
        ),
        cost_estimate=pl.CostEstimate(flops=flops, bytes_accessed=1_000_000, transcendentals=0),
    )(
        scalars,
        *(pltpu.with_memory_space_constraint(array, pltpu.HBM) for array, _ in blocks),
        *args,
        *waits,
    )
    return result if many else result[0]


def group_call(kernel, scalars, arrays, args, sums, extra_out, rows, scratch, flops, waits=()):
    shape = (1, 2, SPAN, D)
    outs = [(shape, BF, whole(shape))] + [(shape, BF, ANYWHERE)] * 2 + SUMS + extra_out
    start = 1 + len(arrays) + len(args)
    aliases = {start + n: 3 + n for n in range(len(sums))}
    stage = [pltpu.VMEM(rows + (D,), F32)] + [pltpu.VMEM((2, SPAN, D), BF)] * 2 + [pltpu.SemaphoreType.DMA((2,))]
    blocks = [(a, ANYWHERE) for a in arrays]
    return kernel_call(kernel, 1, scalars, blocks, args + sums, outs, stage + scratch, waits, aliases, flops)


def halo_kernel(scalars, tok, cot, w_qkv, w_out, lat, lon, cor, weights, strips, w, sems):
    core = scalars[2]
    copies = [
        pltpu.make_async_copy(w_qkv, w, sems.at[0]),
        pltpu.make_async_copy(w_out, weights.at[384:512], sems.at[1]),
    ]
    for n, ref in enumerate((tok, cot)):
        for m, (source, at, rows) in enumerate(
            ((0, 0, 3), (3 + 6 * core, 3, 6), (15 + 6 * core, 9, 3), (18 + 3 * core, 12, 3))
        ):
            copies.append(
                pltpu.make_async_copy(
                    ref.at[:, pl.ds(source, rows), 0:16, :], strips.at[n, :, at : at + rows], sems.at[2 + 5 * n + m]
                )
            )
        columns = pl.ds(pl.multiple_of(16 * core, 16), 32)
        copies.append(
            pltpu.make_async_copy(
                ref.at[:, 0:3, columns, :], lat.at[2 * n : 2 * n + 2], sems.at[6 + 5 * n]
            )
        )
    for copy in copies:
        copy.start()
    copies[0].wait()
    for t in range(3):
        weights[128 * t : 128 * t + 128, :] = w[t].T
    for copy in copies[1:]:
        copy.wait()
    for n in range(2):
        strip = strips[n].astype(F32)[:, :, 0:8].astype(BF)
        cor[2 * n : 2 * n + 2] = strip[:, 0:3]
        lon[2 * n : 2 * n + 2] = strip[:, 3:15]


def moved_gradient(x, g, parts, gain):
    unit, inv_std = normalised(x.astype(F32))
    d_normed = parts[0].astype(F32) + parts[1].astype(F32)
    scaled = d_normed * gain
    mean = jnp.sum(scaled, axis=-1, keepdims=True) * (1.0 / D)
    along = jnp.sum(scaled * unit, axis=-1, keepdims=True) * (1.0 / D)
    return g.astype(F32) + inv_std * (scaled - mean - unit * along)


def norm_kernel(scalars, x0, g0, half0, x1, g1, half1, other0, other1, gain, out):
    for group, (x, g, half, other) in enumerate(((x0, g0, half0, other0), (x1, g1, half1, other1))):
        for n in range(2):
            parts = half[0, n], other[0, n]
            out[group, n] = moved_gradient(x[0, n], g[0, n], parts, gain[...]).astype(BF)


def last_norm_kernel(scalars, x2, g2, half2, x3, g3, half3, other2, other3, gain, out, lat, lon, cor):
    corner = scalars[2] == 1
    for n in range(2):
        row = moved_gradient(x2[0, n], g2[0, n], (half2[0, n], other2[0, n]), gain[...])
        column = moved_gradient(x3[0, n], g3[0, n], (half3[0, n], other3[0, n]), gain[...])
        out[0, n] = row.astype(BF)
        out[1, n] = column.astype(BF)
        if n == 1:
            row = jnp.where(corner, column, row)
            cor[...] = column[:96].reshape(2, 6, 8, D)[:, 3:6].reshape(48, D).astype(BF)
        edge = row.reshape(3, 6, 8, D)[:, 3:6].reshape(72, D)
        lat[n] = jnp.concatenate([edge, jnp.zeros((8, D), F32)], 0).astype(BF)
        lon[n] = column[:96].astype(BF)


def join_kernel(scalars, lat, lon, cor, out):
    out[0:80] = lat[0]
    out[80:160] = lat[1]
    out[160:256] = lon[0]
    out[256:352] = lon[1]
    out[352:400] = cor[...]


def pack_kernel(scalars, payload, first, second, small, small_theirs, out):
    share = out.shape[0]
    other = jnp.concatenate([first[...], second[...]], 0).astype(F32)
    rows = (payload[...] + other).reshape(share, 2048 // share, 128)
    small = small[...] + small_theirs[...]
    high = small.astype(BF).astype(F32)
    pair = jnp.concatenate([high[:, None], (small - high)[:, None], jnp.zeros((8, 6, 128), F32)], 1)
    ride = jnp.concatenate([pair, jnp.zeros((share - 8, 8, 128), F32)], 0)
    out[...] = jnp.concatenate([rows, ride], 1).astype(BF)


def sum_kernel(scalars, parts, out):
    out[...] = jnp.sum(parts[...].astype(F32), axis=0)


def spread_kernel(scalars, a, b, out):
    total = a[...] + b[...]
    rows = total.shape[0] - 8
    extra = total[rows : rows + 1] + total[rows + 1 : rows + 2]
    high = extra.astype(BF).astype(F32)
    total = jnp.concatenate([total[:rows], high, extra - high, jnp.zeros((6, 128), F32)], 0)
    out[...] = jnp.broadcast_to(total.astype(BF)[None], out.shape)


def small_kernel(scalars, parts, small):
    rows = parts.shape[1] - 8
    values = parts[0:8].astype(F32)
    small[...] = values[:, rows] + values[:, rows + 1]


def unpack_kernel(scalars, parts, gq, go):
    values = parts[...].astype(F32)
    rows = values.shape[1] - 8
    rows = values[:, :rows].reshape(2048, 128)
    for t in range(3):
        gq[t] = rows[512 * t : 512 * t + 512]
    for n in range(4):
        go[:, 128 * n : 128 * n + 128] = rows[1536 + 128 * n : 1664 + 128 * n]


def tile_kernel(scalars, a0, a1, b0, b1, ha, hb, out, windows, halos, stage):
    for n, (early, late, halo) in enumerate(((a0, a1, ha), (b0, b1, hb))):
        windows[n, 0:2] = early[...]
        windows[n, 2:4] = late[...]
        halos[n] = halo[...]
    core = scalars[2]

    def holder(j):
        return jnp.where(core == j % 2, 0, 1)

    for j in range(4):
        at = 80 * (j % 2)
        edge = halos[holder(j // 2), at : at + 80, :].astype(F32)[:72].reshape(3, 3, 8, D)
        column = 14 + 12 * j
        wide, narrow = (0, 8) if j < 3 else (4, 0)
        stage[:, 0:3, column + wide : column + wide + 8, :] = edge[0:2]
        stage[0, 0:3, column + narrow : column + narrow + 4, :] = edge[2, :, 0:4]
        stage[1, 0:3, column + narrow : column + narrow + 4, :] = edge[2, :, 4:8]
        rows = 6 if j < 3 else 3
        at = 160 + 96 * (j // 2)
        strip = halos[holder(j), at : at + 96, :].astype(F32).reshape(2, 6, 8, D)
        stage[:, 3 + 6 * j : 3 + 6 * j + rows, 6:14, :] = strip[:, :rows]
    stage[:, 0:3, 6:14, :] = halos[holder(3), 352:400, :].astype(F32).reshape(2, 3, 8, D)
    for group in range(4):
        for j in range(4):
            row, col = PLACE[group][j]
            rows = 6 if row < 3 else 3
            value = windows[holder(j), group, j // 2].astype(F32)
            full = value[:96].reshape(2, 6, 8, D)[:, :rows]
            rest = value[96:].reshape(6, 8, D)[:rows]
            column = 14 + 12 * col
            wide, narrow = (0, 8) if group < 3 else (4, 0)
            at = slice(3 + 6 * row, 3 + 6 * row + rows)
            stage[:, at, column + wide : column + wide + 8, :] = full
            stage[0, at, column + narrow : column + narrow + 4, :] = rest[:, 0:4]
            stage[1, at, column + narrow : column + narrow + 4, :] = rest[:, 4:8]
    out[...] = stage[:, :, 8:56, :].astype(BF)


def per_device(tokens, cotangent, norm_gain, norm_bias, w_qkv, w_out):
    core = lax.axis_index("tp") % 2
    edge = lax.axis_index("lat") == lax.axis_size("lat") - 1

    def scalars(first, second):
        masked = jnp.stack([edge & first, edge & second])
        return jnp.concatenate([jnp.where(masked, 1, 0), core.reshape(1)]).astype(jnp.int32)

    never = core < 0
    no_mask, row_mask, column_mask = scalars(never, never), scalars(core >= 0, core == 0), scalars(never, core == 1)

    def swap(block, bit):
        return move(block, ("tp",), lambda t: (t ^ bit,))

    both = (tokens, cotangent)
    h_lat, h_lon, h_cor, mine = kernel_call(
        halo_kernel,
        1,
        no_mask,
        [(a, ANYWHERE) for a in (tokens, cotangent, w_qkv.transpose(1, 0, 2), w_out)],
        [],
        [((4, 3, 32, D), BF), ((4, 12, 8, D), BF), ((4, 3, 8, D), BF), ((512, D), BF)],
        [
            pltpu.VMEM((2, 2, 15, 16, D), BF),
            pltpu.VMEM((3, D, 128), BF),
            pltpu.SemaphoreType.DMA((12,)),
        ],
    )
    theirs = swap(mine, 1)
    h_lat = move(h_lat, ("lat", "tp"), lambda a, t: (a - 1, t ^ 2))
    h_lon = move(h_lon, ("lon",), lambda a: (a - 1,))
    h_cor = move(h_cor, ("lat", "lon"), lambda a, b: (a - 1, b - 1))

    gain = norm_gain.reshape(1, D)
    params = [gain, norm_bias.reshape(1, D), mine, theirs]
    masks = [pltpu.VMEM((2, SPAN, SPAN), F32)]
    half0, x0, g0, *sums, tile_x, tile_g = group_call(
        inner_kernel(0),
        no_mask,
        both,
        params,
        [],
        [(t.shape, BF) for t in both],
        (2, 6, 48),
        [pltpu.SemaphoreType.DMA((2, 4))],
        FLOPS[0],
    )
    other0 = swap(half0, 2)
    tiles_in = [tile_x, tile_g]
    half1, x1, g1, *sums = group_call(
        inner_kernel(1), no_mask, [], tiles_in + params, sums, [], (2, 12, 48), [], FLOPS[1]
    )
    other1 = swap(half1, 2)
    half2, x2, g2, *sums = group_call(
        row_kernel, row_mask, [], tiles_in + [h_lat] + params, sums, [], (2, 12, 48), masks, FLOPS[2]
    )
    other2 = swap(half2, 2)
    half3, x3, g3, _, _, _, payload, *payload_theirs, small = group_call(
        column_kernel,
        column_mask,
        [],
        tiles_in + [h_lat, h_lon, h_cor] + params,
        sums,
        [((2048, 128), F32), ((1024, 128), BF), ((1024, 128), BF), ((8, 128), F32)],
        (2, 12, 24),
        masks,
        FLOPS[3],
        [other0],
    )
    other3 = swap(half3, 2)

    lats, lons = lax.axis_size("lat"), lax.axis_size("lon")
    tiles = lats // 2 * lons
    shares = ((tiles, 2048 // tiles + 8, 128), BF)
    groups = [[a * lons + b for a in range(half, lats, 2) for b in range(lons)] for half in range(2)]

    def exchange(block):
        return lax.all_to_all(block, ("lat", "lon"), 0, 0, axis_index_groups=groups, tiled=True)

    packed = kernel_call(
        pack_kernel, 1, no_mask, [], [payload, *(swap(p, 1) for p in payload_theirs), small, swap(small, 1)], shares, (), [other1, other2]
    )
    parts = exchange(packed)

    early = kernel_call(
        norm_kernel,
        1,
        no_mask,
        [(a, whole(a.shape)) for a in (x0, g0, half0, x1, g1, half1)],
        [other0, other1, gain],
        ((2, 2, SPAN, D), BF),
    )
    late, lat_edge, lon_edge, cor_edge = kernel_call(
        last_norm_kernel,
        1,
        no_mask,
        [(a, whole(a.shape)) for a in (x2, g2, half2, x3, g3, half3)],
        [other2, other3, gain],
        [((2, 2, SPAN, D), BF), ((2, 80, D), BF), ((2, 96, D), BF), ((48, D), BF)],
        flops=FLOPS[4],
    )
    lat_edge = move(lat_edge, ("lat", "tp"), lambda a, t: (a + 1, t ^ 2))
    lon_edge = move(lon_edge, ("lon",), lambda a: (a + 1,))
    cor_edge = move(cor_edge, ("lat", "lon"), lambda a, b: (a + 1, b + 1))
    edges = kernel_call(join_kernel, 1, no_mask, [], [lat_edge, lon_edge, cor_edge], ((400, D), BF))
    total = kernel_call(sum_kernel, 1, no_mask, [], [parts], (shares[0][1:], F32))
    other = move(total, ("lat",), lambda a: (a ^ 1,))
    spread = kernel_call(spread_kernel, 1, no_mask, [], [total, other], shares, (), [edges])
    gathered = exchange(spread)
    grad_tokens = kernel_call(
        tile_kernel,
        1,
        no_mask,
        [],
        [early, late, swap(early, 1), swap(late, 1), edges, swap(edges, 1)],
        (tokens.shape, BF, whole(tokens.shape)),
        [
            pltpu.VMEM((2, 4, 2, SPAN, D), BF),
            pltpu.VMEM((2, 400, D), BF),
            pltpu.VMEM((2, 24, 64, D), F32),
        ],
    )
    tokens_done = pltpu.with_memory_space_constraint(grad_tokens, pltpu.HBM)
    small = kernel_call(small_kernel, 1, no_mask, [], [gathered], ((8, 128), F32), (), [tokens_done])
    small_y = swap(small, 2)
    grad_qkv, grad_out = kernel_call(
        unpack_kernel,
        1,
        no_mask,
        [],
        [gathered],
        [((3, D, 128), F32, whole((3, D, 128))), ((128, D), F32, whole((128, D)))],
        (),
        [small],
    )
    small = small + small_y
    small = small.reshape(2, D)
    return (grad_tokens, small[0], small[1], grad_qkv.transpose(1, 0, 2), grad_out)


def solution(mesh):
    return jax.shard_map(
        per_device,
        mesh=mesh,
        in_specs=(
            P(None, "lat", "lon", None),
            P(None, "lat", "lon", None),
            P(),
            P(),
            P(None, None, "tp"),
            P("tp", None),
        ),
        out_specs=(P(None, "lat", "lon", None), P(), P(), P(None, None, "tp"), P("tp", None)),
        check_vma=False,
    )
```

```python
import jax
import jax.numpy as jnp
from jax import lax
from jax.experimental import pallas as pl
from jax.experimental.pallas import tpu as pltpu
from jax.sharding import PartitionSpec as P

HEAD = 64
SLAT = 3
SLON = 6
SPAN = 144
D = 512
BF = jnp.bfloat16
F32 = jnp.float32
NT = (((1,), (1,)), ((), ()))
NN = (((1,), (0,)), ((), ()))
TN = (((0,), (0,)), ((), ()))
FLOPS = 4_000_000_000, 50_000_000, 50_000_000, 50_000_000, 8_000_000_000
INSIDE = pl.BlockSpec(memory_space=pltpu.VMEM)
ANYWHERE = pl.BlockSpec(memory_space=pl.ANY)
VMEM_BYTES = 32 * 1024 * 1024

PLACE = (
    ((0, 0), (2, 0), (0, 1), (2, 1)),
    ((1, 0), (0, 2), (1, 1), (1, 2)),
    ((3, 0), (3, 2), (3, 1), (2, 2)),
    ((0, 3), (1, 3), (2, 3), (3, 3)),
)


def dot(a, b, form):
    return lax.dot_general(a, b, form, preferred_element_type=F32)


def move(block, axes, step):
    sizes = [lax.axis_size(axis) for axis in axes]
    total = 1
    for size in sizes:
        total *= size

    def index(coords):
        flat = 0
        for size, coord in zip(sizes, coords):
            flat = flat * size + coord % size
        return flat

    def coords(flat):
        out = []
        for size in reversed(sizes):
            out.append(flat % size)
            flat //= size
        return tuple(reversed(out))

    return lax.ppermute(block, axes, [(i, index(step(*coords(i)))) for i in range(total)])


def even_window(ref, row, column):
    rows = slice(row, row + 6)
    top = lax.broadcasted_iota(jnp.int32, (6, 8, D), 1) < 4
    full = ref[:, rows, column : column + 8, :].reshape(96, D)
    rest = jnp.where(
        top, ref[0, rows, column + 8 : column + 16, :], ref[1, rows, column + 4 : column + 12, :]
    )
    return jnp.concatenate([full, rest.reshape(48, D)], 0)


def odd_window(ref, row, column):
    rows = slice(row, row + 6)
    top = lax.broadcasted_iota(jnp.int32, (6, 8, D), 1) < 4
    full = ref[:, rows, column + 4 : column + 12, :].reshape(96, D)
    rest = jnp.where(
        top, ref[0, rows, column : column + 8, :], ref[1, rows, column - 4 : column + 4, :]
    )
    return jnp.concatenate([full, rest.reshape(48, D)], 0)


def normalised(x):
    mean = jnp.sum(x, axis=-1, keepdims=True) * (1.0 / D)
    centered = x - mean
    inv_std = lax.rsqrt(jnp.sum(centered * centered, axis=-1, keepdims=True) * (1.0 / D) + 1e-05)
    return centered * inv_std, inv_std


def window_steps(xs, gs, gain, bias, weights, masks, sums, gb_acc):
    left = lax.broadcasted_iota(jnp.int32, (SPAN, 128), 1) < HEAD
    zero = jnp.zeros((SPAN, 128), BF)

    def by_head(a):
        parts = [(jnp.where(left, half, zero), jnp.where(left, zero, half)) for half in (a[:, :128], a[:, 128:])]
        rows = [jnp.concatenate([part, zero], 1) for part in parts[0]]
        return jnp.concatenate(rows + [jnp.concatenate([zero, part], 1) for part in parts[1]], 0)

    count = range(len(xs))
    unit = [normalised(x.astype(F32))[0] for x in xs]
    normed = [(u * gain + bias).astype(BF) for u in unit]
    both = [(n, w) for n in count for w in range(2)]
    to_heads = jnp.concatenate([weights[w][0:384, :] for w in range(2)], 0)
    to_keys = jnp.concatenate([weights[w][r : r + 128, :] for r in (128, 256) for w in range(2)], 0)
    to_grads = jnp.concatenate([weights[w][384:512, :] for w in range(2)], 0)
    all_proj = [dot(to_heads, normed[n], NT).astype(BF) for n in count]
    all_kv = [dot(normed[n], to_keys, NT).astype(BF) for n in count]
    all_da = [dot(to_grads, gs[n], NT).astype(BF) for n in count]
    proj = {(n, w): all_proj[n][384 * w : 384 * w + 384] for n, w in both}
    da = {(n, w): all_da[n][128 * w : 128 * w + 128] for n, w in both}
    q = {i: p[0:128] * 0.125 for i, p in proj.items()}
    k = {i: p[128:256] for i, p in proj.items()}
    v = {i: p[256:384] for i, p in proj.items()}
    all_q = [jnp.concatenate([q[n, 0], q[n, 1]], 0) for n in count]
    scores = [dot(by_head(all_kv[n][:, :256]), all_q[n], NN) for n in count]
    d_probs = [dot(by_head(all_kv[n][:, 256:]), all_da[n], NN) for n in count]
    heads = [(i, head) for i in both for head in range(2)]
    probs, ds = {}, {}
    for i, head in heads:
        at = (2 * i[1] + head) * SPAN
        s = scores[i[0]][at : at + SPAN]
        if masks is not None:
            s = s + masks[i[0]]
        raised = jnp.exp(s - jnp.max(s, axis=0, keepdims=True))
        probs[i, head] = (raised * (1.0 / jnp.sum(raised, axis=0, keepdims=True))).astype(BF)
    for i, head in heads:
        pf = probs[i, head].astype(F32)
        at = (2 * i[1] + head) * SPAN
        dp = d_probs[i[0]][at : at + SPAN]
        ds[i, head] = (pf * (dp - jnp.sum(pf * dp, axis=0, keepdims=True))).astype(BF)
    cuts = [slice(0, HEAD), slice(HEAD, 2 * HEAD)]
    att = {(i, h): dot(v[i][cuts[h]], probs[i, h], NN).astype(BF) for i, h in heads}
    dv = {(i, h): dot(da[i][cuts[h]], probs[i, h], NT).astype(BF) for i, h in heads}
    dq = {(i, h): (dot(k[i][cuts[h]], ds[i, h], NN) * 0.125).astype(BF) for i, h in heads}
    dk = {(i, h): dot(q[i][cuts[h]], ds[i, h], NT).astype(BF) for i, h in heads}
    attended = {i: jnp.concatenate([att[i, 0], att[i, 1]], 0) for i in both}
    d_project = {
        i: jnp.concatenate([dq[i, 0], dq[i, 1], dk[i, 0], dk[i, 1], dv[i, 0], dv[i, 1]], 0) for i in both
    }
    d_heads = [jnp.concatenate([d_project[n, w] for w in range(2)], 0) for n in count]
    heads_out = [jnp.concatenate([attended[n, w] for w in range(2)], 0) for n in count]
    d_weights = sum(dot(d_heads[n], normed[n], NN) for n in count)
    d_out = sum(dot(heads_out[n], gs[n], NN) for n in count)
    for w in range(2):
        sums[w][0:384, :] += d_weights[384 * w : 384 * w + 384]
        sums[w][384:512, :] += d_out[128 * w : 128 * w + 128]
    dn = [dot(d_heads[n], to_heads, TN) for n in count]
    gb_acc[0:8, :] += sum(jnp.sum((dn[n] * unit[n]).reshape(SPAN // 8, 8, D), axis=0) for n in count)
    gb_acc[8:16, :] += sum(jnp.sum(dn[n].reshape(SPAN // 8, 8, D), axis=0) for n in count)
    return [d.astype(BF) for d in dn]


def group_steps(scalars, windows, masks, gain_ref, bias_ref, weights, sums, gb_acc, out):
    xs, gs = ([ref[n] for n in range(2)] for ref in windows)
    added = None if masks is None else [masks[scalars[n]] for n in range(2)]
    dn = window_steps(xs, gs, gain_ref[...], bias_ref[...], weights, added, sums, gb_acc)
    for n in range(2):
        out[0, n] = dn[n]


def inner_kernel(group):
    def kernel(scalars, *refs):
        core = scalars[2]
        if group == 0:
            hbm, refs = refs[:2], refs[2:]
            gain, bias, mine, theirs, dn, sum_mine, sum_theirs, gb, *tiles = refs[:10]
            stage, xw, gw, load_sems = refs[10:]
            pieces = ((3 + 12 * core, 6), (9, 6), (15 - 12 * core, 6), (21, 3))
            loads = [
                [
                    pltpu.make_async_copy(
                        hbm[n].at[:, pl.ds(start, rows)], tiles[n].at[:, pl.ds(start, rows)], load_sems.at[n, m]
                    )
                    for n in range(2)
                ]
                for m, (start, rows) in enumerate(pieces)
            ]
            for piece in loads:
                for load in piece:
                    load.start()
            sum_mine[...] = jnp.zeros_like(sum_mine)
            sum_theirs[...] = jnp.zeros_like(sum_theirs)
            gb[...] = jnp.zeros_like(gb)
            for load in loads[0]:
                load.wait()
            rows = [2 * core]
        else:
            tiles, refs = refs[:2], refs[2:]
            gain, bias, mine, theirs = refs[:4]
            dn, sum_mine, sum_theirs, gb, stage, xw, gw = refs[7:]
            loads = []
            rows = [1 - core, 1]
        for tile, out in zip(tiles, (xw, gw)):
            for n, row in enumerate(rows):
                stage[:, 6 * n : 6 * n + 6, :, :] = tile[:, pl.ds(3 + 6 * row, 6), :, :].astype(F32)
            for c in range(2):

                @pl.when(core == c)
                def _():
                    for n in range(2):
                        column = PLACE[group][2 * n + c][1]
                        out[n] = even_window(stage, 6 * n * group, SLON + 12 * column).astype(BF)

        group_steps(scalars, (xw, gw), None, gain, bias, (mine, theirs), (sum_mine, sum_theirs), gb, dn)
        for piece in loads[1:]:
            for load in piece:
                load.wait()

    return kernel


def row_kernel(
    scalars, tok, cot, h_lat, gain_ref, bias_ref, mine, theirs, in_mine, in_theirs, gb_in,
    dn, sum_mine, sum_theirs, gb, stage, xw, gw, masks,
):
    fill_masks(masks)
    core = scalars[2]
    for part, tile, out in ((0, tok, xw), (2, cot, gw)):
        stage[:, 0:9, :, :] = tile[:, 15:24, :, :].astype(F32)
        for c in range(2):

            @pl.when(core == c)
            def _():
                stage[:, 9:12, 16 * c : 16 * c + 32, :] = h_lat[part : part + 2].astype(F32)
                for n in range(2):
                    row, column = PLACE[2][2 * n + c]
                    out[n] = even_window(stage, 6 * (row - 2), SLON + 12 * column).astype(BF)

    group_steps(scalars, (xw, gw), masks, gain_ref, bias_ref, (mine, theirs), (sum_mine, sum_theirs), gb, dn)


def column_kernel(
    scalars, tok, cot, h_lat, h_lon, h_cor, gain_ref, bias_ref, mine, theirs, in_mine, in_theirs, gb_in,
    dn, sum_mine, sum_theirs, gb, payload_mine, first_theirs, second_theirs, small,
    stage, xw, gw, masks,
):
    fill_masks(masks)
    core = scalars[2]
    for part, tile, out in ((0, tok, xw), (2, cot, gw)):
        for n in range(2):
            rows = pl.ds(3 + 12 * n + 6 * core, 3)
            stage[:, 6 * n : 6 * n + 3, 0:16, :] = tile[:, rows, 32:48, :].astype(F32)
            stage[:, 6 * n : 6 * n + 6, 16:24, :] = h_lon[part : part + 2, 6 * n : 6 * n + 6].astype(F32)
        stage[:, 3:6, 0:16, :] = tile[:, pl.ds(6 + 6 * core, 3), 32:48, :].astype(F32)

        @pl.when(core == 0)
        def _():
            stage[:, 9:12, 0:16, :] = tile[:, 18:21, 32:48, :].astype(F32)

        @pl.when(core == 1)
        def _():
            stage[:, 9:12, 0:16, :] = h_lat[part : part + 2, :, 16:32, :].astype(F32)
            stage[:, 9:12, 16:24, :] = h_cor[part : part + 2].astype(F32)

        for n in range(2):
            out[n] = odd_window(stage, 6 * n, 10).astype(BF)
    group_steps(scalars, (xw, gw), masks, gain_ref, bias_ref, (mine, theirs), (sum_mine, sum_theirs), gb, dn)
    for t in range(4):
        for sums, payload in (sum_mine, (payload_mine, t)), (sum_theirs, ((first_theirs, second_theirs)[t // 2], t % 2)):
            ref, place = payload
            if t < 3:
                rows = sums[128 * t : 128 * t + 128, :].T
            else:
                rows = jnp.concatenate([sums[384:512, 128 * n : 128 * n + 128] for n in range(4)], 0)
            ref[512 * place : 512 * place + 512, :] = rows.astype(ref.dtype)
    pair = [jnp.sum(gb[8 * n : 8 * n + 8, :], axis=0, keepdims=True) for n in range(2)]
    small[...] = jnp.concatenate([s[:, 128 * n : 128 * n + 128] for s in pair for n in range(4)], 0)


def fill_masks(masks):
    key_row = lax.broadcasted_iota(jnp.int32, (SPAN, SPAN), 0) // 8 % 6
    query_row = lax.broadcasted_iota(jnp.int32, (SPAN, SPAN), 1) // 8 % 6
    masks[0] = jnp.zeros((SPAN, SPAN), F32)
    masks[1] = jnp.where((key_row >= 3) != (query_row >= 3), -1e30, 0.0)


def whole(shape):
    return pl.BlockSpec(shape, lambda i, scalars: (0,) * len(shape))


SUMS = [((512, D), F32), ((512, D), F32), ((16, D), F32)]


def kernel_call(kernel, steps, scalars, blocks, args, outs, scratch=(), waits=(), aliases=None, flops=5_000_000):
    many = isinstance(outs, list)
    out_list = outs if many else [outs]
    first = 1 + len(blocks) + len(args)

    def body(*refs):
        kernel(*refs[:first], *refs[first + len(waits) :])

    result = pl.pallas_call(
        body,
        grid_spec=pltpu.PrefetchScalarGridSpec(
            num_scalar_prefetch=1,
            grid=(steps,),
            in_specs=[spec for _, spec in blocks] + [INSIDE] * len(args) + [ANYWHERE] * len(waits),
            out_specs=[out[2] if len(out) > 2 else INSIDE for out in out_list],
            scratch_shapes=scratch,
        ),
        out_shape=[
            pltpu.HBM(*out[:2]) if len(out) > 2 else jax.ShapeDtypeStruct(*out) for out in out_list
        ],
        input_output_aliases=aliases or {},
        compiler_params=pltpu.CompilerParams(
            dimension_semantics=("arbitrary",), vmem_limit_bytes=VMEM_BYTES
        ),
        cost_estimate=pl.CostEstimate(flops=flops, bytes_accessed=1_000_000, transcendentals=0),
    )(
        scalars,
        *(pltpu.with_memory_space_constraint(array, pltpu.HBM) for array, _ in blocks),
        *args,
        *waits,
    )
    return result if many else result[0]


def group_call(kernel, scalars, arrays, args, sums, extra_out, rows, scratch, flops, waits=()):
    shape = (1, 2, SPAN, D)
    outs = [(shape, BF, whole(shape))] + SUMS + extra_out
    start = 1 + len(arrays) + len(args)
    aliases = {start + n: 1 + n for n in range(len(sums))}
    stage = [pltpu.VMEM(rows + (D,), F32)] + [pltpu.VMEM((2, SPAN, D), BF)] * 2
    blocks = [(a, ANYWHERE) for a in arrays]
    return kernel_call(kernel, 1, scalars, blocks, args + sums, outs, stage + scratch, waits, aliases, flops)


def halo_kernel(scalars, tok, cot, w_qkv, w_out, lat, lon, cor, weights, strips, w, sems):
    core = scalars[2]
    copies = [
        pltpu.make_async_copy(w_qkv, w, sems.at[0]),
        pltpu.make_async_copy(w_out, weights.at[384:512], sems.at[1]),
    ]
    for n, ref in enumerate((tok, cot)):
        for m, (source, at, rows) in enumerate(
            ((0, 0, 3), (3 + 6 * core, 3, 6), (15 + 6 * core, 9, 3), (18 + 3 * core, 12, 3))
        ):
            copies.append(
                pltpu.make_async_copy(
                    ref.at[:, pl.ds(source, rows), 0:16, :], strips.at[n, :, at : at + rows], sems.at[2 + 5 * n + m]
                )
            )
        columns = pl.ds(pl.multiple_of(16 * core, 16), 32)
        copies.append(
            pltpu.make_async_copy(
                ref.at[:, 0:3, columns, :], lat.at[2 * n : 2 * n + 2], sems.at[6 + 5 * n]
            )
        )
    for copy in copies:
        copy.start()
    copies[0].wait()
    for t in range(3):
        weights[128 * t : 128 * t + 128, :] = w[t].T
    for copy in copies[1:]:
        copy.wait()
    for n in range(2):
        strip = strips[n].astype(F32)[:, :, 0:8].astype(BF)
        cor[2 * n : 2 * n + 2] = strip[:, 0:3]
        lon[2 * n : 2 * n + 2] = strip[:, 3:15]


def early_kernel(scalars, half0, half1, other0, other1, out):
    for group, (half, other) in enumerate(((half0, other0), (half1, other1))):
        out[group] = (half[0].astype(F32) + other[0].astype(F32)).astype(BF)


def late_kernel(scalars, half2, half3, other2, other3, out, lat, lon, cor):
    corner = scalars[2] == 1
    for n in range(2):
        row = half2[0, n].astype(F32) + other2[0, n].astype(F32)
        column = half3[0, n].astype(F32) + other3[0, n].astype(F32)
        out[0, n] = row.astype(BF)
        out[1, n] = column.astype(BF)
        if n == 1:
            row = jnp.where(corner, column, row)
            cor[...] = column[:96].reshape(2, 6, 8, D)[:, 3:6].reshape(48, D).astype(BF)
        edge = row.reshape(3, 6, 8, D)[:, 3:6].reshape(72, D)
        lat[n] = jnp.concatenate([edge, jnp.zeros((8, D), F32)], 0).astype(BF)
        lon[n] = column[:96].astype(BF)


def join_kernel(scalars, lat, lon, cor, out):
    out[0:80] = lat[0]
    out[80:160] = lat[1]
    out[160:256] = lon[0]
    out[256:352] = lon[1]
    out[352:400] = cor[...]


def pack_kernel(scalars, payload, first, second, small, small_theirs, out):
    share = out.shape[0]
    other = jnp.concatenate([first[...], second[...]], 0).astype(F32)
    rows = (payload[...] + other).reshape(share, 2048 // share, 128)
    small = small[...] + small_theirs[...]
    high = small.astype(BF).astype(F32)
    pair = jnp.concatenate([high[:, None], (small - high)[:, None], jnp.zeros((8, 6, 128), F32)], 1)
    ride = jnp.concatenate([pair, jnp.zeros((share - 8, 8, 128), F32)], 0)
    out[...] = jnp.concatenate([rows, ride], 1).astype(BF)


def copy_kernel(scalars, a, out):
    out[...] = a[...]


def sum_kernel(scalars, parts, out):
    out[...] = jnp.sum(parts[...].astype(F32), axis=0)


def spread_kernel(scalars, a, b, out):
    total = a[...] + b[...]
    rows = total.shape[0] - 8
    extra = total[rows : rows + 1] + total[rows + 1 : rows + 2]
    high = extra.astype(BF).astype(F32)
    total = jnp.concatenate([total[:rows], high, extra - high, jnp.zeros((6, 128), F32)], 0)
    out[...] = jnp.broadcast_to(total.astype(BF)[None], out.shape)


def small_kernel(scalars, parts, small):
    rows = parts.shape[1] - 8
    values = parts[0:8].astype(F32)
    small[...] = values[:, rows] + values[:, rows + 1]


def unpack_kernel(scalars, parts, gq, go):
    values = parts[...].astype(F32)
    rows = values.shape[1] - 8
    rows = values[:, :rows].reshape(2048, 128)
    for t in range(3):
        gq[t] = rows[512 * t : 512 * t + 512]
    for n in range(4):
        go[:, 128 * n : 128 * n + 128] = rows[1536 + 128 * n : 1664 + 128 * n]


def tile_kernel(scalars, tok, cot, a0, a1, b0, b1, ha, hb, gain, out, windows, halos, stage):
    step = pl.program_id(0)

    @pl.when(step == 0)
    def _():
        place_windows(scalars, a0, a1, b0, b1, ha, hb, windows, halos, stage)

    x, g = tok[...].astype(F32), cot[...].astype(F32)
    unit, inv_std = normalised(x)
    scaled = stage[:, pl.ds(3 * step, 3), 8:56, :] * gain[...].reshape(1, 1, 1, D)
    mean = jnp.sum(scaled, axis=-1, keepdims=True) * (1.0 / D)
    along = jnp.sum(scaled * unit, axis=-1, keepdims=True) * (1.0 / D)
    out[...] = (g + inv_std * (scaled - mean - unit * along)).astype(BF)


def place_windows(scalars, a0, a1, b0, b1, ha, hb, windows, halos, stage):
    for n, (early, late, halo) in enumerate(((a0, a1, ha), (b0, b1, hb))):
        windows[n, 0:2] = early[...]
        windows[n, 2:4] = late[...]
        halos[n] = halo[...]
    core = scalars[2]

    def holder(j):
        return jnp.where(core == j % 2, 0, 1)

    for j in range(4):
        at = 80 * (j % 2)
        edge = halos[holder(j // 2), at : at + 80, :].astype(F32)[:72].reshape(3, 3, 8, D)
        column = 14 + 12 * j
        wide, narrow = (0, 8) if j < 3 else (4, 0)
        stage[:, 0:3, column + wide : column + wide + 8, :] = edge[0:2]
        stage[0, 0:3, column + narrow : column + narrow + 4, :] = edge[2, :, 0:4]
        stage[1, 0:3, column + narrow : column + narrow + 4, :] = edge[2, :, 4:8]
        rows = 6 if j < 3 else 3
        at = 160 + 96 * (j // 2)
        strip = halos[holder(j), at : at + 96, :].astype(F32).reshape(2, 6, 8, D)
        stage[:, 3 + 6 * j : 3 + 6 * j + rows, 6:14, :] = strip[:, :rows]
    stage[:, 0:3, 6:14, :] = halos[holder(3), 352:400, :].astype(F32).reshape(2, 3, 8, D)
    for group in range(4):
        for j in range(4):
            row, col = PLACE[group][j]
            rows = 6 if row < 3 else 3
            value = windows[holder(j), group, j // 2].astype(F32)
            full = value[:96].reshape(2, 6, 8, D)[:, :rows]
            rest = value[96:].reshape(6, 8, D)[:rows]
            column = 14 + 12 * col
            wide, narrow = (0, 8) if group < 3 else (4, 0)
            at = slice(3 + 6 * row, 3 + 6 * row + rows)
            stage[:, at, column + wide : column + wide + 8, :] = full
            stage[0, at, column + narrow : column + narrow + 4, :] = rest[:, 0:4]
            stage[1, at, column + narrow : column + narrow + 4, :] = rest[:, 4:8]


def per_device(tokens, cotangent, norm_gain, norm_bias, w_qkv, w_out):
    core = lax.axis_index("tp") % 2
    edge = lax.axis_index("lat") == lax.axis_size("lat") - 1

    def scalars(first, second):
        masked = jnp.stack([edge & first, edge & second])
        return jnp.concatenate([jnp.where(masked, 1, 0), core.reshape(1)]).astype(jnp.int32)

    never = core < 0
    no_mask, row_mask, column_mask = scalars(never, never), scalars(core >= 0, core == 0), scalars(never, core == 1)

    def swap(block, bit):
        return move(block, ("tp",), lambda t: (t ^ bit,))

    both = (tokens, cotangent)
    h_lat, h_lon, h_cor, mine = kernel_call(
        halo_kernel,
        1,
        no_mask,
        [(a, ANYWHERE) for a in (tokens, cotangent, w_qkv.transpose(1, 0, 2), w_out)],
        [],
        [((4, 3, 32, D), BF), ((4, 12, 8, D), BF), ((4, 3, 8, D), BF), ((512, D), BF)],
        [
            pltpu.VMEM((2, 2, 15, 16, D), BF),
            pltpu.VMEM((3, D, 128), BF),
            pltpu.SemaphoreType.DMA((12,)),
        ],
    )
    theirs = swap(mine, 1)
    h_lat = move(h_lat, ("lat", "tp"), lambda a, t: (a - 1, t ^ 2))
    h_lon = move(h_lon, ("lon",), lambda a: (a - 1,))
    h_cor = move(h_cor, ("lat", "lon"), lambda a, b: (a - 1, b - 1))

    gain = norm_gain.reshape(1, D)
    params = [gain, norm_bias.reshape(1, D), mine, theirs]
    masks = [pltpu.VMEM((2, SPAN, SPAN), F32)]
    half0, *sums, tile_x, tile_g = group_call(
        inner_kernel(0),
        no_mask,
        both,
        params,
        [],
        [(t.shape, BF) for t in both],
        (2, 6, 48),
        [pltpu.SemaphoreType.DMA((2, 4))],
        FLOPS[0],
    )
    other0 = swap(half0, 2)
    tiles_in = [tile_x, tile_g]
    half1, *sums = group_call(
        inner_kernel(1), no_mask, [], tiles_in + params, sums, [], (2, 12, 48), [], FLOPS[1]
    )
    other1 = swap(half1, 2)
    half2, *sums = group_call(
        row_kernel, row_mask, [], tiles_in + [h_lat] + params, sums, [], (2, 12, 48), masks, FLOPS[2]
    )
    other2 = swap(half2, 2)
    half3, _, _, _, payload, *payload_theirs, small = group_call(
        column_kernel,
        column_mask,
        [],
        tiles_in + [h_lat, h_lon, h_cor] + params,
        sums,
        [((2048, 128), F32), ((1024, 128), BF), ((1024, 128), BF), ((8, 128), F32)],
        (2, 12, 24),
        masks,
        FLOPS[3],
        [other0],
    )
    other3 = swap(half3, 2)

    lats, lons = lax.axis_size("lat"), lax.axis_size("lon")
    tiles = lats // 2 * lons
    shares = ((tiles, 2048 // tiles + 8, 128), BF)
    groups = [[a * lons + b for a in range(half, lats, 2) for b in range(lons)] for half in range(2)]

    def exchange(block):
        return lax.all_to_all(block, ("lat", "lon"), 0, 0, axis_index_groups=groups, tiled=True)

    small = kernel_call(copy_kernel, 1, no_mask, [], [small], ((8, 128), F32), (), [other1])
    packed = kernel_call(
        pack_kernel, 1, no_mask, [], [payload, *(swap(p, 1) for p in payload_theirs), small, swap(small, 1)], shares, (), [other2]
    )
    parts = exchange(packed)

    early = kernel_call(
        early_kernel,
        1,
        no_mask,
        [(a, whole(a.shape)) for a in (half0, half1)],
        [other0, other1],
        ((2, 2, SPAN, D), BF),
    )
    late, lat_edge, lon_edge, cor_edge = kernel_call(
        late_kernel,
        1,
        no_mask,
        [(a, whole(a.shape)) for a in (half2, half3)],
        [other2, other3],
        [((2, 2, SPAN, D), BF), ((2, 80, D), BF), ((2, 96, D), BF), ((48, D), BF)],
        flops=FLOPS[4],
    )
    lat_edge = move(lat_edge, ("lat", "tp"), lambda a, t: (a + 1, t ^ 2))
    lon_edge = move(lon_edge, ("lon",), lambda a: (a + 1,))
    cor_edge = move(cor_edge, ("lat", "lon"), lambda a, b: (a + 1, b + 1))
    edges = kernel_call(join_kernel, 1, no_mask, [], [lat_edge, lon_edge, cor_edge], ((400, D), BF))
    total = kernel_call(sum_kernel, 1, no_mask, [], [parts], (shares[0][1:], F32))
    other = move(total, ("lat",), lambda a: (a ^ 1,))
    spread = kernel_call(spread_kernel, 1, no_mask, [], [total, other], shares, (), [edges])
    gathered = exchange(spread)
    rows = pl.BlockSpec((2, 3, 48, D), lambda i, scalars: (0, i, 0, 0))
    grad_tokens = kernel_call(
        tile_kernel,
        8,
        no_mask,
        [(tokens, rows), (cotangent, rows)],
        [early, late, swap(early, 1), swap(late, 1), edges, swap(edges, 1), gain],
        (tokens.shape, BF, rows),
        [
            pltpu.VMEM((2, 4, 2, SPAN, D), BF),
            pltpu.VMEM((2, 400, D), BF),
            pltpu.VMEM((2, 24, 64, D), F32),
        ],
    )
    tokens_done = pltpu.with_memory_space_constraint(grad_tokens, pltpu.HBM)
    small = kernel_call(small_kernel, 1, no_mask, [], [gathered], ((8, 128), F32), (), [tokens_done])
    small_y = swap(small, 2)
    grad_qkv, grad_out = kernel_call(
        unpack_kernel,
        1,
        no_mask,
        [],
        [gathered],
        [((3, D, 128), F32, whole((3, D, 128))), ((128, D), F32, whole((128, D)))],
        (),
        [small],
    )
    small = small + small_y
    small = small.reshape(2, D)
    return (grad_tokens, small[0], small[1], grad_qkv.transpose(1, 0, 2), grad_out)


def solution(mesh):
    return jax.shard_map(
        per_device,
        mesh=mesh,
        in_specs=(
            P(None, "lat", "lon", None),
            P(None, "lat", "lon", None),
            P(),
            P(),
            P(None, None, "tp"),
            P("tp", None),
        ),
        out_specs=(P(None, "lat", "lon", None), P(), P(), P(None, None, "tp"), P("tp", None)),
        check_vma=False,
    )
```

```python
import jax
import jax.numpy as jnp
from jax import lax
from jax.experimental import pallas as pl
from jax.experimental.pallas import tpu as pltpu
from jax.sharding import PartitionSpec as P

HEAD = 64
SLAT = 3
SLON = 6
SPAN = 144
D = 512
BF = jnp.bfloat16
F32 = jnp.float32
NT = (((1,), (1,)), ((), ()))
NN = (((1,), (0,)), ((), ()))
TN = (((0,), (0,)), ((), ()))
FLOPS = 4_000_000_000, 50_000_000, 50_000_000, 50_000_000, 8_000_000_000
INSIDE = pl.BlockSpec(memory_space=pltpu.VMEM)
ANYWHERE = pl.BlockSpec(memory_space=pl.ANY)
VMEM_BYTES = 32 * 1024 * 1024

PLACE = (
    ((0, 0), (2, 0), (0, 1), (2, 1)),
    ((1, 0), (0, 2), (1, 1), (1, 2)),
    ((3, 0), (3, 2), (3, 1), (2, 2)),
    ((0, 3), (1, 3), (2, 3), (3, 3)),
)


def dot(a, b, form):
    return lax.dot_general(a, b, form, preferred_element_type=F32)


def move(block, axes, step):
    sizes = [lax.axis_size(axis) for axis in axes]
    total = 1
    for size in sizes:
        total *= size

    def index(coords):
        flat = 0
        for size, coord in zip(sizes, coords):
            flat = flat * size + coord % size
        return flat

    def coords(flat):
        out = []
        for size in reversed(sizes):
            out.append(flat % size)
            flat //= size
        return tuple(reversed(out))

    return lax.ppermute(block, axes, [(i, index(step(*coords(i)))) for i in range(total)])


def even_window(ref, row, column):
    rows = slice(row, row + 6)
    top = lax.broadcasted_iota(jnp.int32, (6, 8, D), 1) < 4
    full = ref[:, rows, column : column + 8, :].reshape(96, D)
    rest = jnp.where(
        top, ref[0, rows, column + 8 : column + 16, :], ref[1, rows, column + 4 : column + 12, :]
    )
    return jnp.concatenate([full, rest.reshape(48, D)], 0)


def odd_window(ref, row, column):
    rows = slice(row, row + 6)
    top = lax.broadcasted_iota(jnp.int32, (6, 8, D), 1) < 4
    full = ref[:, rows, column + 4 : column + 12, :].reshape(96, D)
    rest = jnp.where(
        top, ref[0, rows, column : column + 8, :], ref[1, rows, column - 4 : column + 4, :]
    )
    return jnp.concatenate([full, rest.reshape(48, D)], 0)


def normalised(x):
    mean = jnp.sum(x, axis=-1, keepdims=True) * (1.0 / D)
    centered = x - mean
    inv_std = lax.rsqrt(jnp.sum(centered * centered, axis=-1, keepdims=True) * (1.0 / D) + 1e-05)
    return centered * inv_std, inv_std


def window_steps(xs, gs, gain, bias, weights, masks, sums, gb_acc):
    left = lax.broadcasted_iota(jnp.int32, (SPAN, 128), 1) < HEAD
    zero = jnp.zeros((SPAN, 128), BF)

    def by_head(a):
        parts = [(jnp.where(left, half, zero), jnp.where(left, zero, half)) for half in (a[:, :128], a[:, 128:])]
        rows = [jnp.concatenate([part, zero], 1) for part in parts[0]]
        return jnp.concatenate(rows + [jnp.concatenate([zero, part], 1) for part in parts[1]], 0)

    count = range(len(xs))
    unit = [normalised(x.astype(F32))[0] for x in xs]
    normed = [(u * gain + bias).astype(BF) for u in unit]
    both = [(n, w) for n in count for w in range(2)]
    to_heads = jnp.concatenate([weights[w][0:384, :] for w in range(2)], 0)
    to_keys = jnp.concatenate([weights[w][r : r + 128, :] for r in (128, 256) for w in range(2)], 0)
    to_grads = jnp.concatenate([weights[w][384:512, :] for w in range(2)], 0)
    all_proj = [dot(to_heads, normed[n], NT).astype(BF) for n in count]
    all_kv = [dot(normed[n], to_keys, NT).astype(BF) for n in count]
    all_da = [dot(to_grads, gs[n], NT).astype(BF) for n in count]
    proj = {(n, w): all_proj[n][384 * w : 384 * w + 384] for n, w in both}
    da = {(n, w): all_da[n][128 * w : 128 * w + 128] for n, w in both}
    q = {i: p[0:128] * 0.125 for i, p in proj.items()}
    k = {i: p[128:256] for i, p in proj.items()}
    v = {i: p[256:384] for i, p in proj.items()}
    all_q = [jnp.concatenate([q[n, 0], q[n, 1]], 0) for n in count]
    scores = [dot(by_head(all_kv[n][:, :256]), all_q[n], NN) for n in count]
    d_probs = [dot(by_head(all_kv[n][:, 256:]), all_da[n], NN) for n in count]
    heads = [(i, head) for i in both for head in range(2)]
    probs, ds = {}, {}
    for i, head in heads:
        at = (2 * i[1] + head) * SPAN
        s = scores[i[0]][at : at + SPAN]
        if masks is not None:
            s = s + masks[i[0]]
        raised = jnp.exp(s - jnp.max(s, axis=0, keepdims=True))
        probs[i, head] = (raised * (1.0 / jnp.sum(raised, axis=0, keepdims=True))).astype(BF)
    for i, head in heads:
        pf = probs[i, head].astype(F32)
        at = (2 * i[1] + head) * SPAN
        dp = d_probs[i[0]][at : at + SPAN]
        ds[i, head] = (pf * (dp - jnp.sum(pf * dp, axis=0, keepdims=True))).astype(BF)
    cuts = [slice(0, HEAD), slice(HEAD, 2 * HEAD)]
    att = {(i, h): dot(v[i][cuts[h]], probs[i, h], NN).astype(BF) for i, h in heads}
    dv = {(i, h): dot(da[i][cuts[h]], probs[i, h], NT).astype(BF) for i, h in heads}
    dq = {(i, h): (dot(k[i][cuts[h]], ds[i, h], NN) * 0.125).astype(BF) for i, h in heads}
    dk = {(i, h): dot(q[i][cuts[h]], ds[i, h], NT).astype(BF) for i, h in heads}
    attended = {i: jnp.concatenate([att[i, 0], att[i, 1]], 0) for i in both}
    d_project = {
        i: jnp.concatenate([dq[i, 0], dq[i, 1], dk[i, 0], dk[i, 1], dv[i, 0], dv[i, 1]], 0) for i in both
    }
    d_heads = [jnp.concatenate([d_project[n, w] for w in range(2)], 0) for n in count]
    heads_out = [jnp.concatenate([attended[n, w] for w in range(2)], 0) for n in count]
    d_weights = sum(dot(d_heads[n], normed[n], NN) for n in count)
    d_out = sum(dot(heads_out[n], gs[n], NN) for n in count)
    for w in range(2):
        sums[w][0:384, :] += d_weights[384 * w : 384 * w + 384]
        sums[w][384:512, :] += d_out[128 * w : 128 * w + 128]
    dn = [dot(d_heads[n], to_heads, TN) for n in count]
    gb_acc[0:8, :] += sum(jnp.sum((dn[n] * unit[n]).reshape(SPAN // 8, 8, D), axis=0) for n in count)
    gb_acc[8:16, :] += sum(jnp.sum(dn[n].reshape(SPAN // 8, 8, D), axis=0) for n in count)
    return [d.astype(BF) for d in dn]


def group_steps(scalars, windows, masks, gain_ref, bias_ref, weights, sums, gb_acc, out):
    xs, gs = ([ref[n] for n in range(2)] for ref in windows)
    added = None if masks is None else [masks[scalars[n]] for n in range(2)]
    dn = window_steps(xs, gs, gain_ref[...], bias_ref[...], weights, added, sums, gb_acc)
    for n in range(2):
        out[0, n] = dn[n]


def inner_kernel(group):
    def kernel(scalars, *refs):
        core = scalars[2]
        if group == 0:
            hbm, rows_in, refs = refs[:2], refs[2:4], refs[4:]
            gain, bias, mine, theirs, dn, sum_mine, sum_theirs, gb, *tiles = refs[:10]
            stage, xw, gw, load_sems = refs[10:]
            pieces = ((3 + 12 * core, 6), (9, 6), (15 - 12 * core, 6), (21, 3))
            loads = [
                [
                    pltpu.make_async_copy(
                        hbm[n].at[:, pl.ds(start, rows)], tiles[n].at[:, pl.ds(start, rows)], load_sems.at[n, m]
                    )
                    for n in range(2)
                ]
                for m, (start, rows) in enumerate(pieces)
            ]
            for piece in loads:
                for load in piece:
                    load.start()
            sum_mine[...] = jnp.zeros_like(sum_mine)
            sum_theirs[...] = jnp.zeros_like(sum_theirs)
            gb[...] = jnp.zeros_like(gb)
            rows = []
        else:
            tiles, refs = refs[:2], refs[2:]
            gain, bias, mine, theirs = refs[:4]
            dn, sum_mine, sum_theirs, gb, stage, xw, gw = refs[7:]
            loads = []
            rows = [1 - core, 1]
        for tile, out in zip(rows_in if group == 0 else tiles, (xw, gw)):
            if group == 0:
                stage[...] = tile[...].astype(F32)
            for n, row in enumerate(rows):
                stage[:, 6 * n : 6 * n + 6, :, :] = tile[:, pl.ds(3 + 6 * row, 6), :, :].astype(F32)
            for c in range(2):

                @pl.when(core == c)
                def _():
                    for n in range(2):
                        column = PLACE[group][2 * n + c][1]
                        out[n] = even_window(stage, 6 * n * group, SLON + 12 * column).astype(BF)

        group_steps(scalars, (xw, gw), None, gain, bias, (mine, theirs), (sum_mine, sum_theirs), gb, dn)
        for piece in loads:
            for load in piece:
                load.wait()

    return kernel


def row_kernel(
    scalars, tok, cot, h_lat, gain_ref, bias_ref, mine, theirs, in_mine, in_theirs, gb_in,
    dn, sum_mine, sum_theirs, gb, stage, xw, gw, masks,
):
    fill_masks(masks)
    core = scalars[2]
    for part, tile, out in ((0, tok, xw), (2, cot, gw)):
        stage[:, 0:9, :, :] = tile[:, 15:24, :, :].astype(F32)
        for c in range(2):

            @pl.when(core == c)
            def _():
                stage[:, 9:12, 16 * c : 16 * c + 32, :] = h_lat[part : part + 2].astype(F32)
                for n in range(2):
                    row, column = PLACE[2][2 * n + c]
                    out[n] = even_window(stage, 6 * (row - 2), SLON + 12 * column).astype(BF)

    group_steps(scalars, (xw, gw), masks, gain_ref, bias_ref, (mine, theirs), (sum_mine, sum_theirs), gb, dn)


def column_kernel(
    scalars, tok, cot, h_lat, h_lon, h_cor, gain_ref, bias_ref, mine, theirs, in_mine, in_theirs, gb_in,
    dn, sum_mine, sum_theirs, gb, payload_mine, first_theirs, second_theirs, small,
    stage, xw, gw, masks,
):
    fill_masks(masks)
    core = scalars[2]
    for part, tile, out in ((0, tok, xw), (2, cot, gw)):
        for n in range(2):
            rows = pl.ds(3 + 12 * n + 6 * core, 3)
            stage[:, 6 * n : 6 * n + 3, 0:16, :] = tile[:, rows, 32:48, :].astype(F32)
            stage[:, 6 * n : 6 * n + 6, 16:24, :] = h_lon[part : part + 2, 6 * n : 6 * n + 6].astype(F32)
        stage[:, 3:6, 0:16, :] = tile[:, pl.ds(6 + 6 * core, 3), 32:48, :].astype(F32)

        @pl.when(core == 0)
        def _():
            stage[:, 9:12, 0:16, :] = tile[:, 18:21, 32:48, :].astype(F32)

        @pl.when(core == 1)
        def _():
            stage[:, 9:12, 0:16, :] = h_lat[part : part + 2, :, 16:32, :].astype(F32)
            stage[:, 9:12, 16:24, :] = h_cor[part : part + 2].astype(F32)

        for n in range(2):
            out[n] = odd_window(stage, 6 * n, 10).astype(BF)
    group_steps(scalars, (xw, gw), masks, gain_ref, bias_ref, (mine, theirs), (sum_mine, sum_theirs), gb, dn)
    for t in range(4):
        for sums, payload in (sum_mine, (payload_mine, t)), (sum_theirs, ((first_theirs, second_theirs)[t // 2], t % 2)):
            ref, place = payload
            if t < 3:
                rows = sums[128 * t : 128 * t + 128, :].T
            else:
                rows = jnp.concatenate([sums[384:512, 128 * n : 128 * n + 128] for n in range(4)], 0)
            ref[512 * place : 512 * place + 512, :] = rows.astype(ref.dtype)
    pair = [jnp.sum(gb[8 * n : 8 * n + 8, :], axis=0, keepdims=True) for n in range(2)]
    small[...] = jnp.concatenate([s[:, 128 * n : 128 * n + 128] for s in pair for n in range(4)], 0)


def fill_masks(masks):
    key_row = lax.broadcasted_iota(jnp.int32, (SPAN, SPAN), 0) // 8 % 6
    query_row = lax.broadcasted_iota(jnp.int32, (SPAN, SPAN), 1) // 8 % 6
    masks[0] = jnp.zeros((SPAN, SPAN), F32)
    masks[1] = jnp.where((key_row >= 3) != (query_row >= 3), -1e30, 0.0)


def whole(shape):
    return pl.BlockSpec(shape, lambda i, scalars: (0,) * len(shape))


SUMS = [((512, D), F32), ((512, D), F32), ((16, D), F32)]


def kernel_call(kernel, steps, scalars, blocks, args, outs, scratch=(), waits=(), aliases=None, flops=5_000_000):
    many = isinstance(outs, list)
    out_list = outs if many else [outs]
    first = 1 + len(blocks) + len(args)

    def body(*refs):
        kernel(*refs[:first], *refs[first + len(waits) :])

    result = pl.pallas_call(
        body,
        grid_spec=pltpu.PrefetchScalarGridSpec(
            num_scalar_prefetch=1,
            grid=(steps,),
            in_specs=[spec for _, spec in blocks] + [INSIDE] * len(args) + [ANYWHERE] * len(waits),
            out_specs=[out[2] if len(out) > 2 else INSIDE for out in out_list],
            scratch_shapes=scratch,
        ),
        out_shape=[
            pltpu.HBM(*out[:2]) if len(out) > 2 else jax.ShapeDtypeStruct(*out) for out in out_list
        ],
        input_output_aliases=aliases or {},
        compiler_params=pltpu.CompilerParams(
            dimension_semantics=("arbitrary",), vmem_limit_bytes=VMEM_BYTES
        ),
        cost_estimate=pl.CostEstimate(flops=flops, bytes_accessed=1_000_000, transcendentals=0),
    )(
        scalars,
        *(pltpu.with_memory_space_constraint(array, pltpu.HBM) for array, _ in blocks),
        *args,
        *waits,
    )
    return result if many else result[0]


def group_call(kernel, scalars, arrays, args, sums, extra_out, rows, scratch, flops, waits=()):
    shape = (1, 2, SPAN, D)
    outs = [(shape, BF, whole(shape))] + SUMS + extra_out
    start = 1 + len(arrays) + len(args)
    aliases = {start + n: 1 + n for n in range(len(sums))}
    stage = [pltpu.VMEM(rows + (D,), F32)] + [pltpu.VMEM((2, SPAN, D), BF)] * 2
    blocks = [(a, ANYWHERE) for a in arrays]
    return kernel_call(kernel, 1, scalars, blocks, args + sums, outs, stage + scratch, waits, aliases, flops)


def halo_kernel(scalars, tok, cot, w_qkv, w_out, lat, lon, cor, weights, first_x, first_g, strips, w, sems):
    core = scalars[2]
    copies = [
        pltpu.make_async_copy(w_qkv, w, sems.at[0]),
        pltpu.make_async_copy(w_out, weights.at[384:512], sems.at[1]),
    ]
    for n, ref in enumerate((tok, cot)):
        for m, (source, at, rows) in enumerate(
            ((0, 0, 3), (3 + 6 * core, 3, 6), (15 + 6 * core, 9, 3), (18 + 3 * core, 12, 3))
        ):
            copies.append(
                pltpu.make_async_copy(
                    ref.at[:, pl.ds(source, rows), 0:16, :], strips.at[n, :, at : at + rows], sems.at[2 + 5 * n + m]
                )
            )
        columns = pl.ds(pl.multiple_of(16 * core, 16), 32)
        copies.append(
            pltpu.make_async_copy(
                ref.at[:, 0:3, columns, :], lat.at[2 * n : 2 * n + 2], sems.at[6 + 5 * n]
            )
        )
    for n, (ref, first) in enumerate(((tok, first_x), (cot, first_g))):
        copies.append(pltpu.make_async_copy(ref.at[:, pl.ds(3 + 12 * core, 6)], first, sems.at[12 + n]))
    for copy in copies:
        copy.start()
    copies[0].wait()
    for t in range(3):
        weights[128 * t : 128 * t + 128, :] = w[t].T
    for copy in copies[1:]:
        copy.wait()
    for n in range(2):
        strip = strips[n].astype(F32)[:, :, 0:8].astype(BF)
        cor[2 * n : 2 * n + 2] = strip[:, 0:3]
        lon[2 * n : 2 * n + 2] = strip[:, 3:15]


def early_kernel(scalars, half0, half1, other0, other1, out):
    for group, (half, other) in enumerate(((half0, other0), (half1, other1))):
        out[group] = (half[0].astype(F32) + other[0].astype(F32)).astype(BF)


def late_kernel(scalars, half2, half3, other2, other3, out, lat, lon, cor):
    corner = scalars[2] == 1
    for n in range(2):
        row = half2[0, n].astype(F32) + other2[0, n].astype(F32)
        column = half3[0, n].astype(F32) + other3[0, n].astype(F32)
        out[0, n] = row.astype(BF)
        out[1, n] = column.astype(BF)
        if n == 1:
            row = jnp.where(corner, column, row)
            cor[...] = column[:96].reshape(2, 6, 8, D)[:, 3:6].reshape(48, D).astype(BF)
        edge = row.reshape(3, 6, 8, D)[:, 3:6].reshape(72, D)
        lat[n] = jnp.concatenate([edge, jnp.zeros((8, D), F32)], 0).astype(BF)
        lon[n] = column[:96].astype(BF)


def join_kernel(scalars, lat, lon, cor, out):
    out[0:80] = lat[0]
    out[80:160] = lat[1]
    out[160:256] = lon[0]
    out[256:352] = lon[1]
    out[352:400] = cor[...]


def pack_kernel(scalars, payload, first, second, small, small_theirs, out):
    share = out.shape[0]
    other = jnp.concatenate([first[...], second[...]], 0).astype(F32)
    rows = (payload[...] + other).reshape(share, 2048 // share, 128)
    small = small[...] + small_theirs[...]
    high = small.astype(BF).astype(F32)
    pair = jnp.concatenate([high[:, None], (small - high)[:, None], jnp.zeros((8, 6, 128), F32)], 1)
    ride = jnp.concatenate([pair, jnp.zeros((share - 8, 8, 128), F32)], 0)
    out[...] = jnp.concatenate([rows, ride], 1).astype(BF)


def copy_kernel(scalars, a, out):
    out[...] = a[...]


def sum_kernel(scalars, parts, out):
    out[...] = jnp.sum(parts[...].astype(F32), axis=0)


def spread_kernel(scalars, a, b, out):
    total = a[...] + b[...]
    rows = total.shape[0] - 8
    extra = total[rows : rows + 1] + total[rows + 1 : rows + 2]
    high = extra.astype(BF).astype(F32)
    total = jnp.concatenate([total[:rows], high, extra - high, jnp.zeros((6, 128), F32)], 0)
    out[...] = jnp.broadcast_to(total.astype(BF)[None], out.shape)


def small_kernel(scalars, parts, small):
    rows = parts.shape[1] - 8
    values = parts[0:8].astype(F32)
    small[...] = values[:, rows] + values[:, rows + 1]


def unpack_kernel(scalars, parts, gq, go):
    values = parts[...].astype(F32)
    rows = values.shape[1] - 8
    rows = values[:, :rows].reshape(2048, 128)
    for t in range(3):
        gq[t] = rows[512 * t : 512 * t + 512]
    for n in range(4):
        go[:, 128 * n : 128 * n + 128] = rows[1536 + 128 * n : 1664 + 128 * n]


def tile_kernel(scalars, tok, cot, a0, a1, b0, b1, ha, hb, gain, out, windows, halos, stage):
    step = pl.program_id(0)

    @pl.when(step == 0)
    def _():
        place_windows(scalars, a0, a1, b0, b1, ha, hb, windows, halos, stage)

    x, g = tok[...].astype(F32), cot[...].astype(F32)
    unit, inv_std = normalised(x)
    scaled = stage[:, pl.ds(3 * step, 3), 8:56, :] * gain[...].reshape(1, 1, 1, D)
    mean = jnp.sum(scaled, axis=-1, keepdims=True) * (1.0 / D)
    along = jnp.sum(scaled * unit, axis=-1, keepdims=True) * (1.0 / D)
    out[...] = (g + inv_std * (scaled - mean - unit * along)).astype(BF)


def place_windows(scalars, a0, a1, b0, b1, ha, hb, windows, halos, stage):
    for n, (early, late, halo) in enumerate(((a0, a1, ha), (b0, b1, hb))):
        windows[n, 0:2] = early[...]
        windows[n, 2:4] = late[...]
        halos[n] = halo[...]
    core = scalars[2]

    def holder(j):
        return jnp.where(core == j % 2, 0, 1)

    for j in range(4):
        at = 80 * (j % 2)
        edge = halos[holder(j // 2), at : at + 80, :].astype(F32)[:72].reshape(3, 3, 8, D)
        column = 14 + 12 * j
        wide, narrow = (0, 8) if j < 3 else (4, 0)
        stage[:, 0:3, column + wide : column + wide + 8, :] = edge[0:2]
        stage[0, 0:3, column + narrow : column + narrow + 4, :] = edge[2, :, 0:4]
        stage[1, 0:3, column + narrow : column + narrow + 4, :] = edge[2, :, 4:8]
        rows = 6 if j < 3 else 3
        at = 160 + 96 * (j // 2)
        strip = halos[holder(j), at : at + 96, :].astype(F32).reshape(2, 6, 8, D)
        stage[:, 3 + 6 * j : 3 + 6 * j + rows, 6:14, :] = strip[:, :rows]
    stage[:, 0:3, 6:14, :] = halos[holder(3), 352:400, :].astype(F32).reshape(2, 3, 8, D)
    for group in range(4):
        for j in range(4):
            row, col = PLACE[group][j]
            rows = 6 if row < 3 else 3
            value = windows[holder(j), group, j // 2].astype(F32)
            full = value[:96].reshape(2, 6, 8, D)[:, :rows]
            rest = value[96:].reshape(6, 8, D)[:rows]
            column = 14 + 12 * col
            wide, narrow = (0, 8) if group < 3 else (4, 0)
            at = slice(3 + 6 * row, 3 + 6 * row + rows)
            stage[:, at, column + wide : column + wide + 8, :] = full
            stage[0, at, column + narrow : column + narrow + 4, :] = rest[:, 0:4]
            stage[1, at, column + narrow : column + narrow + 4, :] = rest[:, 4:8]


def per_device(tokens, cotangent, norm_gain, norm_bias, w_qkv, w_out):
    core = lax.axis_index("tp") % 2
    edge = lax.axis_index("lat") == lax.axis_size("lat") - 1

    def scalars(first, second):
        masked = jnp.stack([edge & first, edge & second])
        return jnp.concatenate([jnp.where(masked, 1, 0), core.reshape(1)]).astype(jnp.int32)

    never = core < 0
    no_mask, row_mask, column_mask = scalars(never, never), scalars(core >= 0, core == 0), scalars(never, core == 1)

    def swap(block, bit):
        return move(block, ("tp",), lambda t: (t ^ bit,))

    both = (tokens, cotangent)
    h_lat, h_lon, h_cor, mine, *first_rows = kernel_call(
        halo_kernel,
        1,
        no_mask,
        [(a, ANYWHERE) for a in (tokens, cotangent, w_qkv.transpose(1, 0, 2), w_out)],
        [],
        [((4, 3, 32, D), BF), ((4, 12, 8, D), BF), ((4, 3, 8, D), BF), ((512, D), BF)] + [((2, 6, 48, D), BF)] * 2,
        [
            pltpu.VMEM((2, 2, 15, 16, D), BF),
            pltpu.VMEM((3, D, 128), BF),
            pltpu.SemaphoreType.DMA((14,)),
        ],
    )
    theirs = swap(mine, 1)
    h_lat = move(h_lat, ("lat", "tp"), lambda a, t: (a - 1, t ^ 2))
    h_lon = move(h_lon, ("lon",), lambda a: (a - 1,))
    h_cor = move(h_cor, ("lat", "lon"), lambda a, b: (a - 1, b - 1))

    gain = norm_gain.reshape(1, D)
    params = [gain, norm_bias.reshape(1, D), mine, theirs]
    masks = [pltpu.VMEM((2, SPAN, SPAN), F32)]
    half0, *sums, tile_x, tile_g = group_call(
        inner_kernel(0),
        no_mask,
        both,
        first_rows + params,
        [],
        [(t.shape, BF) for t in both],
        (2, 6, 48),
        [pltpu.SemaphoreType.DMA((2, 4))],
        FLOPS[0],
    )
    other0 = swap(half0, 2)
    tiles_in = [tile_x, tile_g]
    half1, *sums = group_call(
        inner_kernel(1), no_mask, [], tiles_in + params, sums, [], (2, 12, 48), [], FLOPS[1]
    )
    other1 = swap(half1, 2)
    half2, *sums = group_call(
        row_kernel, row_mask, [], tiles_in + [h_lat] + params, sums, [], (2, 12, 48), masks, FLOPS[2]
    )
    other2 = swap(half2, 2)
    half3, _, _, _, payload, *payload_theirs, small = group_call(
        column_kernel,
        column_mask,
        [],
        tiles_in + [h_lat, h_lon, h_cor] + params,
        sums,
        [((2048, 128), F32), ((1024, 128), BF), ((1024, 128), BF), ((8, 128), F32)],
        (2, 12, 24),
        masks,
        FLOPS[3],
        [other0],
    )
    other3 = swap(half3, 2)

    lats, lons = lax.axis_size("lat"), lax.axis_size("lon")
    tiles = lats // 2 * lons
    shares = ((tiles, 2048 // tiles + 8, 128), BF)
    groups = [[a * lons + b for a in range(half, lats, 2) for b in range(lons)] for half in range(2)]

    def exchange(block):
        return lax.all_to_all(block, ("lat", "lon"), 0, 0, axis_index_groups=groups, tiled=True)

    small = kernel_call(copy_kernel, 1, no_mask, [], [small], ((8, 128), F32), (), [other1])
    packed = kernel_call(
        pack_kernel, 1, no_mask, [], [payload, *(swap(p, 1) for p in payload_theirs), small, swap(small, 1)], shares, (), [other2]
    )
    parts = exchange(packed)

    early = kernel_call(
        early_kernel,
        1,
        no_mask,
        [(a, whole(a.shape)) for a in (half0, half1)],
        [other0, other1],
        ((2, 2, SPAN, D), BF),
    )
    late, lat_edge, lon_edge, cor_edge = kernel_call(
        late_kernel,
        1,
        no_mask,
        [(a, whole(a.shape)) for a in (half2, half3)],
        [other2, other3],
        [((2, 2, SPAN, D), BF), ((2, 80, D), BF), ((2, 96, D), BF), ((48, D), BF)],
        flops=FLOPS[4],
    )
    lat_edge = move(lat_edge, ("lat", "tp"), lambda a, t: (a + 1, t ^ 2))
    lon_edge = move(lon_edge, ("lon",), lambda a: (a + 1,))
    cor_edge = move(cor_edge, ("lat", "lon"), lambda a, b: (a + 1, b + 1))
    edges = kernel_call(join_kernel, 1, no_mask, [], [lat_edge, lon_edge, cor_edge], ((400, D), BF))
    total = kernel_call(sum_kernel, 1, no_mask, [], [parts], (shares[0][1:], F32))
    other = move(total, ("lat",), lambda a: (a ^ 1,))
    spread = kernel_call(spread_kernel, 1, no_mask, [], [total, other], shares, (), [edges])
    gathered = exchange(spread)
    rows = pl.BlockSpec((2, 3, 48, D), lambda i, scalars: (0, i, 0, 0))
    grad_tokens = kernel_call(
        tile_kernel,
        8,
        no_mask,
        [(tokens, rows), (cotangent, rows)],
        [early, late, swap(early, 1), swap(late, 1), edges, swap(edges, 1), gain],
        (tokens.shape, BF, rows),
        [
            pltpu.VMEM((2, 4, 2, SPAN, D), BF),
            pltpu.VMEM((2, 400, D), BF),
            pltpu.VMEM((2, 24, 64, D), F32),
        ],
    )
    tokens_done = pltpu.with_memory_space_constraint(grad_tokens, pltpu.HBM)
    small = kernel_call(small_kernel, 1, no_mask, [], [gathered], ((8, 128), F32), (), [tokens_done])
    small_y = swap(small, 2)
    grad_qkv, grad_out = kernel_call(
        unpack_kernel,
        1,
        no_mask,
        [],
        [gathered],
        [((3, D, 128), F32, whole((3, D, 128))), ((128, D), F32, whole((128, D)))],
        (),
        [small],
    )
    small = small + small_y
    small = small.reshape(2, D)
    return (grad_tokens, small[0], small[1], grad_qkv.transpose(1, 0, 2), grad_out)


def solution(mesh):
    return jax.shard_map(
        per_device,
        mesh=mesh,
        in_specs=(
            P(None, "lat", "lon", None),
            P(None, "lat", "lon", None),
            P(),
            P(),
            P(None, None, "tp"),
            P("tp", None),
        ),
        out_specs=(P(None, "lat", "lon", None), P(), P(), P(None, None, "tp"), P("tp", None)),
        check_vma=False,
    )
```

```python
import jax
import jax.numpy as jnp
from jax import lax
from jax.experimental import pallas as pl
from jax.experimental.pallas import tpu as pltpu
from jax.sharding import PartitionSpec as P

HEAD = 64
SLAT = 3
SLON = 6
SPAN = 144
D = 512
BF = jnp.bfloat16
F32 = jnp.float32
NT = (((1,), (1,)), ((), ()))
NN = (((1,), (0,)), ((), ()))
TN = (((0,), (0,)), ((), ()))
FLOPS = 4_000_000_000, 50_000_000, 50_000_000, 50_000_000, 8_000_000_000
INSIDE = pl.BlockSpec(memory_space=pltpu.VMEM)
ANYWHERE = pl.BlockSpec(memory_space=pl.ANY)
VMEM_BYTES = 32 * 1024 * 1024

PLACE = (
    ((0, 0), (2, 0), (0, 1), (2, 1)),
    ((1, 0), (0, 2), (1, 1), (1, 2)),
    ((3, 0), (3, 2), (3, 1), (2, 2)),
    ((0, 3), (1, 3), (2, 3), (3, 3)),
)


def dot(a, b, form):
    return lax.dot_general(a, b, form, preferred_element_type=F32)


def move(block, axes, step):
    sizes = [lax.axis_size(axis) for axis in axes]
    total = 1
    for size in sizes:
        total *= size

    def index(coords):
        flat = 0
        for size, coord in zip(sizes, coords):
            flat = flat * size + coord % size
        return flat

    def coords(flat):
        out = []
        for size in reversed(sizes):
            out.append(flat % size)
            flat //= size
        return tuple(reversed(out))

    return lax.ppermute(block, axes, [(i, index(step(*coords(i)))) for i in range(total)])


def even_window(ref, row, column):
    rows = slice(row, row + 6)
    top = lax.broadcasted_iota(jnp.int32, (6, 8, D), 1) < 4
    full = ref[:, rows, column : column + 8, :].reshape(96, D)
    rest = jnp.where(
        top, ref[0, rows, column + 8 : column + 16, :], ref[1, rows, column + 4 : column + 12, :]
    )
    return jnp.concatenate([full, rest.reshape(48, D)], 0)


def odd_window(ref, row, column):
    rows = slice(row, row + 6)
    top = lax.broadcasted_iota(jnp.int32, (6, 8, D), 1) < 4
    full = ref[:, rows, column + 4 : column + 12, :].reshape(96, D)
    rest = jnp.where(
        top, ref[0, rows, column : column + 8, :], ref[1, rows, column - 4 : column + 4, :]
    )
    return jnp.concatenate([full, rest.reshape(48, D)], 0)


def normalised(x):
    mean = jnp.sum(x, axis=-1, keepdims=True) * (1.0 / D)
    centered = x - mean
    inv_std = lax.rsqrt(jnp.sum(centered * centered, axis=-1, keepdims=True) * (1.0 / D) + 1e-05)
    return centered * inv_std, inv_std


def window_steps(xs, gs, gain, bias, weights, masks, sums, gb_acc):
    left = lax.broadcasted_iota(jnp.int32, (SPAN, 128), 1) < HEAD
    zero = jnp.zeros((SPAN, 128), BF)

    def by_head(a):
        parts = [(jnp.where(left, half, zero), jnp.where(left, zero, half)) for half in (a[:, :128], a[:, 128:])]
        rows = [jnp.concatenate([part, zero], 1) for part in parts[0]]
        return jnp.concatenate(rows + [jnp.concatenate([zero, part], 1) for part in parts[1]], 0)

    count = range(len(xs))
    unit = [normalised(x.astype(F32))[0] for x in xs]
    normed = [(u * gain + bias).astype(BF) for u in unit]
    both = [(n, w) for n in count for w in range(2)]
    to_heads = jnp.concatenate([weights[w][0:384, :] for w in range(2)], 0)
    to_keys = jnp.concatenate([weights[w][r : r + 128, :] for r in (128, 256) for w in range(2)], 0)
    to_grads = jnp.concatenate([weights[w][384:512, :] for w in range(2)], 0)
    all_proj = [dot(to_heads, normed[n], NT).astype(BF) for n in count]
    all_kv = [dot(normed[n], to_keys, NT).astype(BF) for n in count]
    all_da = [dot(to_grads, gs[n], NT).astype(BF) for n in count]
    proj = {(n, w): all_proj[n][384 * w : 384 * w + 384] for n, w in both}
    da = {(n, w): all_da[n][128 * w : 128 * w + 128] for n, w in both}
    q = {i: p[0:128] * 0.125 for i, p in proj.items()}
    k = {i: p[128:256] for i, p in proj.items()}
    v = {i: p[256:384] for i, p in proj.items()}
    all_q = [jnp.concatenate([q[n, 0], q[n, 1]], 0) for n in count]
    scores = [dot(by_head(all_kv[n][:, :256]), all_q[n], NN) for n in count]
    d_probs = [dot(by_head(all_kv[n][:, 256:]), all_da[n], NN) for n in count]
    heads = [(i, head) for i in both for head in range(2)]
    probs, ds = {}, {}
    for i, head in heads:
        at = (2 * i[1] + head) * SPAN
        s = scores[i[0]][at : at + SPAN]
        if masks is not None:
            s = s + masks[i[0]]
        raised = jnp.exp(s - jnp.max(s, axis=0, keepdims=True))
        probs[i, head] = (raised * (1.0 / jnp.sum(raised, axis=0, keepdims=True))).astype(BF)
    for i, head in heads:
        pf = probs[i, head].astype(F32)
        at = (2 * i[1] + head) * SPAN
        dp = d_probs[i[0]][at : at + SPAN]
        ds[i, head] = (pf * (dp - jnp.sum(pf * dp, axis=0, keepdims=True))).astype(BF)
    cuts = [slice(0, HEAD), slice(HEAD, 2 * HEAD)]
    att = {(i, h): dot(v[i][cuts[h]], probs[i, h], NN).astype(BF) for i, h in heads}
    dv = {(i, h): dot(da[i][cuts[h]], probs[i, h], NT).astype(BF) for i, h in heads}
    dq = {(i, h): (dot(k[i][cuts[h]], ds[i, h], NN) * 0.125).astype(BF) for i, h in heads}
    dk = {(i, h): dot(q[i][cuts[h]], ds[i, h], NT).astype(BF) for i, h in heads}
    attended = {i: jnp.concatenate([att[i, 0], att[i, 1]], 0) for i in both}
    d_project = {
        i: jnp.concatenate([dq[i, 0], dq[i, 1], dk[i, 0], dk[i, 1], dv[i, 0], dv[i, 1]], 0) for i in both
    }
    d_heads = [jnp.concatenate([d_project[n, w] for w in range(2)], 0) for n in count]
    heads_out = [jnp.concatenate([attended[n, w] for w in range(2)], 0) for n in count]
    d_weights = sum(dot(d_heads[n], normed[n], NN) for n in count)
    d_out = sum(dot(heads_out[n], gs[n], NN) for n in count)
    for w in range(2):
        sums[w][0:384, :] += d_weights[384 * w : 384 * w + 384]
        sums[w][384:512, :] += d_out[128 * w : 128 * w + 128]
    dn = [dot(d_heads[n], to_heads, TN) for n in count]
    gb_acc[0:8, :] += sum(jnp.sum((dn[n] * unit[n]).reshape(SPAN // 8, 8, D), axis=0) for n in count)
    gb_acc[8:16, :] += sum(jnp.sum(dn[n].reshape(SPAN // 8, 8, D), axis=0) for n in count)
    return [d.astype(BF) for d in dn]


def group_steps(scalars, windows, masks, gain_ref, bias_ref, weights, sums, gb_acc, out):
    xs, gs = ([ref[n] for n in range(2)] for ref in windows)
    added = None if masks is None else [masks[scalars[n]] for n in range(2)]
    dn = window_steps(xs, gs, gain_ref[...], bias_ref[...], weights, added, sums, gb_acc)
    for n in range(2):
        out[0, n] = dn[n]


def inner_kernel(group):
    def kernel(scalars, *refs):
        core = scalars[2]
        if group == 0:
            hbm, rows_in, refs = refs[:2], refs[2:4], refs[4:]
            gain, bias, mine, theirs, dn, sum_mine, sum_theirs, gb, *tiles = refs[:10]
            stage, xw, gw, load_sems = refs[10:]
            pieces = ((3 + 12 * core, 6), (9, 6), (15 - 12 * core, 6), (21, 3))
            loads = [
                [
                    pltpu.make_async_copy(
                        hbm[n].at[:, pl.ds(start, rows)], tiles[n].at[:, pl.ds(start, rows)], load_sems.at[n, m]
                    )
                    for n in range(2)
                ]
                for m, (start, rows) in enumerate(pieces)
            ]
            for piece in loads:
                for load in piece:
                    load.start()
            sum_mine[...] = jnp.zeros_like(sum_mine)
            sum_theirs[...] = jnp.zeros_like(sum_theirs)
            gb[...] = jnp.zeros_like(gb)
            rows = []
        else:
            tiles, refs = refs[:2], refs[2:]
            gain, bias, mine, theirs = refs[:4]
            dn, sum_mine, sum_theirs, gb, stage, xw, gw = refs[7:]
            loads = []
            rows = [1 - core, 1]
        for tile, out in zip(rows_in if group == 0 else tiles, (xw, gw)):
            if group == 0:
                stage[...] = tile[...].astype(F32)
            for n, row in enumerate(rows):
                stage[:, 6 * n : 6 * n + 6, :, :] = tile[:, pl.ds(3 + 6 * row, 6), :, :].astype(F32)
            for c in range(2):

                @pl.when(core == c)
                def _():
                    for n in range(2):
                        column = PLACE[group][2 * n + c][1]
                        out[n] = even_window(stage, 6 * n * group, SLON + 12 * column).astype(BF)

        group_steps(scalars, (xw, gw), None, gain, bias, (mine, theirs), (sum_mine, sum_theirs), gb, dn)
        for piece in loads:
            for load in piece:
                load.wait()

    return kernel


def row_kernel(
    scalars, tok, cot, h_lat, gain_ref, bias_ref, mine, theirs, in_mine, in_theirs, gb_in,
    dn, sum_mine, sum_theirs, gb, stage, xw, gw, masks,
):
    fill_masks(masks)
    core = scalars[2]
    for part, tile, out in ((0, tok, xw), (2, cot, gw)):
        stage[:, 0:9, :, :] = tile[:, 15:24, :, :].astype(F32)
        for c in range(2):

            @pl.when(core == c)
            def _():
                stage[:, 9:12, 16 * c : 16 * c + 32, :] = h_lat[part : part + 2].astype(F32)
                for n in range(2):
                    row, column = PLACE[2][2 * n + c]
                    out[n] = even_window(stage, 6 * (row - 2), SLON + 12 * column).astype(BF)

    group_steps(scalars, (xw, gw), masks, gain_ref, bias_ref, (mine, theirs), (sum_mine, sum_theirs), gb, dn)


def column_kernel(
    scalars, tok, cot, h_lat, h_lon, h_cor, gain_ref, bias_ref, mine, theirs, in_mine, in_theirs, gb_in,
    dn, sum_mine, sum_theirs, gb, payload_mine, first_theirs, second_theirs, small,
    stage, xw, gw, masks,
):
    fill_masks(masks)
    core = scalars[2]
    for part, tile, out in ((0, tok, xw), (2, cot, gw)):
        for n in range(2):
            rows = pl.ds(3 + 12 * n + 6 * core, 3)
            stage[:, 6 * n : 6 * n + 3, 0:16, :] = tile[:, rows, 32:48, :].astype(F32)
            stage[:, 6 * n : 6 * n + 6, 16:24, :] = h_lon[part : part + 2, 6 * n : 6 * n + 6].astype(F32)
        stage[:, 3:6, 0:16, :] = tile[:, pl.ds(6 + 6 * core, 3), 32:48, :].astype(F32)

        @pl.when(core == 0)
        def _():
            stage[:, 9:12, 0:16, :] = tile[:, 18:21, 32:48, :].astype(F32)

        @pl.when(core == 1)
        def _():
            stage[:, 9:12, 0:16, :] = h_lat[part : part + 2, :, 16:32, :].astype(F32)
            stage[:, 9:12, 16:24, :] = h_cor[part : part + 2].astype(F32)

        for n in range(2):
            out[n] = odd_window(stage, 6 * n, 10).astype(BF)
    group_steps(scalars, (xw, gw), masks, gain_ref, bias_ref, (mine, theirs), (sum_mine, sum_theirs), gb, dn)
    for t in range(4):
        for sums, payload in (sum_mine, (payload_mine, t)), (sum_theirs, ((first_theirs, second_theirs)[t // 2], t % 2)):
            ref, place = payload
            if t < 3:
                rows = sums[128 * t : 128 * t + 128, :].T
            else:
                rows = jnp.concatenate([sums[384:512, 128 * n : 128 * n + 128] for n in range(4)], 0)
            ref[512 * place : 512 * place + 512, :] = rows.astype(ref.dtype)
    pair = [jnp.sum(gb[8 * n : 8 * n + 8, :], axis=0, keepdims=True) for n in range(2)]
    small[...] = jnp.concatenate([s[:, 128 * n : 128 * n + 128] for s in pair for n in range(4)], 0)


def fill_masks(masks):
    key_row = lax.broadcasted_iota(jnp.int32, (SPAN, SPAN), 0) // 8 % 6
    query_row = lax.broadcasted_iota(jnp.int32, (SPAN, SPAN), 1) // 8 % 6
    masks[0] = jnp.zeros((SPAN, SPAN), F32)
    masks[1] = jnp.where((key_row >= 3) != (query_row >= 3), -1e30, 0.0)


def whole(shape):
    return pl.BlockSpec(shape, lambda i, scalars: (0,) * len(shape))


SUMS = [((512, D), F32), ((512, D), F32), ((16, D), F32)]


def kernel_call(kernel, steps, scalars, blocks, args, outs, scratch=(), waits=(), aliases=None, flops=5_000_000):
    many = isinstance(outs, list)
    out_list = outs if many else [outs]
    first = 1 + len(blocks) + len(args)

    def body(*refs):
        kernel(*refs[:first], *refs[first + len(waits) :])

    result = pl.pallas_call(
        body,
        grid_spec=pltpu.PrefetchScalarGridSpec(
            num_scalar_prefetch=1,
            grid=(steps,),
            in_specs=[spec for _, spec in blocks] + [INSIDE] * len(args) + [ANYWHERE] * len(waits),
            out_specs=[out[2] if len(out) > 2 else INSIDE for out in out_list],
            scratch_shapes=scratch,
        ),
        out_shape=[
            pltpu.HBM(*out[:2]) if len(out) > 2 else jax.ShapeDtypeStruct(*out) for out in out_list
        ],
        input_output_aliases=aliases or {},
        compiler_params=pltpu.CompilerParams(
            dimension_semantics=("arbitrary",), vmem_limit_bytes=VMEM_BYTES
        ),
        cost_estimate=pl.CostEstimate(flops=flops, bytes_accessed=1_000_000, transcendentals=0),
    )(
        scalars,
        *(pltpu.with_memory_space_constraint(array, pltpu.HBM) for array, _ in blocks),
        *args,
        *waits,
    )
    return result if many else result[0]


def group_call(kernel, scalars, arrays, args, sums, extra_out, rows, scratch, flops, waits=()):
    shape = (1, 2, SPAN, D)
    outs = [(shape, BF, whole(shape))] + SUMS + extra_out
    start = 1 + len(arrays) + len(args)
    aliases = {start + n: 1 + n for n in range(len(sums))}
    stage = [pltpu.VMEM(rows + (D,), F32)] + [pltpu.VMEM((2, SPAN, D), BF)] * 2
    blocks = [(a, ANYWHERE) for a in arrays]
    return kernel_call(kernel, 1, scalars, blocks, args + sums, outs, stage + scratch, waits, aliases, flops)


def halo_kernel(scalars, tok, cot, w_qkv, w_out, lat, lon, cor, weights, first_x, first_g, strips, w, sems):
    core = scalars[2]
    copies = [
        pltpu.make_async_copy(w_qkv, w, sems.at[0]),
        pltpu.make_async_copy(w_out, weights.at[384:512], sems.at[1]),
    ]
    for n, ref in enumerate((tok, cot)):
        for m, (source, at, rows) in enumerate(
            ((0, 0, 3), (3 + 6 * core, 3, 6), (15 + 6 * core, 9, 3), (18 + 3 * core, 12, 3))
        ):
            copies.append(
                pltpu.make_async_copy(
                    ref.at[:, pl.ds(source, rows), 0:16, :], strips.at[n, :, at : at + rows], sems.at[2 + 5 * n + m]
                )
            )
        columns = pl.ds(pl.multiple_of(16 * core, 16), 32)
        copies.append(
            pltpu.make_async_copy(
                ref.at[:, 0:3, columns, :], lat.at[2 * n : 2 * n + 2], sems.at[6 + 5 * n]
            )
        )
    for n, (ref, first) in enumerate(((tok, first_x), (cot, first_g))):
        copies.append(pltpu.make_async_copy(ref.at[:, pl.ds(3 + 12 * core, 6)], first, sems.at[12 + n]))
    for copy in copies:
        copy.start()
    copies[0].wait()
    for t in range(3):
        weights[128 * t : 128 * t + 128, :] = w[t].T
    for copy in copies[1:]:
        copy.wait()
    for n in range(2):
        strip = strips[n].astype(F32)[:, :, 0:8].astype(BF)
        cor[2 * n : 2 * n + 2] = strip[:, 0:3]
        lon[2 * n : 2 * n + 2] = strip[:, 3:15]


def early_kernel(scalars, half0, half1, other0, other1, out):
    for group, (half, other) in enumerate(((half0, other0), (half1, other1))):
        out[group] = (half[0].astype(F32) + other[0].astype(F32)).astype(BF)


def late_kernel(scalars, half2, half3, other2, other3, out, lat, lon, cor):
    corner = scalars[2] == 1
    for n in range(2):
        row = half2[0, n].astype(F32) + other2[0, n].astype(F32)
        column = half3[0, n].astype(F32) + other3[0, n].astype(F32)
        out[0, n] = row.astype(BF)
        out[1, n] = column.astype(BF)
        if n == 1:
            row = jnp.where(corner, column, row)
            cor[...] = column[:96].reshape(2, 6, 8, D)[:, 3:6].reshape(48, D).astype(BF)
        edge = row.reshape(3, 6, 8, D)[:, 3:6].reshape(72, D)
        lat[n] = jnp.concatenate([edge, jnp.zeros((8, D), F32)], 0).astype(BF)
        lon[n] = column[:96].astype(BF)


def join_kernel(scalars, lat, lon, cor, out):
    out[0:80] = lat[0]
    out[80:160] = lat[1]
    out[160:256] = lon[0]
    out[256:352] = lon[1]
    out[352:400] = cor[...]


def pack_kernel(scalars, payload, first, second, small, small_theirs, out):
    share = out.shape[0]
    other = jnp.concatenate([first[...], second[...]], 0).astype(F32)
    rows = (payload[...] + other).reshape(share, 2048 // share, 128)
    small = small[...] + small_theirs[...]
    high = small.astype(BF).astype(F32)
    pair = jnp.concatenate([high[:, None], (small - high)[:, None], jnp.zeros((8, 6, 128), F32)], 1)
    ride = jnp.concatenate([pair, jnp.zeros((share - 8, 8, 128), F32)], 0)
    out[...] = jnp.concatenate([rows, ride], 1).astype(BF)


def copy_kernel(scalars, a, out):
    out[...] = a[...]


def sum_kernel(scalars, parts, out):
    out[...] = jnp.sum(parts[...].astype(F32), axis=0)


def spread_kernel(scalars, a, b, out):
    total = a[...] + b[...]
    rows = total.shape[0] - 8
    extra = total[rows : rows + 1] + total[rows + 1 : rows + 2]
    high = extra.astype(BF).astype(F32)
    total = jnp.concatenate([total[:rows], high, extra - high, jnp.zeros((6, 128), F32)], 0)
    out[...] = jnp.broadcast_to(total.astype(BF)[None], out.shape)


def small_kernel(scalars, parts, small):
    rows = parts.shape[1] - 8
    values = parts[0:8].astype(F32)
    small[...] = values[:, rows] + values[:, rows + 1]


def unpack_kernel(scalars, parts, gq, go):
    values = parts[...].astype(F32)
    rows = values.shape[1] - 8
    rows = values[:, :rows].reshape(2048, 128)
    for t in range(3):
        gq[t] = rows[512 * t : 512 * t + 512]
    for n in range(4):
        go[:, 128 * n : 128 * n + 128] = rows[1536 + 128 * n : 1664 + 128 * n]


def tile_kernel(scalars, tok, cot, a0, a1, b0, b1, ha, hb, gain, out, windows, halos, stage):
    step = pl.program_id(0)

    @pl.when(step == 0)
    def _():
        place_windows(scalars, a0, a1, b0, b1, ha, hb, windows, halos, stage)

    x, g = tok[...].astype(F32), cot[...].astype(F32)
    unit, inv_std = normalised(x)
    scaled = stage[:, pl.ds(3 * step, 3), 8:56, :] * gain[...].reshape(1, 1, 1, D)
    mean = jnp.sum(scaled, axis=-1, keepdims=True) * (1.0 / D)
    along = jnp.sum(scaled * unit, axis=-1, keepdims=True) * (1.0 / D)
    out[...] = (g + inv_std * (scaled - mean - unit * along)).astype(BF)


def place_windows(scalars, a0, a1, b0, b1, ha, hb, windows, halos, stage):
    for n, (early, late, halo) in enumerate(((a0, a1, ha), (b0, b1, hb))):
        windows[n, 0:2] = early[...]
        windows[n, 2:4] = late[...]
        halos[n] = halo[...]
    core = scalars[2]

    def holder(j):
        return jnp.where(core == j % 2, 0, 1)

    for j in range(4):
        at = 80 * (j % 2)
        edge = halos[holder(j // 2), at : at + 80, :].astype(F32)[:72].reshape(3, 3, 8, D)
        column = 14 + 12 * j
        wide, narrow = (0, 8) if j < 3 else (4, 0)
        stage[:, 0:3, column + wide : column + wide + 8, :] = edge[0:2]
        stage[0, 0:3, column + narrow : column + narrow + 4, :] = edge[2, :, 0:4]
        stage[1, 0:3, column + narrow : column + narrow + 4, :] = edge[2, :, 4:8]
        rows = 6 if j < 3 else 3
        at = 160 + 96 * (j // 2)
        strip = halos[holder(j), at : at + 96, :].astype(F32).reshape(2, 6, 8, D)
        stage[:, 3 + 6 * j : 3 + 6 * j + rows, 6:14, :] = strip[:, :rows]
    stage[:, 0:3, 6:14, :] = halos[holder(3), 352:400, :].astype(F32).reshape(2, 3, 8, D)
    for group in range(4):
        for j in range(4):
            row, col = PLACE[group][j]
            rows = 6 if row < 3 else 3
            value = windows[holder(j), group, j // 2].astype(F32)
            full = value[:96].reshape(2, 6, 8, D)[:, :rows]
            rest = value[96:].reshape(6, 8, D)[:rows]
            column = 14 + 12 * col
            wide, narrow = (0, 8) if group < 3 else (4, 0)
            at = slice(3 + 6 * row, 3 + 6 * row + rows)
            stage[:, at, column + wide : column + wide + 8, :] = full
            stage[0, at, column + narrow : column + narrow + 4, :] = rest[:, 0:4]
            stage[1, at, column + narrow : column + narrow + 4, :] = rest[:, 4:8]


def per_device(tokens, cotangent, norm_gain, norm_bias, w_qkv, w_out):
    core = lax.axis_index("tp") % 2
    edge = lax.axis_index("lat") == lax.axis_size("lat") - 1

    def scalars(first, second):
        masked = jnp.stack([edge & first, edge & second])
        return jnp.concatenate([jnp.where(masked, 1, 0), core.reshape(1)]).astype(jnp.int32)

    never = core < 0
    no_mask, row_mask, column_mask = scalars(never, never), scalars(core >= 0, core == 0), scalars(never, core == 1)

    def swap(block, bit):
        return move(block, ("tp",), lambda t: (t ^ bit,))

    both = (tokens, cotangent)
    h_lat, h_lon, h_cor, mine, *first_rows = kernel_call(
        halo_kernel,
        1,
        no_mask,
        [(a, ANYWHERE) for a in (tokens, cotangent, w_qkv.transpose(1, 0, 2), w_out)],
        [],
        [((4, 3, 32, D), BF), ((4, 12, 8, D), BF), ((4, 3, 8, D), BF), ((512, D), BF)] + [((2, 6, 48, D), BF)] * 2,
        [
            pltpu.VMEM((2, 2, 15, 16, D), BF),
            pltpu.VMEM((3, D, 128), BF),
            pltpu.SemaphoreType.DMA((14,)),
        ],
    )
    theirs = swap(mine, 1)
    h_lat = move(h_lat, ("lat", "tp"), lambda a, t: (a - 1, t ^ 2))
    h_lon = move(h_lon, ("lon",), lambda a: (a - 1,))
    h_cor = move(h_cor, ("lat", "lon"), lambda a, b: (a - 1, b - 1))

    gain = norm_gain.reshape(1, D)
    params = [gain, norm_bias.reshape(1, D), mine, theirs]
    masks = [pltpu.VMEM((2, SPAN, SPAN), F32)]
    half0, *sums, tile_x, tile_g = group_call(
        inner_kernel(0),
        no_mask,
        both,
        first_rows + params,
        [],
        [(t.shape, BF) for t in both],
        (2, 6, 48),
        [pltpu.SemaphoreType.DMA((2, 4))],
        FLOPS[0],
    )
    other0 = swap(half0, 2)
    tiles_in = [tile_x, tile_g]
    half1, *sums = group_call(
        inner_kernel(1), no_mask, [], tiles_in + params, sums, [], (2, 12, 48), [], FLOPS[1]
    )
    other1 = swap(half1, 2)
    half2, *sums = group_call(
        row_kernel, row_mask, [], tiles_in + [h_lat] + params, sums, [], (2, 12, 48), masks, FLOPS[2]
    )
    other2 = swap(half2, 2)
    half3, _, _, _, payload, *payload_theirs, small = group_call(
        column_kernel,
        column_mask,
        [],
        tiles_in + [h_lat, h_lon, h_cor] + params,
        sums,
        [((2048, 128), F32), ((1024, 128), BF), ((1024, 128), BF), ((8, 128), F32)],
        (2, 12, 24),
        masks,
        FLOPS[3],
        [other0],
    )
    other3 = swap(half3, 2)

    lats, lons = lax.axis_size("lat"), lax.axis_size("lon")
    tiles = lats // 2 * lons
    shares = ((tiles, 2048 // tiles + 8, 128), BF)
    groups = [[a * lons + b for a in range(half, lats, 2) for b in range(lons)] for half in range(2)]

    def exchange(block):
        return lax.all_to_all(block, ("lat", "lon"), 0, 0, axis_index_groups=groups, tiled=True)

    small = kernel_call(copy_kernel, 1, no_mask, [], [small], ((8, 128), F32), (), [other1])
    packed = kernel_call(
        pack_kernel, 1, no_mask, [], [payload, *(swap(p, 1) for p in payload_theirs), small, swap(small, 1)], shares, (), [other2]
    )
    parts = exchange(packed)

    early = kernel_call(
        early_kernel,
        1,
        no_mask,
        [(a, whole(a.shape)) for a in (half0, half1)],
        [other0, other1],
        ((2, 2, SPAN, D), BF),
    )
    late, lat_edge, lon_edge, cor_edge = kernel_call(
        late_kernel,
        1,
        no_mask,
        [(a, whole(a.shape)) for a in (half2, half3)],
        [other2, other3],
        [((2, 2, SPAN, D), BF), ((2, 80, D), BF), ((2, 96, D), BF), ((48, D), BF)],
        flops=FLOPS[4],
    )
    lat_edge = move(lat_edge, ("lat", "tp"), lambda a, t: (a + 1, t ^ 2))
    lon_edge = move(lon_edge, ("lon",), lambda a: (a + 1,))
    cor_edge = move(cor_edge, ("lat", "lon"), lambda a, b: (a + 1, b + 1))
    edges = kernel_call(join_kernel, 1, no_mask, [], [lat_edge, lon_edge, cor_edge], ((400, D), BF))
    total = kernel_call(sum_kernel, 1, no_mask, [], [parts], (shares[0][1:], F32))
    other = move(total, ("lat",), lambda a: (a ^ 1,))
    spread = kernel_call(spread_kernel, 1, no_mask, [], [total, other], shares, (), [edges, early])
    gathered = exchange(spread)
    rows = pl.BlockSpec((2, 3, 48, D), lambda i, scalars: (0, i, 0, 0))
    grad_tokens = kernel_call(
        tile_kernel,
        8,
        no_mask,
        [(tokens, rows), (cotangent, rows)],
        [early, late, swap(early, 1), swap(late, 1), edges, swap(edges, 1), gain],
        (tokens.shape, BF, rows),
        [
            pltpu.VMEM((2, 4, 2, SPAN, D), BF),
            pltpu.VMEM((2, 400, D), BF),
            pltpu.VMEM((2, 24, 64, D), F32),
        ],
    )
    tokens_done = pltpu.with_memory_space_constraint(grad_tokens, pltpu.HBM)
    small = kernel_call(small_kernel, 1, no_mask, [], [gathered], ((8, 128), F32), (), [tokens_done])
    small_y = swap(small, 2)
    grad_qkv, grad_out = kernel_call(
        unpack_kernel,
        1,
        no_mask,
        [],
        [gathered],
        [((3, D, 128), F32, whole((3, D, 128))), ((128, D), F32, whole((128, D)))],
        (),
        [small],
    )
    small = small + small_y
    small = small.reshape(2, D)
    return (grad_tokens, small[0], small[1], grad_qkv.transpose(1, 0, 2), grad_out)


def solution(mesh):
    return jax.shard_map(
        per_device,
        mesh=mesh,
        in_specs=(
            P(None, "lat", "lon", None),
            P(None, "lat", "lon", None),
            P(),
            P(),
            P(None, None, "tp"),
            P("tp", None),
        ),
        out_specs=(P(None, "lat", "lon", None), P(), P(), P(None, None, "tp"), P("tp", None)),
        check_vma=False,
    )
```

```python
import jax
import jax.numpy as jnp
from jax import lax
from jax.experimental import pallas as pl
from jax.experimental.pallas import tpu as pltpu
from jax.sharding import PartitionSpec as P

HEAD = 64
SLAT = 3
SLON = 6
SPAN = 144
D = 512
BF = jnp.bfloat16
F32 = jnp.float32
NT = (((1,), (1,)), ((), ()))
NN = (((1,), (0,)), ((), ()))
TN = (((0,), (0,)), ((), ()))
FLOPS = 4_000_000_000, 50_000_000, 50_000_000, 50_000_000, 8_000_000_000
INSIDE = pl.BlockSpec(memory_space=pltpu.VMEM)
ANYWHERE = pl.BlockSpec(memory_space=pl.ANY)
VMEM_BYTES = 32 * 1024 * 1024

PLACE = (
    ((0, 0), (2, 0), (0, 1), (2, 1)),
    ((1, 0), (0, 2), (1, 1), (1, 2)),
    ((3, 0), (3, 2), (3, 1), (2, 2)),
    ((0, 3), (1, 3), (2, 3), (3, 3)),
)


def dot(a, b, form):
    return lax.dot_general(a, b, form, preferred_element_type=F32)


def move(block, axes, step):
    sizes = [lax.axis_size(axis) for axis in axes]
    total = 1
    for size in sizes:
        total *= size

    def index(coords):
        flat = 0
        for size, coord in zip(sizes, coords):
            flat = flat * size + coord % size
        return flat

    def coords(flat):
        out = []
        for size in reversed(sizes):
            out.append(flat % size)
            flat //= size
        return tuple(reversed(out))

    return lax.ppermute(block, axes, [(i, index(step(*coords(i)))) for i in range(total)])


def even_window(ref, row, column):
    rows = slice(row, row + 6)
    top = lax.broadcasted_iota(jnp.int32, (6, 8, D), 1) < 4
    full = ref[:, rows, column : column + 8, :].reshape(96, D)
    rest = jnp.where(
        top, ref[0, rows, column + 8 : column + 16, :], ref[1, rows, column + 4 : column + 12, :]
    )
    return jnp.concatenate([full, rest.reshape(48, D)], 0)


def odd_window(ref, row, column):
    rows = slice(row, row + 6)
    top = lax.broadcasted_iota(jnp.int32, (6, 8, D), 1) < 4
    full = ref[:, rows, column + 4 : column + 12, :].reshape(96, D)
    rest = jnp.where(
        top, ref[0, rows, column : column + 8, :], ref[1, rows, column - 4 : column + 4, :]
    )
    return jnp.concatenate([full, rest.reshape(48, D)], 0)


def normalised(x):
    mean = jnp.sum(x, axis=-1, keepdims=True) * (1.0 / D)
    centered = x - mean
    inv_std = lax.rsqrt(jnp.sum(centered * centered, axis=-1, keepdims=True) * (1.0 / D) + 1e-05)
    return centered * inv_std, inv_std


def window_steps(xs, gs, gain, bias, weights, masks, sums, gb_acc):
    left = lax.broadcasted_iota(jnp.int32, (SPAN, 128), 1) < HEAD
    zero = jnp.zeros((SPAN, 128), BF)

    def by_head(a):
        parts = [(jnp.where(left, half, zero), jnp.where(left, zero, half)) for half in (a[:, :128], a[:, 128:])]
        rows = [jnp.concatenate([part, zero], 1) for part in parts[0]]
        return jnp.concatenate(rows + [jnp.concatenate([zero, part], 1) for part in parts[1]], 0)

    count = range(len(xs))
    unit = [normalised(x.astype(F32))[0] for x in xs]
    normed = [(u * gain + bias).astype(BF) for u in unit]
    both = [(n, w) for n in count for w in range(2)]
    to_heads = jnp.concatenate([weights[w][0:384, :] for w in range(2)], 0)
    to_keys = jnp.concatenate([weights[w][r : r + 128, :] for r in (128, 256) for w in range(2)], 0)
    to_grads = jnp.concatenate([weights[w][384:512, :] for w in range(2)], 0)
    all_proj = [dot(to_heads, normed[n], NT).astype(BF) for n in count]
    all_kv = [dot(normed[n], to_keys, NT).astype(BF) for n in count]
    all_da = [dot(to_grads, gs[n], NT).astype(BF) for n in count]
    proj = {(n, w): all_proj[n][384 * w : 384 * w + 384] for n, w in both}
    da = {(n, w): all_da[n][128 * w : 128 * w + 128] for n, w in both}
    q = {i: p[0:128] * 0.125 for i, p in proj.items()}
    k = {i: p[128:256] for i, p in proj.items()}
    v = {i: p[256:384] for i, p in proj.items()}
    all_q = [jnp.concatenate([q[n, 0], q[n, 1]], 0) for n in count]
    scores = [dot(by_head(all_kv[n][:, :256]), all_q[n], NN) for n in count]
    d_probs = [dot(by_head(all_kv[n][:, 256:]), all_da[n], NN) for n in count]
    heads = [(i, head) for i in both for head in range(2)]
    probs, ds = {}, {}
    for i, head in heads:
        at = (2 * i[1] + head) * SPAN
        s = scores[i[0]][at : at + SPAN]
        if masks is not None:
            s = s + masks[i[0]]
        raised = jnp.exp(s - jnp.max(s, axis=0, keepdims=True))
        probs[i, head] = (raised * (1.0 / jnp.sum(raised, axis=0, keepdims=True))).astype(BF)
    for i, head in heads:
        pf = probs[i, head].astype(F32)
        at = (2 * i[1] + head) * SPAN
        dp = d_probs[i[0]][at : at + SPAN]
        ds[i, head] = (pf * (dp - jnp.sum(pf * dp, axis=0, keepdims=True))).astype(BF)
    cuts = [slice(0, HEAD), slice(HEAD, 2 * HEAD)]
    att = {(i, h): dot(v[i][cuts[h]], probs[i, h], NN).astype(BF) for i, h in heads}
    dv = {(i, h): dot(da[i][cuts[h]], probs[i, h], NT).astype(BF) for i, h in heads}
    dq = {(i, h): (dot(k[i][cuts[h]], ds[i, h], NN) * 0.125).astype(BF) for i, h in heads}
    dk = {(i, h): dot(q[i][cuts[h]], ds[i, h], NT).astype(BF) for i, h in heads}
    attended = {i: jnp.concatenate([att[i, 0], att[i, 1]], 0) for i in both}
    d_project = {
        i: jnp.concatenate([dq[i, 0], dq[i, 1], dk[i, 0], dk[i, 1], dv[i, 0], dv[i, 1]], 0) for i in both
    }
    d_heads = [jnp.concatenate([d_project[n, w] for w in range(2)], 0) for n in count]
    heads_out = [jnp.concatenate([attended[n, w] for w in range(2)], 0) for n in count]
    d_weights = sum(dot(d_heads[n], normed[n], NN) for n in count)
    d_out = sum(dot(heads_out[n], gs[n], NN) for n in count)
    for w in range(2):
        sums[w][0:384, :] += d_weights[384 * w : 384 * w + 384]
        sums[w][384:512, :] += d_out[128 * w : 128 * w + 128]
    dn = [dot(d_heads[n], to_heads, TN) for n in count]
    gb_acc[0:8, :] += sum(jnp.sum((dn[n] * unit[n]).reshape(SPAN // 8, 8, D), axis=0) for n in count)
    gb_acc[8:16, :] += sum(jnp.sum(dn[n].reshape(SPAN // 8, 8, D), axis=0) for n in count)
    return [d.astype(BF) for d in dn]


def group_steps(scalars, windows, masks, gain_ref, bias_ref, weights, sums, gb_acc, out):
    xs, gs = ([ref[n] for n in range(2)] for ref in windows)
    added = None if masks is None else [masks[scalars[n]] for n in range(2)]
    dn = window_steps(xs, gs, gain_ref[...], bias_ref[...], weights, added, sums, gb_acc)
    for n in range(2):
        out[0, n] = dn[n]


def inner_kernel(group):
    def kernel(scalars, *refs):
        core = scalars[2]
        if group == 0:
            hbm, rows_in, refs = refs[:2], refs[2:4], refs[4:]
            gain, bias, mine, theirs, dn, sum_mine, sum_theirs, gb, *tiles = refs[:10]
            stage, xw, gw, load_sems = refs[10:]
            pieces = ((3 + 12 * core, 6), (9, 6), (15 - 12 * core, 6), (21, 3))
            loads = [
                [
                    pltpu.make_async_copy(
                        hbm[n].at[:, pl.ds(start, rows)], tiles[n].at[:, pl.ds(start, rows)], load_sems.at[n, m]
                    )
                    for n in range(2)
                ]
                for m, (start, rows) in enumerate(pieces)
            ]
            for piece in loads:
                for load in piece:
                    load.start()
            sum_mine[...] = jnp.zeros_like(sum_mine)
            sum_theirs[...] = jnp.zeros_like(sum_theirs)
            gb[...] = jnp.zeros_like(gb)
            rows = []
        else:
            tiles, refs = refs[:2], refs[2:]
            gain, bias, mine, theirs = refs[:4]
            dn, sum_mine, sum_theirs, gb, stage, xw, gw = refs[7:]
            loads = []
            rows = [1 - core, 1]
        for tile, out in zip(rows_in if group == 0 else tiles, (xw, gw)):
            if group == 0:
                stage[...] = tile[...].astype(F32)
            for n, row in enumerate(rows):
                stage[:, 6 * n : 6 * n + 6, :, :] = tile[:, pl.ds(3 + 6 * row, 6), :, :].astype(F32)
            for c in range(2):

                @pl.when(core == c)
                def _():
                    for n in range(2):
                        column = PLACE[group][2 * n + c][1]
                        out[n] = even_window(stage, 6 * n * group, SLON + 12 * column).astype(BF)

        group_steps(scalars, (xw, gw), None, gain, bias, (mine, theirs), (sum_mine, sum_theirs), gb, dn)
        for piece in loads:
            for load in piece:
                load.wait()

    return kernel


def row_kernel(
    scalars, tok, cot, h_lat, gain_ref, bias_ref, mine, theirs, in_mine, in_theirs, gb_in,
    dn, sum_mine, sum_theirs, gb, stage, xw, gw, masks,
):
    fill_masks(masks)
    core = scalars[2]
    for part, tile, out in ((0, tok, xw), (2, cot, gw)):
        stage[:, 0:9, :, :] = tile[:, 15:24, :, :].astype(F32)
        for c in range(2):

            @pl.when(core == c)
            def _():
                stage[:, 9:12, 16 * c : 16 * c + 32, :] = h_lat[part : part + 2].astype(F32)
                for n in range(2):
                    row, column = PLACE[2][2 * n + c]
                    out[n] = even_window(stage, 6 * (row - 2), SLON + 12 * column).astype(BF)

    group_steps(scalars, (xw, gw), masks, gain_ref, bias_ref, (mine, theirs), (sum_mine, sum_theirs), gb, dn)


def column_kernel(
    scalars, tok, cot, h_lat, h_lon, h_cor, gain_ref, bias_ref, mine, theirs, in_mine, in_theirs, gb_in,
    dn, sum_mine, sum_theirs, gb, payload_mine, first_theirs, second_theirs, small,
    stage, xw, gw, masks,
):
    fill_masks(masks)
    core = scalars[2]
    for part, tile, out in ((0, tok, xw), (2, cot, gw)):
        for n in range(2):
            rows = pl.ds(3 + 12 * n + 6 * core, 3)
            stage[:, 6 * n : 6 * n + 3, 0:16, :] = tile[:, rows, 32:48, :].astype(F32)
            stage[:, 6 * n : 6 * n + 6, 16:24, :] = h_lon[part : part + 2, 6 * n : 6 * n + 6].astype(F32)
        stage[:, 3:6, 0:16, :] = tile[:, pl.ds(6 + 6 * core, 3), 32:48, :].astype(F32)

        @pl.when(core == 0)
        def _():
            stage[:, 9:12, 0:16, :] = tile[:, 18:21, 32:48, :].astype(F32)

        @pl.when(core == 1)
        def _():
            stage[:, 9:12, 0:16, :] = h_lat[part : part + 2, :, 16:32, :].astype(F32)
            stage[:, 9:12, 16:24, :] = h_cor[part : part + 2].astype(F32)

        for n in range(2):
            out[n] = odd_window(stage, 6 * n, 10).astype(BF)
    group_steps(scalars, (xw, gw), masks, gain_ref, bias_ref, (mine, theirs), (sum_mine, sum_theirs), gb, dn)
    for t in range(4):
        for sums, payload in (sum_mine, (payload_mine, t)), (sum_theirs, ((first_theirs, second_theirs)[t // 2], t % 2)):
            ref, place = payload
            if t < 3:
                rows = sums[128 * t : 128 * t + 128, :].T
            else:
                rows = jnp.concatenate([sums[384:512, 128 * n : 128 * n + 128] for n in range(4)], 0)
            ref[512 * place : 512 * place + 512, :] = rows.astype(ref.dtype)
    pair = [jnp.sum(gb[8 * n : 8 * n + 8, :], axis=0, keepdims=True) for n in range(2)]
    small[...] = jnp.concatenate([s[:, 128 * n : 128 * n + 128] for s in pair for n in range(4)], 0)


def fill_masks(masks):
    key_row = lax.broadcasted_iota(jnp.int32, (SPAN, SPAN), 0) // 8 % 6
    query_row = lax.broadcasted_iota(jnp.int32, (SPAN, SPAN), 1) // 8 % 6
    masks[0] = jnp.zeros((SPAN, SPAN), F32)
    masks[1] = jnp.where((key_row >= 3) != (query_row >= 3), -1e30, 0.0)


def whole(shape):
    return pl.BlockSpec(shape, lambda i, scalars: (0,) * len(shape))


SUMS = [((512, D), F32), ((512, D), F32), ((16, D), F32)]


def kernel_call(kernel, steps, scalars, blocks, args, outs, scratch=(), waits=(), aliases=None, flops=5_000_000):
    many = isinstance(outs, list)
    out_list = outs if many else [outs]
    first = 1 + len(blocks) + len(args)

    def body(*refs):
        kernel(*refs[:first], *refs[first + len(waits) :])

    result = pl.pallas_call(
        body,
        grid_spec=pltpu.PrefetchScalarGridSpec(
            num_scalar_prefetch=1,
            grid=(steps,),
            in_specs=[spec for _, spec in blocks] + [INSIDE] * len(args) + [ANYWHERE] * len(waits),
            out_specs=[out[2] if len(out) > 2 else INSIDE for out in out_list],
            scratch_shapes=scratch,
        ),
        out_shape=[
            pltpu.HBM(*out[:2]) if len(out) > 2 else jax.ShapeDtypeStruct(*out) for out in out_list
        ],
        input_output_aliases=aliases or {},
        compiler_params=pltpu.CompilerParams(
            dimension_semantics=("arbitrary",), vmem_limit_bytes=VMEM_BYTES
        ),
        cost_estimate=pl.CostEstimate(flops=flops, bytes_accessed=1_000_000, transcendentals=0),
    )(
        scalars,
        *(pltpu.with_memory_space_constraint(array, pltpu.HBM) for array, _ in blocks),
        *args,
        *waits,
    )
    return result if many else result[0]


def group_call(kernel, scalars, arrays, args, sums, extra_out, rows, scratch, flops, waits=()):
    shape = (1, 2, SPAN, D)
    outs = [(shape, BF, whole(shape))] + SUMS + extra_out
    start = 1 + len(arrays) + len(args)
    aliases = {start + n: 1 + n for n in range(len(sums))}
    stage = [pltpu.VMEM(rows + (D,), F32)] + [pltpu.VMEM((2, SPAN, D), BF)] * 2
    blocks = [(a, ANYWHERE) for a in arrays]
    return kernel_call(kernel, 1, scalars, blocks, args + sums, outs, stage + scratch, waits, aliases, flops)


def halo_kernel(scalars, tok, cot, w_qkv, w_out, lat, lon, cor, weights, first_x, first_g, strips, w, sems):
    core = scalars[2]
    copies = [
        pltpu.make_async_copy(w_qkv, w, sems.at[0]),
        pltpu.make_async_copy(w_out, weights.at[384:512], sems.at[1]),
    ]
    for n, ref in enumerate((tok, cot)):
        for m, (source, at, rows) in enumerate(
            ((0, 0, 3), (3 + 6 * core, 3, 6), (15 + 6 * core, 9, 3), (18 + 3 * core, 12, 3))
        ):
            copies.append(
                pltpu.make_async_copy(
                    ref.at[:, pl.ds(source, rows), 0:16, :], strips.at[n, :, at : at + rows], sems.at[2 + 5 * n + m]
                )
            )
        columns = pl.ds(pl.multiple_of(16 * core, 16), 32)
        copies.append(
            pltpu.make_async_copy(
                ref.at[:, 0:3, columns, :], lat.at[2 * n : 2 * n + 2], sems.at[6 + 5 * n]
            )
        )
    for n, (ref, first) in enumerate(((tok, first_x), (cot, first_g))):
        copies.append(pltpu.make_async_copy(ref.at[:, pl.ds(3 + 12 * core, 6)], first, sems.at[12 + n]))
    for copy in copies:
        copy.start()
    copies[0].wait()
    for t in range(3):
        weights[128 * t : 128 * t + 128, :] = w[t].T
    for copy in copies[1:]:
        copy.wait()
    for n in range(2):
        strip = strips[n].astype(F32)[:, :, 0:8].astype(BF)
        cor[2 * n : 2 * n + 2] = strip[:, 0:3]
        lon[2 * n : 2 * n + 2] = strip[:, 3:15]


def early_kernel(scalars, half0, half1, other0, other1, out):
    for group, (half, other) in enumerate(((half0, other0), (half1, other1))):
        out[group] = (half[0].astype(F32) + other[0].astype(F32)).astype(BF)


def late_kernel(scalars, half2, half3, other2, other3, out, lat, lon, cor):
    corner = scalars[2] == 1
    for n in range(2):
        row = half2[0, n].astype(F32) + other2[0, n].astype(F32)
        column = half3[0, n].astype(F32) + other3[0, n].astype(F32)
        out[0, n] = row.astype(BF)
        out[1, n] = column.astype(BF)
        if n == 1:
            row = jnp.where(corner, column, row)
            cor[...] = column[:96].reshape(2, 6, 8, D)[:, 3:6].reshape(48, D).astype(BF)
        edge = row.reshape(3, 6, 8, D)[:, 3:6].reshape(72, D)
        lat[n] = jnp.concatenate([edge, jnp.zeros((8, D), F32)], 0).astype(BF)
        lon[n] = column[:96].astype(BF)


def join_kernel(scalars, lat, lon, cor, out):
    out[0:80] = lat[0]
    out[80:160] = lat[1]
    out[160:256] = lon[0]
    out[256:352] = lon[1]
    out[352:400] = cor[...]


def pack_kernel(scalars, payload, first, second, small, small_theirs, out):
    share = out.shape[0]
    other = jnp.concatenate([first[...], second[...]], 0).astype(F32)
    rows = (payload[...] + other).reshape(share, 2048 // share, 128)
    small = small[...] + small_theirs[...]
    high = small.astype(BF).astype(F32)
    pair = jnp.concatenate([high[:, None], (small - high)[:, None], jnp.zeros((8, 6, 128), F32)], 1)
    ride = jnp.concatenate([pair, jnp.zeros((share - 8, 8, 128), F32)], 0)
    out[...] = jnp.concatenate([rows, ride], 1).astype(BF)


def copy_kernel(scalars, a, out):
    out[...] = a[...]


def sum_kernel(scalars, parts, out):
    out[...] = jnp.sum(parts[...].astype(F32), axis=0)


def spread_kernel(scalars, a, b, out):
    total = a[...] + b[...]
    rows = total.shape[0] - 8
    extra = total[rows : rows + 1] + total[rows + 1 : rows + 2]
    high = extra.astype(BF).astype(F32)
    total = jnp.concatenate([total[:rows], high, extra - high, jnp.zeros((6, 128), F32)], 0)
    out[...] = jnp.broadcast_to(total.astype(BF)[None], out.shape)


def small_kernel(scalars, parts, small):
    rows = parts.shape[1] - 8
    values = parts[0:8].astype(F32)
    small[...] = values[:, rows] + values[:, rows + 1]


def unpack_kernel(scalars, parts, gq, go):
    values = parts[...].astype(F32)
    rows = values.shape[1] - 8
    rows = values[:, :rows].reshape(2048, 128)
    for t in range(3):
        gq[t] = rows[512 * t : 512 * t + 512]
    for n in range(4):
        go[:, 128 * n : 128 * n + 128] = rows[1536 + 128 * n : 1664 + 128 * n]


def tile_kernel(scalars, tok, cot, a0, a1, b0, b1, ha, hb, gain, out, windows, halos, stage):
    step = pl.program_id(0)

    @pl.when(step == 0)
    def _():
        place_windows(scalars, a0, a1, b0, b1, ha, hb, windows, halos, stage)

    x, g = tok[...].astype(F32), cot[...].astype(F32)
    unit, inv_std = normalised(x)
    scaled = stage[:, pl.ds(6 * step, 6), 8:56, :] * gain[...].reshape(1, 1, 1, D)
    mean = jnp.sum(scaled, axis=-1, keepdims=True) * (1.0 / D)
    along = jnp.sum(scaled * unit, axis=-1, keepdims=True) * (1.0 / D)
    out[...] = (g + inv_std * (scaled - mean - unit * along)).astype(BF)


def place_windows(scalars, a0, a1, b0, b1, ha, hb, windows, halos, stage):
    for n, (early, late, halo) in enumerate(((a0, a1, ha), (b0, b1, hb))):
        windows[n, 0:2] = early[...]
        windows[n, 2:4] = late[...]
        halos[n] = halo[...]
    core = scalars[2]

    def holder(j):
        return jnp.where(core == j % 2, 0, 1)

    for j in range(4):
        at = 80 * (j % 2)
        edge = halos[holder(j // 2), at : at + 80, :].astype(F32)[:72].reshape(3, 3, 8, D)
        column = 14 + 12 * j
        wide, narrow = (0, 8) if j < 3 else (4, 0)
        stage[:, 0:3, column + wide : column + wide + 8, :] = edge[0:2]
        stage[0, 0:3, column + narrow : column + narrow + 4, :] = edge[2, :, 0:4]
        stage[1, 0:3, column + narrow : column + narrow + 4, :] = edge[2, :, 4:8]
        rows = 6 if j < 3 else 3
        at = 160 + 96 * (j // 2)
        strip = halos[holder(j), at : at + 96, :].astype(F32).reshape(2, 6, 8, D)
        stage[:, 3 + 6 * j : 3 + 6 * j + rows, 6:14, :] = strip[:, :rows]
    stage[:, 0:3, 6:14, :] = halos[holder(3), 352:400, :].astype(F32).reshape(2, 3, 8, D)
    for group in range(4):
        for j in range(4):
            row, col = PLACE[group][j]
            rows = 6 if row < 3 else 3
            value = windows[holder(j), group, j // 2].astype(F32)
            full = value[:96].reshape(2, 6, 8, D)[:, :rows]
            rest = value[96:].reshape(6, 8, D)[:rows]
            column = 14 + 12 * col
            wide, narrow = (0, 8) if group < 3 else (4, 0)
            at = slice(3 + 6 * row, 3 + 6 * row + rows)
            stage[:, at, column + wide : column + wide + 8, :] = full
            stage[0, at, column + narrow : column + narrow + 4, :] = rest[:, 0:4]
            stage[1, at, column + narrow : column + narrow + 4, :] = rest[:, 4:8]


def per_device(tokens, cotangent, norm_gain, norm_bias, w_qkv, w_out):
    core = lax.axis_index("tp") % 2
    edge = lax.axis_index("lat") == lax.axis_size("lat") - 1

    def scalars(first, second):
        masked = jnp.stack([edge & first, edge & second])
        return jnp.concatenate([jnp.where(masked, 1, 0), core.reshape(1)]).astype(jnp.int32)

    never = core < 0
    no_mask, row_mask, column_mask = scalars(never, never), scalars(core >= 0, core == 0), scalars(never, core == 1)

    def swap(block, bit):
        return move(block, ("tp",), lambda t: (t ^ bit,))

    both = (tokens, cotangent)
    h_lat, h_lon, h_cor, mine, *first_rows = kernel_call(
        halo_kernel,
        1,
        no_mask,
        [(a, ANYWHERE) for a in (tokens, cotangent, w_qkv.transpose(1, 0, 2), w_out)],
        [],
        [((4, 3, 32, D), BF), ((4, 12, 8, D), BF), ((4, 3, 8, D), BF), ((512, D), BF)] + [((2, 6, 48, D), BF)] * 2,
        [
            pltpu.VMEM((2, 2, 15, 16, D), BF),
            pltpu.VMEM((3, D, 128), BF),
            pltpu.SemaphoreType.DMA((14,)),
        ],
    )
    theirs = swap(mine, 1)
    h_lat = move(h_lat, ("lat", "tp"), lambda a, t: (a - 1, t ^ 2))
    h_lon = move(h_lon, ("lon",), lambda a: (a - 1,))
    h_cor = move(h_cor, ("lat", "lon"), lambda a, b: (a - 1, b - 1))

    gain = norm_gain.reshape(1, D)
    params = [gain, norm_bias.reshape(1, D), mine, theirs]
    masks = [pltpu.VMEM((2, SPAN, SPAN), F32)]
    half0, *sums, tile_x, tile_g = group_call(
        inner_kernel(0),
        no_mask,
        both,
        first_rows + params,
        [],
        [(t.shape, BF) for t in both],
        (2, 6, 48),
        [pltpu.SemaphoreType.DMA((2, 4))],
        FLOPS[0],
    )
    other0 = swap(half0, 2)
    tiles_in = [tile_x, tile_g]
    half1, *sums = group_call(
        inner_kernel(1), no_mask, [], tiles_in + params, sums, [], (2, 12, 48), [], FLOPS[1]
    )
    other1 = swap(half1, 2)
    half2, *sums = group_call(
        row_kernel, row_mask, [], tiles_in + [h_lat] + params, sums, [], (2, 12, 48), masks, FLOPS[2]
    )
    other2 = swap(half2, 2)
    half3, _, _, _, payload, *payload_theirs, small = group_call(
        column_kernel,
        column_mask,
        [],
        tiles_in + [h_lat, h_lon, h_cor] + params,
        sums,
        [((2048, 128), F32), ((1024, 128), BF), ((1024, 128), BF), ((8, 128), F32)],
        (2, 12, 24),
        masks,
        FLOPS[3],
        [other0],
    )
    other3 = swap(half3, 2)

    lats, lons = lax.axis_size("lat"), lax.axis_size("lon")
    tiles = lats // 2 * lons
    shares = ((tiles, 2048 // tiles + 8, 128), BF)
    groups = [[a * lons + b for a in range(half, lats, 2) for b in range(lons)] for half in range(2)]

    def exchange(block):
        return lax.all_to_all(block, ("lat", "lon"), 0, 0, axis_index_groups=groups, tiled=True)

    small = kernel_call(copy_kernel, 1, no_mask, [], [small], ((8, 128), F32), (), [other1])
    packed = kernel_call(
        pack_kernel, 1, no_mask, [], [payload, *(swap(p, 1) for p in payload_theirs), small, swap(small, 1)], shares, (), [other2]
    )
    parts = exchange(packed)

    early = kernel_call(
        early_kernel,
        1,
        no_mask,
        [(a, whole(a.shape)) for a in (half0, half1)],
        [other0, other1],
        ((2, 2, SPAN, D), BF),
    )
    late, lat_edge, lon_edge, cor_edge = kernel_call(
        late_kernel,
        1,
        no_mask,
        [(a, whole(a.shape)) for a in (half2, half3)],
        [other2, other3],
        [((2, 2, SPAN, D), BF), ((2, 80, D), BF), ((2, 96, D), BF), ((48, D), BF)],
        flops=FLOPS[4],
    )
    lat_edge = move(lat_edge, ("lat", "tp"), lambda a, t: (a + 1, t ^ 2))
    lon_edge = move(lon_edge, ("lon",), lambda a: (a + 1,))
    cor_edge = move(cor_edge, ("lat", "lon"), lambda a, b: (a + 1, b + 1))
    edges = kernel_call(join_kernel, 1, no_mask, [], [lat_edge, lon_edge, cor_edge], ((400, D), BF))
    total = kernel_call(sum_kernel, 1, no_mask, [], [parts], (shares[0][1:], F32))
    other = move(total, ("lat",), lambda a: (a ^ 1,))
    spread = kernel_call(spread_kernel, 1, no_mask, [], [total, other], shares, (), [edges, early])
    gathered = exchange(spread)
    rows = pl.BlockSpec((2, 6, 48, D), lambda i, scalars: (0, i, 0, 0))
    grad_tokens = kernel_call(
        tile_kernel,
        4,
        no_mask,
        [(tokens, rows), (cotangent, rows)],
        [early, late, swap(early, 1), swap(late, 1), edges, swap(edges, 1), gain],
        (tokens.shape, BF, rows),
        [
            pltpu.VMEM((2, 4, 2, SPAN, D), BF),
            pltpu.VMEM((2, 400, D), BF),
            pltpu.VMEM((2, 24, 64, D), F32),
        ],
    )
    tokens_done = pltpu.with_memory_space_constraint(grad_tokens, pltpu.HBM)
    small = kernel_call(small_kernel, 1, no_mask, [], [gathered], ((8, 128), F32), (), [tokens_done])
    small_y = swap(small, 2)
    grad_qkv, grad_out = kernel_call(
        unpack_kernel,
        1,
        no_mask,
        [],
        [gathered],
        [((3, D, 128), F32, whole((3, D, 128))), ((128, D), F32, whole((128, D)))],
        (),
        [small],
    )
    small = small + small_y
    small = small.reshape(2, D)
    return (grad_tokens, small[0], small[1], grad_qkv.transpose(1, 0, 2), grad_out)


def solution(mesh):
    return jax.shard_map(
        per_device,
        mesh=mesh,
        in_specs=(
            P(None, "lat", "lon", None),
            P(None, "lat", "lon", None),
            P(),
            P(),
            P(None, None, "tp"),
            P("tp", None),
        ),
        out_specs=(P(None, "lat", "lon", None), P(), P(), P(None, None, "tp"), P("tp", None)),
        check_vma=False,
    )
```
